32 devices in a mesh: pipe: 4 (over y, core), dp: 8 (over z, x).
Axes of the slice: x: 2, y: 2, z: 4, core: 2. Of those that a mesh axis runs over, the one named last changes fastest.
Arguments:
- inputs: bfloat16 [2560, 960], P('dp', 'pipe'), may hold values from -6 to 6
- cotangent: bfloat16 [2560, 960], P('dp', 'pipe'), may hold values from -6 to 6
- lengths: int32 [8, 4], P('dp'), may hold values from 16 to 128, as said below
- w_query: bfloat16 [4, 960, 960], P('pipe'), may hold values from -0.1875 to 0.1875
- w_key: bfloat16 [4, 960, 320], P('pipe'), may hold values from -0.1875 to 0.1875
- w_value: bfloat16 [4, 960, 320], P('pipe'), may hold values from -0.1875 to 0.1875
- w_proj: bfloat16 [4, 960, 960], P('pipe'), may hold values from -0.75 to 0.75
- w_gate: bfloat16 [4, 960, 2560], P('pipe'), may hold values from -0.1875 to 0.1875
- w_up: bfloat16 [4, 960, 2560], P('pipe'), may hold values from -0.1875 to 0.1875
- w_down: bfloat16 [4, 2560, 960], P('pipe'), may hold values from -0.125 to 0.125
- gain_attn: float32 [4, 960], P('pipe'), may hold values from 0.1 to 1.9
- gain_mlp: float32 [4, 960], P('pipe'), may hold values from 0.1 to 1.9
Outputs:
- layer_output: float32 [2560, 960], P('dp', 'pipe')
- grad_input: float32 [2560, 960], P('dp', 'pipe')
- grad_query: float32 [4, 960, 960], P('pipe', 'dp')
- grad_key: float32 [4, 960, 320], P('pipe', 'dp')
- grad_value: float32 [4, 960, 320], P('pipe', 'dp')
- grad_proj: float32 [4, 960, 960], P('pipe', 'dp')
- grad_gate: float32 [4, 960, 2560], P('pipe', 'dp')
- grad_up: float32 [4, 960, 2560], P('pipe', 'dp')
- grad_down: float32 [4, 2560, 960], P('pipe', 'dp')
- grad_gain_attn: float32 [4, 960], P('pipe', 'dp')
- grad_gain_mlp: float32 [4, 960], P('pipe', 'dp')
The draws below stay inside these ranges and needn't reach their ends.
Inputs may be any that keep to these rules, and one draw needn't show every extreme that they name: lengths[g, m] is between a quarter of micro-batch m's slots and all of them (128 slots for m = 0, 64 for the others); in each data group one micro-batch, drawn from the seed, is full; in some data group the first micro-batch is full, and in some other data group a later micro-batch holds exactly a quarter of its slots.
All inputs are finite; a program needn't handle non-finite values.
Results may differ from the reference program's by a relative error of at most 0.035.
Values may be sent and summed in bfloat16 or wider, within the bound.
No kernel may reach another device: no remote copies, remote signals or barrier semaphores. Data moves between devices by JAX's collectives and lax.ppermute only.
A program may use at most 256 MiB of HBM per device.

```python
import jax
import jax.numpy as jnp
from jax import lax

D = 960
HEADS = 15
KV_HEADS = 5
HEAD_DIM = 64
FF = 2560
SEG = 64
MICRO = 4
SECTIONS = 4
GROUPS = 8
ROWS = 320
TOKENS = 2560
KVD = 320


def draw_lengths(key, part):
    first_key, second_key, third_key, fourth_key = jax.random.split(key, 4)
    positions = jnp.arange(MICRO, dtype=jnp.int32)[None, :]
    group_ids = jnp.arange(GROUPS, dtype=jnp.int32)[:, None]
    capacity = jnp.where(positions == 0, 2 * SEG, SEG) * jnp.ones((GROUPS, 1), jnp.int32)
    sampled = jax.random.randint(first_key, (GROUPS, MICRO), capacity // 4, capacity + 1)
    chosen = jax.random.randint(second_key, (GROUPS, 1), 0, MICRO)
    full_group = jax.random.randint(third_key, (), 0, GROUPS)
    chosen = jnp.where(group_ids == full_group, 0, chosen)
    small_group = (full_group + 1 + jax.random.randint(fourth_key, (), 0, GROUPS - 1)) % GROUPS
    low_position = jnp.where(chosen == 1, 2, 1)
    sampled = jnp.where((group_ids == small_group) & (positions == low_position), capacity // 4, sampled)
    return jnp.where(positions == chosen, capacity, sampled).astype(jnp.int32)


def level_of(own_key, dims, cuts, least, top_value):
    def one(position, blocks):
        draws = jax.random.uniform(jax.random.fold_in(jax.random.fold_in(own_key, 6), position), (blocks,), jnp.float32, least / len(cuts), top_value / len(cuts))
        return jnp.repeat(jnp.exp(draws), dims[position] // blocks).reshape((-1,) + (1,) * (len(dims) - position - 1))

    loudness = one(*cuts[0])
    for cut in cuts[1:]:
        loudness = loudness * one(*cut)
    return loudness


def centred(own_key, extent, spread, most, shards=(), held_as=jnp.bfloat16):
    entries = spread * jax.random.normal(own_key, extent, jnp.float32)
    if shards:
        entries = entries * level_of(own_key, extent, shards, -0.22, 0.18)
    return jnp.clip(entries, -most, most).astype(held_as)


def setup_inputs(seed: int = 0) -> dict:
    splits = jax.random.split(jax.random.key(seed), 13)
    inputs = centred(splits[0], (TOKENS, D), 1.0, 6.0, ((0, 8), (1, 4)))
    cotangent = centred(splits[1], (TOKENS, D), 1.0, 6.0, ((0, 8), (1, 4)))
    lengths = draw_lengths(jax.random.fold_in(splits[12], 71), 0)
    w_query = centred(splits[3], (SECTIONS, D, D), D ** -0.5, 0.1875, ((0, 4),))
    w_key = centred(splits[4], (SECTIONS, D, KVD), D ** -0.5, 0.1875, ((0, 4),))
    w_value = centred(splits[5], (SECTIONS, D, KVD), D ** -0.5, 0.1875, ((0, 4),))
    w_proj = centred(splits[6], (SECTIONS, D, D), (D // 16) ** -0.5, 0.75, ((0, 4),))
    w_gate = centred(splits[7], (SECTIONS, D, FF), D ** -0.5, 0.1875, ((0, 4),))
    w_up = centred(splits[8], (SECTIONS, D, FF), D ** -0.5, 0.1875, ((0, 4),))
    w_down = centred(splits[9], (SECTIONS, FF, D), FF ** -0.5, 0.125, ((0, 4),))
    gain_attn = jnp.clip(1.0 + 0.18 * jax.random.normal(splits[10], (SECTIONS, D), jnp.float32), 0.1, 1.9)
    gain_mlp = jnp.clip(1.0 + 0.18 * jax.random.normal(splits[11], (SECTIONS, D), jnp.float32), 0.1, 1.9)
    return dict(inputs=inputs, cotangent=cotangent, lengths=lengths, w_query=w_query, w_key=w_key, w_value=w_value, w_proj=w_proj, w_gate=w_gate, w_up=w_up, w_down=w_down, gain_attn=gain_attn, gain_mlp=gain_mlp)


@jax.custom_vjp
def low(v):
    return lax.optimization_barrier(v.astype(jnp.bfloat16)).astype(jnp.float32)

@jax.custom_vjp
def low_back(v):
    return v

def low_keep(v):
    return (low(v), None)

def low_pass(kept, grad):
    return (grad,)

def back_keep(v):
    return (v, None)

def back_low(kept, grad):
    return (low(grad),)
low.defvjp(low_keep, low_pass)
low_back.defvjp(back_keep, back_low)
highest = lax.Precision.HIGHEST
epsilon = 1e-05
rope_base = 10000.0
masked_score = -1e+30

def matmul(left_side, right_side):
    return jnp.dot(left_side, right_side, precision=highest)

def rms_normalize(hidden, gain_vector):
    return hidden * lax.rsqrt(lax.optimization_barrier(jnp.mean(hidden * hidden, axis=-1, keepdims=True)) + epsilon) * gain_vector

def rope_tables(row_count):
    half_dim = HEAD_DIM // 2
    positions = jnp.arange(row_count, dtype=jnp.float32)[:, None]
    frequency = rope_base ** (-jnp.arange(half_dim, dtype=jnp.float32) / half_dim)
    angles = positions * frequency[None, :]
    return (jnp.cos(angles)[:, None, :], jnp.sin(angles)[:, None, :])

def rotate(tensor, cosine_table, sine_table):
    half_dim = tensor.shape[-1] // 2
    first_half = tensor[..., :half_dim]
    second_half = tensor[..., half_dim:]
    return jnp.concatenate([first_half * cosine_table - second_half * sine_table, second_half * cosine_table + first_half * sine_table], axis=-1)

def attend(query_rot, key_rot, value_rows, length):
    row_count = query_rot.shape[0]
    grouped = query_rot.reshape(row_count, KV_HEADS, HEADS // KV_HEADS, HEAD_DIM)
    scores = low_back(jnp.einsum('qkgd,skd->kgqs', grouped, key_rot, precision=highest) * HEAD_DIM ** (-0.5))
    row_ids = jnp.arange(row_count)[:, None]
    col_ids = jnp.arange(row_count)[None, :]
    allowed = (col_ids <= row_ids) & (col_ids < length)
    probabilities = low(jax.nn.softmax(jnp.where(allowed, scores, masked_score), axis=-1))
    mixed_heads = jnp.einsum('kgqs,skd->qkgd', probabilities, value_rows, precision=highest)
    return mixed_heads.reshape(row_count, HEADS * HEAD_DIM)

def apply_layer(hidden, params, length, cosine_table, sine_table):
    w_query, w_key, w_value, w_proj, w_gate, w_up, w_down, gain_attn, gain_mlp = params
    row_count = hidden.shape[0]
    normed_attn = low(rms_normalize(hidden, gain_attn))
    queries = low_back(matmul(normed_attn, w_query)).reshape(row_count, HEADS, HEAD_DIM)
    key_rows = low_back(matmul(normed_attn, w_key)).reshape(row_count, KV_HEADS, HEAD_DIM)
    value_rows = low(low_back(matmul(normed_attn, w_value))).reshape(row_count, KV_HEADS, HEAD_DIM)
    query_rot = low(rotate(queries, cosine_table, sine_table))
    key_rot = low(rotate(key_rows, cosine_table, sine_table))
    mixed_heads = low(low_back(attend(query_rot, key_rot, value_rows, length)))
    middle = hidden + low_back(matmul(mixed_heads, w_proj))
    normed_mlp = low(rms_normalize(middle, gain_mlp))
    gate_proj = low_back(matmul(normed_mlp, w_gate))
    up_proj = low_back(matmul(normed_mlp, w_up))
    inner_act = low(jax.nn.silu(gate_proj) * up_proj)
    return middle + low_back(matmul(inner_act, w_down))

def group_forward(rows_in, params, group_lengths):
    pieces = []
    head_params = tuple((weight[:-1] for weight in params))
    last_params = tuple((weight[-1] for weight in params))
    for micro_index in range(MICRO):
        offset = 0 if micro_index == 0 else SEG * (micro_index + 1)
        row_count = 2 * SEG if micro_index == 0 else SEG
        cosine_table, sine_table = rope_tables(row_count)
        length = group_lengths[micro_index]

        def section_step(hidden, section_params):
            hidden = apply_layer(hidden, section_params, length, cosine_table, sine_table)
            hidden = apply_layer(hidden, section_params, length, cosine_table, sine_table)
            return (low(low_back(hidden)), None)
        hidden, ignored = lax.scan(section_step, rows_in[offset:offset + row_count], head_params)
        hidden = apply_layer(hidden, last_params, length, cosine_table, sine_table)
        hidden = apply_layer(hidden, last_params, length, cosine_table, sine_table)
        keep_rows = (jnp.arange(row_count) < length)[:, None]
        pieces.append(jnp.where(keep_rows, hidden, 0.0))
    return jnp.concatenate(pieces, axis=0)

def reference(inputs, cotangent, lengths, w_query, w_key, w_value, w_proj, w_gate, w_up, w_down, gain_attn, gain_mlp):
    params = tuple((weight.astype(jnp.float32) for weight in (w_query, w_key, w_value, w_proj, w_gate, w_up, w_down, gain_attn, gain_mlp)))
    rows_all = inputs.astype(jnp.float32).reshape(GROUPS, ROWS, D)
    cotangents = cotangent.astype(jnp.float32).reshape(GROUPS, ROWS, D)

    def group_step(totals, packed):
        rows_in, rows_cot, group_lengths = packed
        result, pullback = jax.vjp(lambda source, weights: group_forward(source, weights, group_lengths), rows_in, params)
        grad_rows, grad_params = pullback(rows_cot)
        return (jax.tree.map(jnp.add, totals, grad_params), (result, grad_rows))
    zero_grads = tuple((jnp.zeros_like(weight) for weight in params))
    totals, (outputs, grad_rows) = lax.scan(group_step, zero_grads, (rows_all, cotangents, lengths))
    return (outputs.reshape(TOKENS, D), grad_rows.reshape(TOKENS, D), totals[0], totals[1], totals[2], totals[3], totals[4], totals[5], totals[6], totals[7], totals[8])
```

```python
import functools

import jax
import jax.numpy as jnp
import numpy as np
from jax import lax
from jax.experimental import pallas as pl
from jax.experimental.pallas import tpu as pltpu
from jax.sharding import PartitionSpec as P

HEAD_DIM = 64
HALF = HEAD_DIM // 2
LANES = 128
MICRO = 4
CHUNKS = 3
SCALE = HEAD_DIM**-0.5
BF16 = jnp.bfloat16
F32 = jnp.float32

epsilon = 1e-05
rope_base = 10000.0
masked_score = -1e30

SLOT, ACTIVE, EDGE, LONG, LEN_A, LEN_B = range(6)


def round_up(value, multiple):
    return -(-value // multiple) * multiple


def dot(left, right):
    return jnp.dot(left, right, preferred_element_type=F32)


def dot_t(left, right):
    return lax.dot_general(left, right, (((1,), (1,)), ((), ())), preferred_element_type=F32)


def dot_rows(left, right):
    return lax.dot_general(left, right, (((0,), (0,)), ((), ())), preferred_element_type=F32)


def lane_ids(rows):
    return lax.broadcasted_iota(jnp.int32, (rows, LANES), 1)


def in_low_half(rows):
    return lane_ids(rows) < HEAD_DIM


def rotate(slab, cosine, signed_sine):
    first = (lane_ids(slab.shape[0]) % HEAD_DIM) < HALF
    partner = jnp.where(
        first, pltpu.roll(slab, LANES - HALF, 1), pltpu.roll(slab, HALF, 1)
    )
    return slab * cosine + partner * signed_sine


def both_halves(slab, upper):
    swapped = pltpu.roll(slab, HEAD_DIM, 1)
    low = in_low_half(slab.shape[0])
    return jnp.where(low, swapped, slab) if upper else jnp.where(low, slab, swapped)


def reciprocal_rms(value):
    return lax.rsqrt(jnp.mean(value * value, axis=-1, keepdims=True) + epsilon)


def score_bias(meta, rows):
    query = lax.broadcasted_iota(jnp.int32, (rows, rows), 0)
    key = lax.broadcasted_iota(jnp.int32, (rows, rows), 1)
    segment = rows // 2
    is_long = meta[LONG] == 1
    bound = jnp.where(
        is_long,
        meta[LEN_A],
        jnp.where(key < segment, meta[LEN_A], meta[LEN_B] + segment),
    )
    start = jnp.where(is_long, 0, jnp.where(query < segment, 0, segment))
    allowed = (key <= query) & (key < bound) & (key >= start)
    return jnp.where(allowed, 0.0, masked_score).astype(F32)


def start_all(copies, condition):
    @pl.when(condition)
    def _():
        for copy in copies:
            copy.start()


def wait_one(copy, condition):
    @pl.when(condition)
    def _():
        copy.wait()


def forward_kernel(
    sizes,
    meta,
    first_in,
    inbound,
    cosine_ref,
    sine_ref,
    gain_attn,
    gain_mlp,
    w_query,
    w_key,
    w_value,
    w_proj,
    w_gate,
    w_up,
    w_down,
    *rest,
):
    store_count = 11
    rest = rest[sizes["aliased"] :]
    out_round, out_full = rest[0], rest[1]
    (
        hidden_out,
        normed_attn_out,
        query_out,
        key_out,
        value_out,
        probs_out,
        mixed_out,
        middle_out,
        normed_mlp_out,
        slopes_out,
        inner_out,
    ) = rest[2 : 2 + store_count]
    (
        hidden_s,
        query_s,
        key_s,
        value_s,
        wq,
        wk,
        wv,
        wp,
        wg,
        wu,
        wd,
        sems,
    ) = rest[2 + store_count :]
    rows, width = hidden_s.shape
    heads = width // HEAD_DIM
    kv_heads = w_key.shape[1] // HEAD_DIM
    share = heads // kv_heads
    ff = w_gate.shape[1]
    app = pl.program_id(0)
    pairs = (
        (w_query, wq),
        (w_key, wk),
        (w_value, wv),
        (w_proj, wp),
        (w_gate, wg),
        (w_up, wu),
        (w_down, wd),
    )
    copies = [
        pltpu.make_async_copy(source, target, sems.at[i]) for i, (source, target) in enumerate(pairs)
    ]

    @pl.when(meta[ACTIVE] == 1)
    def _():
        start_all(copies, app == 0)

        @pl.when(app == 0)
        def _():
            hidden_s[...] = jnp.where(
                meta[EDGE] == 1, first_in[...].astype(F32), inbound[...].astype(F32)
            )
            query_s[:, query_s.shape[1] - LANES :] = jnp.zeros((rows, LANES), F32)
            key_s[:, key_s.shape[1] - LANES :] = jnp.zeros((rows, LANES), F32)
            value_s[:, value_s.shape[1] - LANES :] = jnp.zeros((rows, LANES), F32)

        hidden = hidden_s[...]
        hidden_out[0, 0] = hidden
        normed = (hidden * reciprocal_rms(hidden) * gain_attn[...]).astype(BF16)
        normed_attn_out[0, 0] = normed
        wait_one(copies[0], app == 0)
        query_s[:, :width] = dot(normed, wq[...])
        wait_one(copies[1], app == 0)
        key_s[:, : kv_heads * HEAD_DIM] = dot(normed, wk[...])
        wait_one(copies[2], app == 0)
        value_s[:, : kv_heads * HEAD_DIM] = dot(normed, wv[...])
        cosine = cosine_ref[meta[LONG]]
        sine = sine_ref[meta[LONG]]
        low = in_low_half(rows)
        query_parts = []
        for j in range(query_s.shape[1] // LANES):
            slab = rotate(query_s[:, j * LANES : (j + 1) * LANES], cosine, sine)
            query_out[0, 0, :, j * LANES : (j + 1) * LANES] = slab.astype(BF16)
            query_parts.append(jnp.where(low, slab, 0.0).astype(BF16))
            query_parts.append(jnp.where(low, 0.0, slab).astype(BF16))
        keys, values = [], []
        for j in range(key_s.shape[1] // LANES):
            slab = rotate(key_s[:, j * LANES : (j + 1) * LANES], cosine, sine)
            key_out[0, 0, :, j * LANES : (j + 1) * LANES] = slab.astype(BF16)
            keys.append(both_halves(slab, False).astype(BF16))
            keys.append(both_halves(slab, True).astype(BF16))
            slab = value_s[:, j * LANES : (j + 1) * LANES]
            value_out[0, 0, :, j * LANES : (j + 1) * LANES] = slab.astype(BF16)
            values.append(both_halves(slab, False).astype(BF16))
            values.append(both_halves(slab, True).astype(BF16))
        bias = score_bias(meta, rows)
        bias = jnp.concatenate([bias] * share, axis=0)
        mixed_parts = []
        for kv in range(kv_heads):
            grouped = jnp.concatenate(query_parts[kv * share : (kv + 1) * share], axis=0)
            scores = dot_t(grouped, keys[kv]) * SCALE + bias
            exponent = jnp.exp(scores - jnp.max(scores, axis=-1, keepdims=True))
            total = jnp.sum(exponent, axis=-1, keepdims=True)
            probs = (exponent * (1.0 / total)).astype(BF16)
            probs_out[0, 0, kv] = probs
            mixed = dot(probs, values[kv])
            mixed_parts += [mixed[i * rows : (i + 1) * rows] for i in range(share)]
        for j in range(heads // 2):
            mixed_out[0, 0, :, j * LANES : (j + 1) * LANES] = jnp.where(
                low, mixed_parts[2 * j], mixed_parts[2 * j + 1]
            ).astype(BF16)
        if heads % 2:
            mixed_out[0, 0, :, width - HEAD_DIM :] = mixed_parts[-1][:, :HEAD_DIM].astype(BF16)
        wait_one(copies[3], app == 0)
        middle = hidden + dot(mixed_out[0, 0], wp[...])
        middle_out[0, 0] = middle
        normed = (middle * reciprocal_rms(middle) * gain_mlp[...]).astype(BF16)
        normed_mlp_out[0, 0] = normed
        wait_one(copies[4], app == 0)
        wait_one(copies[5], app == 0)
        step = sizes["ff_step"]
        for at in range(0, ff, step):
            gate = dot(normed, wg[:, at : at + step])
            up = dot(normed, wu[:, at : at + step])
            sigma = 1.0 / (1.0 + jnp.exp(-gate))
            silu = gate * sigma
            inner_out[0, 0, :, at : at + step] = (silu * up).astype(BF16)
            slopes_out[0, 0, 0, :, at : at + step] = (
                up * (sigma * (1.0 + gate * (1.0 - sigma)))
            ).astype(BF16)
            slopes_out[0, 0, 1, :, at : at + step] = silu.astype(BF16)
        wait_one(copies[6], app == 0)
        result = middle + dot(inner_out[0, 0], wd[...])
        hidden_s[...] = result
        out_round[...] = result.astype(BF16)
        out_full[0] = result


def backward_kernel(
    sizes,
    meta,
    top_rows,
    inbound,
    cosine_ref,
    sine_ref,
    gain_attn,
    gain_mlp,
    w_query,
    w_key,
    w_value,
    w_proj,
    w_gate,
    w_up,
    w_down,
    hidden_in,
    query_in,
    key_in,
    value_in,
    probs_in,
    middle_in,
    slopes_in,
    *rest,
):
    store_count = 8
    rest = rest[sizes["aliased"] :]
    out_round, out_full = rest[0], rest[1]
    (
        branch_out,
        gate_out,
        up_out,
        attn_out,
        query_out,
        key_out,
        value_out,
        gains_out,
    ) = rest[2 : 2 + store_count]
    (
        grad_s,
        mixed_s,
        wq,
        wk,
        wv,
        wp,
        wg,
        wu,
        wd,
        sems,
    ) = rest[2 + store_count :]
    rows, width = grad_s.shape
    heads = width // HEAD_DIM
    kv_heads = w_key.shape[1] // HEAD_DIM
    share = heads // kv_heads
    ff = w_gate.shape[1]
    step_id = pl.program_id(0)
    pairs = (
        (w_down, wd),
        (w_gate, wg),
        (w_up, wu),
        (w_proj, wp),
        (w_query, wq),
        (w_key, wk),
        (w_value, wv),
    )
    copies = [
        pltpu.make_async_copy(source, target, sems.at[i]) for i, (source, target) in enumerate(pairs)
    ]

    def rms_backward(value, gain, grad, running):
        scale = reciprocal_rms(value)
        unit = value * scale
        pulled = grad * gain
        gain_terms = grad * unit
        gain_rows = jnp.sum(gain_terms.reshape(rows // 8, 8, width), axis=0)
        shared = jnp.mean(gain_terms * gain, axis=-1, keepdims=True)
        return running + scale * (pulled - unit * shared), gain_rows

    @pl.when(meta[ACTIVE] == 1)
    def _():
        start_all(copies, step_id == 0)

        @pl.when(step_id == 0)
        def _():
            row = lax.broadcasted_iota(jnp.int32, (rows, 1), 0)
            segment = rows // 2
            bound = jnp.where(
                meta[LONG] == 1,
                meta[LEN_A],
                jnp.where(row < segment, meta[LEN_A], meta[LEN_B] + segment),
            )
            top = jnp.where(row < bound, top_rows[...].astype(F32), 0.0)
            grad_s[...] = jnp.where(meta[EDGE] == 1, top, inbound[...].astype(F32))
            mixed_s[:, mixed_s.shape[1] - LANES :] = jnp.zeros((rows, LANES), F32)

        low = in_low_half(rows)
        grad_top = grad_s[...]
        branch = grad_top.astype(BF16)
        branch_out[0, 0] = branch
        wait_one(copies[0], step_id == 0)
        step = sizes["ff_step"]
        for at in range(0, ff, step):
            inner_grad = dot_t(branch, wd[at : at + step, :])
            gate_out[0, 0, :, at : at + step] = (
                inner_grad * slopes_in[0, 0, 0, :, at : at + step].astype(F32)
            ).astype(BF16)
            up_out[0, 0, :, at : at + step] = (
                inner_grad * slopes_in[0, 0, 1, :, at : at + step].astype(F32)
            ).astype(BF16)
        wait_one(copies[1], step_id == 0)
        pulled = dot_t(gate_out[0, 0], wg[...])
        wait_one(copies[2], step_id == 0)
        pulled += dot_t(up_out[0, 0], wu[...])
        middle_grad, gain_rows = rms_backward(middle_in[0, 0], gain_mlp[...], pulled, grad_top)
        gains_out[0, 0, 1] = gain_rows
        attn_grad = middle_grad.astype(BF16)
        attn_out[0, 0] = attn_grad
        wait_one(copies[3], step_id == 0)
        mixed_s[:, :width] = dot_t(attn_grad, wp[...])
        mixed_parts, query_parts = [], []
        for j in range(mixed_s.shape[1] // LANES):
            slab = mixed_s[:, j * LANES : (j + 1) * LANES]
            mixed_parts.append(jnp.where(low, slab, 0.0).astype(BF16))
            mixed_parts.append(jnp.where(low, 0.0, slab).astype(BF16))
            slab = query_in[0, 0, :, j * LANES : (j + 1) * LANES].astype(F32)
            query_parts.append(jnp.where(low, slab, 0.0).astype(BF16))
            query_parts.append(jnp.where(low, 0.0, slab).astype(BF16))
        keys, values = [], []
        for j in range(key_in.shape[-1] // LANES):
            slab = key_in[0, 0, :, j * LANES : (j + 1) * LANES].astype(F32)
            keys.append(both_halves(slab, False).astype(BF16))
            keys.append(both_halves(slab, True).astype(BF16))
            slab = value_in[0, 0, :, j * LANES : (j + 1) * LANES].astype(F32)
            values.append(both_halves(slab, False).astype(BF16))
            values.append(both_halves(slab, True).astype(BF16))
        cosine = cosine_ref[meta[LONG]]
        sine = -sine_ref[meta[LONG]]
        query_grads, key_grads, value_grads = [], [], []
        for kv in range(kv_heads):
            mixed = jnp.concatenate(mixed_parts[kv * share : (kv + 1) * share], axis=0)
            grouped = jnp.concatenate(query_parts[kv * share : (kv + 1) * share], axis=0)
            probs = probs_in[0, 0, kv]
            probs_wide = probs.astype(F32)
            probs_grad = dot_t(mixed, values[kv])
            shared = jnp.sum(probs_wide * probs_grad, axis=-1, keepdims=True)
            score_grad = (probs_wide * (probs_grad - shared)).astype(BF16)
            pulled = dot(score_grad, keys[kv])
            query_grads += [pulled[i * rows : (i + 1) * rows] for i in range(share)]
            pulled = dot_rows(score_grad, grouped)
            key_grads.append(pulled + pltpu.roll(pulled, HEAD_DIM, 1))
            pulled = dot_rows(probs, mixed)
            value_grads.append(pulled + pltpu.roll(pulled, HEAD_DIM, 1))

        def put(target, parts, finish):
            count = len(parts)
            for j in range(count // 2):
                slab = jnp.where(low, parts[2 * j], parts[2 * j + 1])
                target[0, 0, :, j * LANES : (j + 1) * LANES] = finish(slab).astype(BF16)
            if count % 2:
                target[0, 0, :, (count - 1) * HEAD_DIM :] = finish(parts[-1])[:, :HEAD_DIM].astype(
                    BF16
                )

        put(query_out, query_grads, lambda slab: rotate(slab * SCALE, cosine, sine))
        put(key_out, key_grads, lambda slab: rotate(slab * SCALE, cosine, sine))
        put(value_out, value_grads, lambda slab: slab)
        wait_one(copies[4], step_id == 0)
        wait_one(copies[5], step_id == 0)
        wait_one(copies[6], step_id == 0)
        pulled = dot_t(query_out[0, 0], wq[...])
        pulled += dot_t(key_out[0, 0], wk[...])
        pulled += dot_t(value_out[0, 0], wv[...])
        result, gain_rows = rms_backward(hidden_in[0, 0], gain_attn[...], pulled, middle_grad)
        gains_out[0, 0, 0] = gain_rows
        grad_s[...] = result
        out_round[...] = result.astype(BF16)
        out_full[0] = result


def whole_block(shape):
    return pl.BlockSpec(shape, lambda i, meta: (0,) * len(shape))


def slot_block(shape, reverse=False):
    def place(i, meta):
        return (meta[SLOT], 1 - i if reverse else i) + (0,) * (len(shape) - 2)

    return pl.BlockSpec((1, 1) + tuple(shape[2:]), place)


def slot_only_block(shape):
    return pl.BlockSpec(
        (1,) + tuple(shape[1:]), lambda i, meta: (meta[SLOT],) + (0,) * (len(shape) - 1)
    )


def in_hbm():
    return pl.BlockSpec(memory_space=pl.ANY)


def weight_scratch(weights):
    return [pltpu.VMEM(weight.shape, weight.dtype) for weight in weights]


def run_tick(kernel, sizes, meta, blocks, weights, reads, state, shapes, scratch, reverse, name):
    rows, width = sizes["rows"], sizes["width"]
    slots = sizes["slots"]
    aliased = [] if state is None else list(state)
    outs = [
        jax.ShapeDtypeStruct((rows, width), BF16),
        jax.ShapeDtypeStruct((slots, rows, width), F32),
    ] + shapes
    out_specs = [whole_block((rows, width)), slot_only_block((slots, rows, width))]
    out_specs += [slot_block(shape.shape, reverse) for shape in shapes]
    in_specs = [whole_block(block.shape) for block in blocks]
    in_specs += [in_hbm() for _ in weights]
    in_specs += [slot_block(read.shape, reverse) for read in reads]
    in_specs += [in_hbm() for _ in aliased]
    first_alias = 1 + len(blocks) + len(weights) + len(reads)
    body = functools.partial(kernel, dict(sizes, aliased=len(aliased)))
    flops = 4 * rows * sum(int(np.prod(weight.shape)) for weight in weights)
    return pl.pallas_call(
        body,
        out_shape=outs,
        grid_spec=pltpu.PrefetchScalarGridSpec(
            num_scalar_prefetch=1,
            grid=(2,),
            in_specs=in_specs,
            out_specs=out_specs,
            scratch_shapes=scratch
            + weight_scratch(weights)
            + [pltpu.SemaphoreType.DMA((len(weights),))],
        ),
        input_output_aliases={first_alias + i: 1 + i for i in range(len(aliased))},
        compiler_params=pltpu.CompilerParams(
            dimension_semantics=("arbitrary",), vmem_limit_bytes=56 * 2**20
        ),
        cost_estimate=pl.CostEstimate(
            flops=flops, bytes_accessed=flops // (2 * rows), transcendentals=0
        ),
        name=name,
    )(meta, *blocks, *weights, *reads, *aliased)


def rope_tables(rows):
    segment = rows // 2
    frequency = rope_base ** (-np.arange(HALF, dtype=np.float64) / HALF)
    positions = np.stack([np.arange(rows) % segment, np.arange(rows)]).astype(np.float64)
    angles = np.tile(positions[:, :, None] * frequency, (1, 1, LANES // HALF))
    sign = np.where(np.arange(LANES) % HEAD_DIM < HALF, -1.0, 1.0)
    return (
        jnp.asarray(np.cos(angles), F32),
        jnp.asarray(np.sin(angles) * sign, F32),
    )


def per_device(
    inputs,
    cotangent,
    lengths,
    w_query,
    w_key,
    w_value,
    w_proj,
    w_gate,
    w_up,
    w_down,
    gain_attn,
    gain_mlp,
):
    sections = lax.axis_size("pipe")
    section = lax.axis_index("pipe")
    total_rows, columns = inputs.shape
    width = columns * sections
    rows = 2 * total_rows // (MICRO + 1)
    weights = (
        w_query[0],
        w_key[0],
        w_value[0],
        w_proj[0],
        w_gate[0],
        w_up[0],
        w_down[0],
    )
    kv_width = w_key.shape[-1]
    ff = w_gate.shape[-1]
    kv_heads = kv_width // HEAD_DIM
    share = width // kv_width
    ticks = CHUNKS + sections - 1
    slots = CHUNKS + 1
    sizes = dict(rows=rows, width=width, slots=slots, ff_step=ff // 4)
    cosine, sine = rope_tables(rows)
    is_first = section == 0
    is_last = section == sections - 1

    full_inputs = lax.all_gather(inputs, "pipe", axis=1, tiled=True)
    padding = jnp.zeros((CHUNKS * rows - total_rows, width), BF16)
    chunk_inputs = jnp.concatenate([full_inputs, padding], axis=0)

    spare = jnp.int32(rows // 2)
    group = lengths[0]
    bounds = jnp.stack(
        [
            jnp.stack([group[0], spare]),
            jnp.stack([group[1], group[2]]),
            jnp.stack([group[3], spare]),
        ]
    )

    def tick_scalars(chunk, edge):
        active = (chunk >= 0) & (chunk < CHUNKS)
        current = jnp.clip(chunk, 0, CHUNKS - 1)
        return jnp.stack(
            [
                jnp.where(active, current, CHUNKS),
                active.astype(jnp.int32),
                edge.astype(jnp.int32),
                (current == 0).astype(jnp.int32),
                bounds[current, 0],
                bounds[current, 1],
            ]
        ).astype(jnp.int32)

    def stored(*shape, dtype=BF16):
        return jax.ShapeDtypeStruct((slots, 2) + shape, dtype)

    query_pad, kv_pad = round_up(width, LANES), round_up(kv_width, LANES)
    forward_shapes = [
        stored(rows, width, dtype=F32),
        stored(rows, width),
        stored(rows, query_pad),
        stored(rows, kv_pad),
        stored(rows, kv_pad),
        stored(kv_heads, share * rows, rows),
        stored(rows, width),
        stored(rows, width, dtype=F32),
        stored(rows, width),
        stored(2, rows, ff),
        stored(rows, ff),
    ]
    forward_scratch = [
        pltpu.VMEM((rows, width), F32),
        pltpu.VMEM((rows, query_pad), F32),
        pltpu.VMEM((rows, kv_pad), F32),
        pltpu.VMEM((rows, kv_pad), F32),
    ]
    inbound = jnp.zeros((rows, width), BF16)
    state = None
    for tick in range(ticks):
        at = min(tick, CHUNKS - 1) * rows
        rounded, *state = run_tick(
            forward_kernel,
            sizes,
            tick_scalars(tick - section, is_first),
            (chunk_inputs[at : at + rows], inbound, cosine, sine, gain_attn, gain_mlp),
            weights,
            (),
            state,
            forward_shapes,
            forward_scratch,
            False,
            "layer_pair_forward",
        )
        route = [(s, s + 1) for s in range(sections - 1) if 0 <= tick - s < CHUNKS]
        if route:
            inbound = lax.ppermute(rounded, "pipe", route)
        if tick == 0:
            late_cotangent, _ = lax.optimization_barrier((cotangent, rounded))
    results = state[0]
    (
        hidden,
        normed_attn,
        query_rot,
        key_rot,
        value_rows,
        probs,
        mixed,
        middle,
        normed_mlp,
        slopes,
        inner,
    ) = state[1:]

    full_cotangent = lax.all_gather(late_cotangent, "pipe", axis=1, tiled=True)
    chunk_cotangent = jnp.concatenate([full_cotangent, padding], axis=0)

    backward_shapes = [
        stored(rows, width),
        stored(rows, ff),
        stored(rows, ff),
        stored(rows, width),
        stored(rows, width),
        stored(rows, kv_width),
        stored(rows, kv_width),
        stored(2, 8, width, dtype=F32),
    ]
    backward_scratch = [
        pltpu.VMEM((rows, width), F32),
        pltpu.VMEM((rows, query_pad), F32),
    ]
    reads = (hidden, query_rot, key_rot, value_rows, probs, middle, slopes)
    inbound = jnp.zeros((rows, width), BF16)
    state = None
    for tick in range(ticks):
        at = min(tick, CHUNKS - 1) * rows
        rounded, *state = run_tick(
            backward_kernel,
            sizes,
            tick_scalars(tick - (sections - 1 - section), is_last),
            (chunk_cotangent[at : at + rows], inbound, cosine, sine, gain_attn, gain_mlp),
            weights,
            reads,
            state,
            backward_shapes,
            backward_scratch,
            True,
            "layer_pair_backward",
        )
        route = [
            (s, s - 1) for s in range(1, sections) if 0 <= tick - (sections - 1 - s) < CHUNKS
        ]
        if route:
            inbound = lax.ppermute(rounded, "pipe", route)
    input_grads = state[0]
    branch, gate_grad, up_grad, attn_grad, query_grad, key_grad, value_grad, gains = state[1:]

    def product(left, right):
        left = left[:CHUNKS].reshape(CHUNKS * 2 * rows, left.shape[-1])
        right = right[:CHUNKS].reshape(CHUNKS * 2 * rows, right.shape[-1])
        return dot_rows(left, right).astype(BF16)

    def reduced(value):
        total = lax.psum_scatter(value, "dp", scatter_dimension=0, tiled=True)
        return total.astype(F32)[None]

    grad_down = reduced(product(inner, branch))
    grad_gate = reduced(product(normed_mlp, gate_grad))
    grad_up = reduced(product(normed_mlp, up_grad))
    grad_proj = reduced(product(mixed, attn_grad))
    grad_query = reduced(product(normed_attn, query_grad))
    grad_key = reduced(product(normed_attn, key_grad))
    grad_value = reduced(product(normed_attn, value_grad))
    gain_sums = jnp.sum(gains[:CHUNKS], axis=(0, 1, 3))
    grad_gain_attn = reduced(gain_sums[0])
    grad_gain_mlp = reduced(gain_sums[1])

    def spread(store, source):
        rows_all = store[:CHUNKS].reshape(CHUNKS * rows, width)[:total_rows]
        own = rows_all[:, source * columns : (source + 1) * columns]
        arrived = jnp.where(section == source, own, 0.0)
        for target in range(sections):
            if target != source:
                block = rows_all[:, target * columns : (target + 1) * columns]
                arrived = arrived + lax.ppermute(block, "pipe", [(source, target)])
        return arrived

    segment = rows // 2
    position = jnp.arange(total_rows)
    offsets = jnp.where(position < rows, position, position % segment)
    micro = jnp.where(position < rows, 0, position // segment - 1)
    valid = offsets < group[micro]
    layer_output = jnp.where(valid[:, None], spread(results, sections - 1), 0.0)
    grad_input = spread(input_grads, 0)
    return (
        layer_output,
        grad_input,
        grad_query,
        grad_key,
        grad_value,
        grad_proj,
        grad_gate,
        grad_up,
        grad_down,
        grad_gain_attn,
        grad_gain_mlp,
    )


def solution(mesh):
    placed = (
        P("dp", "pipe"),
        P("dp", "pipe"),
        P("dp", None),
        P("pipe", None, None),
        P("pipe", None, None),
        P("pipe", None, None),
        P("pipe", None, None),
        P("pipe", None, None),
        P("pipe", None, None),
        P("pipe", None, None),
        P("pipe", None),
        P("pipe", None),
    )
    return jax.shard_map(
        per_device,
        mesh=mesh,
        in_specs=placed,
        out_specs=(
            P("dp", "pipe"),
            P("dp", "pipe"),
            P("pipe", "dp", None),
            P("pipe", "dp", None),
            P("pipe", "dp", None),
            P("pipe", "dp", None),
            P("pipe", "dp", None),
            P("pipe", "dp", None),
            P("pipe", "dp", None),
            P("pipe", "dp"),
            P("pipe", "dp"),
        ),
        check_vma=False,
    )
```

```python
import functools

import jax
import jax.numpy as jnp
import numpy as np
from jax import lax
from jax.experimental import pallas as pl
from jax.experimental.pallas import tpu as pltpu
from jax.sharding import PartitionSpec as P

HEAD_DIM = 64
HALF = HEAD_DIM // 2
LANES = 128
MICRO = 4
CHUNKS = 3
SCALE = HEAD_DIM**-0.5
BF16 = jnp.bfloat16
F32 = jnp.float32

epsilon = 1e-05
rope_base = 10000.0
masked_score = -1e30

def round_up(value, multiple):
    return -(-value // multiple) * multiple


def dot(left, right):
    return jnp.dot(left, right, preferred_element_type=F32)


def dot_t(left, right):
    return lax.dot_general(left, right, (((1,), (1,)), ((), ())), preferred_element_type=F32)


def dot_rows(left, right):
    return lax.dot_general(left, right, (((0,), (0,)), ((), ())), preferred_element_type=F32)


def lane_ids(rows):
    return lax.broadcasted_iota(jnp.int32, (rows, LANES), 1)


def in_low_half(rows):
    return lane_ids(rows) < HEAD_DIM


def rotate(slab, cosine, signed_sine):
    first = (lane_ids(slab.shape[0]) % HEAD_DIM) < HALF
    partner = jnp.where(
        first, pltpu.roll(slab, LANES - HALF, 1), pltpu.roll(slab, HALF, 1)
    )
    return slab * cosine + partner * signed_sine


def both_halves(slab, upper):
    swapped = pltpu.roll(slab, HEAD_DIM, 1)
    low = in_low_half(slab.shape[0])
    return jnp.where(low, swapped, slab) if upper else jnp.where(low, slab, swapped)


def reciprocal_rms(value):
    return lax.rsqrt(jnp.mean(value * value, axis=-1, keepdims=True) + epsilon)


class Tick:
    def __init__(self, sizes, lengths):
        sections, depth_step, segment = sizes["sections"], sizes["depth_step"], sizes["rows"] // 2
        section = lax.axis_index("pipe")
        depth = sections - 1 - section if sizes["backward"] else section
        chunk = sizes["tick"] - depth_step * depth
        self.active = (chunk >= 0) & (chunk < CHUNKS)
        self.slot = jnp.clip(chunk, 0, CHUNKS - 1)
        self.edge = depth == 0
        self.final = depth == sections - 1
        self.is_long = self.slot == 0
        self.table = jnp.where(self.is_long, 1, 0)
        self.first_length = jnp.where(
            self.is_long, lengths[0, 0], jnp.where(self.slot == 1, lengths[0, 1], lengths[0, 3])
        )
        self.second_length = jnp.where(self.slot == 1, lengths[0, 2], segment)

    def bound(self, position, segment):
        return jnp.where(
            self.is_long,
            self.first_length,
            jnp.where(position < segment, self.first_length, self.second_length + segment),
        )


def score_bias(tick, rows):
    query = lax.broadcasted_iota(jnp.int32, (rows, rows), 0)
    key = lax.broadcasted_iota(jnp.int32, (rows, rows), 1)
    segment = rows // 2
    start = jnp.where(tick.is_long, 0, jnp.where(query < segment, 0, segment))
    allowed = (key <= query) & (key < tick.bound(key, segment)) & (key >= start)
    return jnp.where(allowed, 0.0, masked_score).astype(F32)


def assemble(target, parts, at):
    rows = target.shape[0]
    count = min(rows, parts[0].shape[0] - at)
    target[:count, :] = jnp.concatenate(
        [part[at : at + count, :].astype(F32) for part in parts], axis=1
    )
    if count < rows:
        target[count:, :] = jnp.zeros((rows - count, target.shape[1]), F32)


def when(condition, action):
    pl.when(condition)(action)


def forward_kernel(sizes, lengths, *refs):
    tick = Tick(sizes, lengths)
    refs = list(refs)

    def take(count):
        taken = refs[:count]
        del refs[:count]
        return taken

    cosine_ref, sine_ref, gain_attn, gain_mlp = take(4)
    edge_parts, inbound = take(sizes["edge_parts"]), take(sizes["inbound"])
    wq, wk, wv, wp, wg, wu, wd = take(7)
    take(sizes["aliased"])
    out_round, out_full = take(2)
    stores = take(sizes["stores"])
    hidden_s, query_s, key_s, value_s = take(4)
    buffers = take(sizes["stores"])
    (
        hidden_b,
        normed_attn_b,
        query_b,
        key_b,
        value_b,
        probs_b,
        mixed_b,
        middle_b,
        normed_mlp_b,
        slopes_b,
        inner_b,
    ) = buffers
    store_sems, final_sem = refs
    rows, width = hidden_s.shape
    heads = width // HEAD_DIM
    kv_width = wk.shape[0]
    kv_heads = kv_width // HEAD_DIM
    share = heads // kv_heads
    ff = wg.shape[1]
    slot = tick.slot

    def store(buffer, app):
        i = [other is buffer for other in buffers].index(True)
        return pltpu.make_async_copy(
            buffer.at[app], stores[i].at[slot, app], store_sems.at[i, app]
        )

    def apply(app, carry):
        hidden = hidden_s[...]
        hidden_b[app] = hidden
        store(hidden_b, app).start()
        normed = (hidden * reciprocal_rms(hidden) * gain_attn[...]).astype(BF16)
        normed_attn_b[app] = normed
        store(normed_attn_b, app).start()
        query_s[:, :width] = dot(normed, wq[...])
        key_s[:, :kv_width] = dot_t(normed, wk[...])
        value_s[:, :kv_width] = dot_t(normed, wv[...])
        cosine = cosine_ref[tick.table]
        sine = sine_ref[tick.table]
        low = in_low_half(rows)
        query_parts = []
        for j in range(query_s.shape[1] // LANES):
            slab = rotate(query_s[:, j * LANES : (j + 1) * LANES], cosine, sine)
            query_b[app, :, j * LANES : (j + 1) * LANES] = slab.astype(BF16)
            query_parts.append(jnp.where(low, slab, 0.0).astype(BF16))
            query_parts.append(jnp.where(low, 0.0, slab).astype(BF16))
        store(query_b, app).start()
        keys, values = [], []
        for j in range(key_s.shape[1] // LANES):
            slab = rotate(key_s[:, j * LANES : (j + 1) * LANES], cosine, sine)
            key_b[app, :, j * LANES : (j + 1) * LANES] = slab.astype(BF16)
            keys.append(both_halves(slab, False).astype(BF16))
            keys.append(both_halves(slab, True).astype(BF16))
            slab = value_s[:, j * LANES : (j + 1) * LANES]
            value_b[app, :, j * LANES : (j + 1) * LANES] = slab.astype(BF16)
            values.append(both_halves(slab, False).astype(BF16))
            values.append(both_halves(slab, True).astype(BF16))
        store(key_b, app).start()
        store(value_b, app).start()
        bias = score_bias(tick, rows)
        bias = jnp.concatenate([bias] * share, axis=0)
        mixed_parts = []
        for kv in range(kv_heads):
            grouped = jnp.concatenate(query_parts[kv * share : (kv + 1) * share], axis=0)
            scores = dot_t(grouped, keys[kv]) * SCALE + bias
            exponent = jnp.exp(scores - jnp.max(scores, axis=-1, keepdims=True))
            total = jnp.sum(exponent, axis=-1, keepdims=True)
            probs = (exponent * (1.0 / total)).astype(BF16)
            probs_b[app, kv] = probs
            mixed = dot(probs, values[kv])
            mixed_parts += [mixed[i * rows : (i + 1) * rows] for i in range(share)]
        store(probs_b, app).start()
        for j in range(heads // 2):
            mixed_b[app, :, j * LANES : (j + 1) * LANES] = jnp.where(
                low, mixed_parts[2 * j], mixed_parts[2 * j + 1]
            ).astype(BF16)
        if heads % 2:
            mixed_b[app, :, width - HEAD_DIM :] = mixed_parts[-1][:, :HEAD_DIM].astype(BF16)
        store(mixed_b, app).start()
        middle = hidden + dot(mixed_b[app], wp[...])
        middle_b[app] = middle
        store(middle_b, app).start()
        normed = (middle * reciprocal_rms(middle) * gain_mlp[...]).astype(BF16)
        normed_mlp_b[app] = normed
        store(normed_mlp_b, app).start()
        step = sizes["ff_step"]
        for at in range(0, ff, step):
            gate = dot(normed, wg[:, at : at + step])
            up = dot(normed, wu[:, at : at + step])
            sigma = 1.0 / (1.0 + jnp.exp(-gate))
            silu = gate * sigma
            inner_b[app, :, at : at + step] = (silu * up).astype(BF16)
            slopes_b[app, 0, :, at : at + step] = (
                up * (sigma * (1.0 + gate * (1.0 - sigma)))
            ).astype(BF16)
            slopes_b[app, 1, :, at : at + step] = silu.astype(BF16)
        store(inner_b, app).start()
        store(slopes_b, app).start()
        hidden_s[...] = middle + dot(inner_b[app], wd[...])
        return carry

    @pl.when(tick.active)
    def _():
        if edge_parts:

            @pl.when(tick.edge)
            def _():
                assemble(hidden_s, edge_parts, sizes["tick"] * rows)

        if inbound:

            @pl.when(jnp.logical_not(tick.edge))
            def _():
                hidden_s[...] = inbound[0][...].astype(F32)

        query_s[:, query_s.shape[1] - LANES :] = jnp.zeros((rows, LANES), F32)
        key_s[:, key_s.shape[1] - LANES :] = jnp.zeros((rows, LANES), F32)
        value_s[:, value_s.shape[1] - LANES :] = jnp.zeros((rows, LANES), F32)
        lax.fori_loop(0, 2, apply, 0)
        out_round[...] = hidden_s[...].astype(BF16)
        final = pltpu.make_async_copy(hidden_s, out_full.at[slot], final_sem.at[0])
        when(tick.final, final.start)
        for buffer in buffers:
            store(buffer, 0).wait()
            store(buffer, 1).wait()
        when(tick.final, final.wait)


def backward_kernel(sizes, lengths, *refs):
    tick = Tick(sizes, lengths)
    refs = list(refs)

    def take(count):
        taken = refs[:count]
        del refs[:count]
        return taken

    cosine_ref, sine_ref, gain_attn, gain_mlp = take(4)
    edge_parts, inbound = take(sizes["edge_parts"]), take(sizes["inbound"])
    wq, wk, wv, wp, wg, wu, wd = take(7)
    saved = take(sizes["reads"])
    take(sizes["aliased"])
    out_round, out_full = take(2)
    stores = take(sizes["stores"])
    grad_s, mixed_s = take(2)
    kept = take(sizes["reads"])
    hidden_k, query_k, key_k, value_k, probs_k, middle_k, slopes_k = kept
    buffers = take(sizes["stores"])
    branch_b, gate_b, up_b, attn_b, query_b, key_b, value_b, gains_b = buffers
    read_sems, store_sems, final_sem = refs
    rows, width = grad_s.shape
    heads = width // HEAD_DIM
    kv_width = wk.shape[0]
    kv_heads = kv_width // HEAD_DIM
    share = heads // kv_heads
    ff = wd.shape[1]
    slot = tick.slot

    def read(buffer, app):
        i = [other is buffer for other in kept].index(True)
        return pltpu.make_async_copy(saved[i].at[slot, app], buffer.at[app], read_sems.at[i, app])

    def store(buffer, app):
        i = [other is buffer for other in buffers].index(True)
        return pltpu.make_async_copy(
            buffer.at[app], stores[i].at[slot, app], store_sems.at[i, app]
        )

    def rms_backward(value, gain, grad, running):
        scale = reciprocal_rms(value)
        unit = value * scale
        pulled = grad * gain
        gain_terms = grad * unit
        gain_rows = jnp.sum(gain_terms.reshape(rows // 8, 8, width), axis=0)
        shared = jnp.mean(gain_terms * gain, axis=-1, keepdims=True)
        return running + scale * (pulled - unit * shared), gain_rows

    def apply(step_id, carry):
        app = 1 - step_id

        low = in_low_half(rows)
        grad_top = grad_s[...]
        branch = grad_top.astype(BF16)
        branch_b[app] = branch
        store(branch_b, app).start()
        read(slopes_k, app).wait()
        step = sizes["ff_step"]
        for at in range(0, ff, step):
            inner_grad = dot(branch, wd[:, at : at + step])
            gate_b[app, :, at : at + step] = (
                inner_grad * slopes_k[app, 0, :, at : at + step].astype(F32)
            ).astype(BF16)
            up_b[app, :, at : at + step] = (
                inner_grad * slopes_k[app, 1, :, at : at + step].astype(F32)
            ).astype(BF16)
        store(gate_b, app).start()
        store(up_b, app).start()
        pulled = dot(gate_b[app], wg[...])
        pulled += dot(up_b[app], wu[...])
        read(middle_k, app).wait()
        middle_grad, gain_rows = rms_backward(middle_k[app], gain_mlp[...], pulled, grad_top)
        gains_b[app, 1] = gain_rows
        attn_grad = middle_grad.astype(BF16)
        attn_b[app] = attn_grad
        store(attn_b, app).start()
        mixed_s[:, :width] = dot(attn_grad, wp[...])
        mixed_parts, query_parts = [], []
        read(query_k, app).wait()
        for j in range(mixed_s.shape[1] // LANES):
            slab = mixed_s[:, j * LANES : (j + 1) * LANES]
            mixed_parts.append(jnp.where(low, slab, 0.0).astype(BF16))
            mixed_parts.append(jnp.where(low, 0.0, slab).astype(BF16))
            slab = query_k[app, :, j * LANES : (j + 1) * LANES].astype(F32)
            query_parts.append(jnp.where(low, slab, 0.0).astype(BF16))
            query_parts.append(jnp.where(low, 0.0, slab).astype(BF16))
        keys, values = [], []
        read(key_k, app).wait()
        read(value_k, app).wait()
        for j in range(key_k.shape[-1] // LANES):
            slab = key_k[app, :, j * LANES : (j + 1) * LANES].astype(F32)
            keys.append(both_halves(slab, False).astype(BF16))
            keys.append(both_halves(slab, True).astype(BF16))
            slab = value_k[app, :, j * LANES : (j + 1) * LANES].astype(F32)
            values.append(both_halves(slab, False).astype(BF16))
            values.append(both_halves(slab, True).astype(BF16))
        cosine = cosine_ref[tick.table]
        sine = -sine_ref[tick.table]
        query_grads, key_grads, value_grads = [], [], []
        read(probs_k, app).wait()
        for kv in range(kv_heads):
            mixed = jnp.concatenate(mixed_parts[kv * share : (kv + 1) * share], axis=0)
            grouped = jnp.concatenate(query_parts[kv * share : (kv + 1) * share], axis=0)
            probs = probs_k[app, kv]
            probs_wide = probs.astype(F32)
            probs_grad = dot_t(mixed, values[kv])
            shared = jnp.sum(probs_wide * probs_grad, axis=-1, keepdims=True)
            score_grad = (probs_wide * (probs_grad - shared)).astype(BF16)
            pulled = dot(score_grad, keys[kv])
            query_grads += [pulled[i * rows : (i + 1) * rows] for i in range(share)]
            pulled = dot_rows(score_grad, grouped)
            key_grads.append(pulled + pltpu.roll(pulled, HEAD_DIM, 1))
            pulled = dot_rows(probs, mixed)
            value_grads.append(pulled + pltpu.roll(pulled, HEAD_DIM, 1))

        def put(target, parts, finish):
            count = len(parts)
            for j in range(count // 2):
                slab = jnp.where(low, parts[2 * j], parts[2 * j + 1])
                target[app, :, j * LANES : (j + 1) * LANES] = finish(slab).astype(BF16)
            if count % 2:
                target[app, :, (count - 1) * HEAD_DIM :] = finish(parts[-1])[:, :HEAD_DIM].astype(
                    BF16
                )
            store(target, app).start()

        put(query_b, query_grads, lambda slab: rotate(slab * SCALE, cosine, sine))
        put(key_b, key_grads, lambda slab: rotate(slab * SCALE, cosine, sine))
        put(value_b, value_grads, lambda slab: slab)
        pulled = dot(query_b[app], wq[...])
        pulled += dot(key_b[app], wk[...])
        pulled += dot(value_b[app], wv[...])
        read(hidden_k, app).wait()
        result, gain_rows = rms_backward(hidden_k[app], gain_attn[...], pulled, middle_grad)
        gains_b[app, 0] = gain_rows
        store(gains_b, app).start()
        grad_s[...] = result
        return carry

    @pl.when(tick.active)
    def _():
        for app in (1, 0):
            for buffer in (slopes_k, middle_k, query_k, key_k, value_k, probs_k, hidden_k):
                read(buffer, app).start()
        if edge_parts:

            @pl.when(tick.edge)
            def _():
                assemble(grad_s, edge_parts, sizes["tick"] * rows)
                row = lax.broadcasted_iota(jnp.int32, (rows, 1), 0)
                grad_s[...] = jnp.where(row < tick.bound(row, rows // 2), grad_s[...], 0.0)

        if inbound:

            @pl.when(jnp.logical_not(tick.edge))
            def _():
                grad_s[...] = inbound[0][...].astype(F32)

        mixed_s[:, mixed_s.shape[1] - LANES :] = jnp.zeros((rows, LANES), F32)
        lax.fori_loop(0, 2, apply, 0)
        out_round[...] = grad_s[...].astype(BF16)
        final = pltpu.make_async_copy(grad_s, out_full.at[slot], final_sem.at[0])
        when(tick.final, final.start)
        for buffer in buffers:
            store(buffer, 0).wait()
            store(buffer, 1).wait()
        when(tick.final, final.wait)


def transpose_to(target, source):
    strip = 256 if source.shape[1] % 256 == 0 else source.shape[1]
    for at in range(0, source.shape[1], strip):
        target[at : at + strip, :] = jnp.transpose(source[:, at : at + strip])


def load_kernel(*refs):
    count = (len(refs) - 2) // 2
    sources, targets, turned, sems = refs[:count], refs[count : 2 * count], refs[-2], refs[-1]
    copies = [
        pltpu.make_async_copy(source, target, sems.at[i])
        for i, (source, target) in enumerate(zip(sources, targets))
    ]
    for copy in reversed(copies):
        copy.start()
    copies[-1].wait()
    transpose_to(turned, targets[-1])
    for copy in copies[:-1]:
        copy.wait()


def turn_kernel(*refs):
    count = len(refs) // 2
    for source, target in zip(refs[:count], refs[count:]):
        transpose_to(target, source)


def vmem_array(shape, dtype):
    return pltpu.VMEM(tuple(shape), dtype)


def load_weights(weights):
    turned = weights[-1].shape[::-1]
    return pl.pallas_call(
        load_kernel,
        out_shape=[vmem_array(weight.shape, weight.dtype) for weight in weights]
        + [vmem_array(turned, weights[-1].dtype)],
        in_specs=[in_hbm() for _ in weights],
        out_specs=[in_vmem() for _ in range(len(weights) + 1)],
        scratch_shapes=[pltpu.SemaphoreType.DMA((len(weights),))],
        compiler_params=pltpu.CompilerParams(vmem_limit_bytes=12 * 2**20),
        name="load_weights",
    )(*[pltpu.with_memory_space_constraint(weight, pltpu.HBM) for weight in weights])


def turn_weights(weights):
    return pl.pallas_call(
        turn_kernel,
        out_shape=[vmem_array(weight.shape[::-1], weight.dtype) for weight in weights],
        in_specs=[in_vmem() for _ in weights],
        out_specs=[in_vmem() for _ in weights],
        compiler_params=pltpu.CompilerParams(vmem_limit_bytes=12 * 2**20),
        name="turn_weights",
    )(*[pltpu.with_memory_space_constraint(weight, pltpu.VMEM) for weight in weights])


def in_vmem():
    return pl.BlockSpec(memory_space=pltpu.VMEM)


def in_hbm():
    return pl.BlockSpec(memory_space=pltpu.HBM)


def buffers_for(shapes):
    return [pltpu.VMEM(tuple(shape.shape[1:]), shape.dtype) for shape in shapes]


def run_tick(
    kernel, sizes, lengths, tables, edge_parts, inbound, weights, reads, state, shapes, scratch, name
):
    rows, width = sizes["rows"], sizes["width"]
    aliased = [] if state is None else list(state)
    inbound = [] if inbound is None else [inbound]
    outs = [jax.ShapeDtypeStruct((rows, width), BF16)] + [
        pltpu.HBM(shape.shape, shape.dtype)
        for shape in (jax.ShapeDtypeStruct((CHUNKS, rows, width), F32), *shapes)
    ]
    scratch = scratch + buffers_for(reads) + buffers_for(shapes)
    if reads:
        scratch.append(pltpu.SemaphoreType.DMA((len(reads), 2)))
    scratch.append(pltpu.SemaphoreType.DMA((len(shapes), 2)))
    scratch.append(pltpu.SemaphoreType.DMA((1,)))
    blocks = [*tables, *edge_parts, *inbound]
    first_alias = 1 + len(blocks) + len(weights) + len(reads)
    sizes = dict(
        sizes,
        edge_parts=len(edge_parts),
        inbound=len(inbound),
        aliased=len(aliased),
        stores=len(shapes),
        reads=len(reads),
    )
    flops = 4 * rows * sum(int(np.prod(weight.shape)) for weight in weights)
    return pl.pallas_call(
        functools.partial(kernel, sizes),
        out_shape=outs,
        grid_spec=pltpu.PrefetchScalarGridSpec(
            num_scalar_prefetch=1,
            grid=(1,),
            in_specs=[in_vmem() for _ in (*blocks, *weights)]
            + [in_hbm() for _ in (*reads, *aliased)],
            out_specs=[in_vmem()] + [in_hbm() for _ in outs[1:]],
            scratch_shapes=scratch,
        ),
        input_output_aliases={first_alias + i: 1 + i for i in range(len(aliased))},
        compiler_params=pltpu.CompilerParams(
            dimension_semantics=("arbitrary",), vmem_limit_bytes=18 * 2**20
        ),
        cost_estimate=pl.CostEstimate(
            flops=flops, bytes_accessed=flops // (2 * rows), transcendentals=0
        ),
        name=name,
    )(
        lengths,
        *blocks,
        *[pltpu.with_memory_space_constraint(weight, pltpu.VMEM) for weight in weights],
        *[pltpu.with_memory_space_constraint(array, pltpu.HBM) for array in (*reads, *aliased)],
    )


def rope_tables(rows):
    segment = rows // 2
    frequency = rope_base ** (-np.arange(HALF, dtype=np.float64) / HALF)
    positions = np.stack([np.arange(rows) % segment, np.arange(rows)]).astype(np.float64)
    angles = np.tile(positions[:, :, None] * frequency, (1, 1, LANES // HALF))
    sign = np.where(np.arange(LANES) % HEAD_DIM < HALF, -1.0, 1.0)
    return (
        jnp.asarray(np.cos(angles), F32),
        jnp.asarray(np.sin(angles) * sign, F32),
    )


def gather_to(block, target):
    return [
        block if source == target else lax.ppermute(block, "pipe", [(source, target)])
        for source in range(lax.axis_size("pipe"))
    ]


def swap_neighbours(mine_and_theirs, axis):
    devices = lax.axis_size("dp")
    odd = lax.axis_index("dp") % 2
    theirs = lax.dynamic_index_in_dim(mine_and_theirs, 1 - odd, axis, keepdims=False)
    mine = lax.dynamic_index_in_dim(mine_and_theirs, odd, axis, keepdims=False)
    return mine + lax.ppermute(theirs, "dp", [(i, i ^ 1) for i in range(devices)])


def line_scatter(value):
    devices = lax.axis_size("dp")
    lines = [list(range(first, devices, 2)) for first in range(2)]
    return lax.psum_scatter(
        value, "dp", scatter_dimension=0, tiled=True, axis_index_groups=lines
    )


def pair_first(value):
    devices = lax.axis_size("dp")
    rows, columns = value.shape
    part = swap_neighbours(value.reshape(devices // 2, 2, rows // devices, columns), 1)
    return line_scatter(part.reshape(rows // 2, columns)).astype(F32)


def line_first(value):
    devices = lax.axis_size("dp")
    rows, columns = value.shape
    part = line_scatter(value)
    return swap_neighbours(part.reshape(2, rows // devices, columns), 0).astype(F32)


def per_device(
    inputs,
    cotangent,
    lengths,
    w_query,
    w_key,
    w_value,
    w_proj,
    w_gate,
    w_up,
    w_down,
    gain_attn,
    gain_mlp,
):
    sections = lax.axis_size("pipe")
    section = lax.axis_index("pipe")
    total_rows, columns = inputs.shape
    width = columns * sections
    rows = 2 * total_rows // (MICRO + 1)
    segment = rows // 2
    kv_width = w_key.shape[-1]
    ff = w_gate.shape[-1]
    kv_heads = kv_width // HEAD_DIM
    share = width // kv_width
    depth_step = 2
    ticks = CHUNKS + depth_step * (sections - 1)
    sizes = dict(
        rows=rows, width=width, ff_step=ff // 4, sections=sections, depth_step=depth_step
    )
    tables = (*rope_tables(rows), gain_attn, gain_mlp)
    group = lengths[0]
    input_parts = gather_to(inputs, 0)
    wq, wk_t, wv_t, wp, wg, wu, wd_t, wd = load_weights(
        (
            w_query[0],
            jnp.swapaxes(w_key[0], 0, 1),
            jnp.swapaxes(w_value[0], 0, 1),
            w_proj[0],
            w_gate[0],
            w_up[0],
            jnp.swapaxes(w_down[0], 0, 1),
        )
    )
    wq_t, wp_t, wg_t, wu_t = turn_weights((wq, wp, wg, wu))
    forward_weights = (wq, wk_t, wv_t, wp, wg, wu, wd)
    backward_weights = (wq_t, wk_t, wv_t, wp_t, wg_t, wu_t, wd_t)

    def stored(*shape, dtype=BF16):
        return jax.ShapeDtypeStruct((CHUNKS, 2) + shape, dtype)

    query_pad, kv_pad = round_up(width, LANES), round_up(kv_width, LANES)
    forward_shapes = [
        stored(rows, width, dtype=F32),
        stored(rows, width),
        stored(rows, query_pad),
        stored(rows, kv_pad),
        stored(rows, kv_pad),
        stored(kv_heads, share * rows, rows),
        stored(rows, width),
        stored(rows, width, dtype=F32),
        stored(rows, width),
        stored(2, rows, ff),
        stored(rows, ff),
    ]
    forward_scratch = [
        pltpu.VMEM((rows, width), F32),
        pltpu.VMEM((rows, query_pad), F32),
        pltpu.VMEM((rows, kv_pad), F32),
        pltpu.VMEM((rows, kv_pad), F32),
    ]
    sent = {}
    state = None
    for tick in range(ticks):
        rounded, *state = run_tick(
            forward_kernel,
            dict(sizes, tick=tick, backward=False),
            lengths,
            tables,
            input_parts if tick < CHUNKS else (),
            sent.get(tick - depth_step),
            forward_weights,
            (),
            state,
            forward_shapes,
            forward_scratch,
            "layer_pair_forward",
        )
        route = [
            (s, s + 1) for s in range(sections - 1) if 0 <= tick - depth_step * s < CHUNKS
        ]
        if route:
            sent[tick] = lax.ppermute(rounded, "pipe", route)
        if tick == 0:
            late_cotangent, _ = lax.optimization_barrier((cotangent, rounded))
            cotangent_parts = gather_to(late_cotangent, sections - 1)
    results = state[0]
    (
        hidden,
        normed_attn,
        query_rot,
        key_rot,
        value_rows,
        probs,
        mixed,
        middle,
        normed_mlp,
        slopes,
        inner,
    ) = state[1:]

    backward_shapes = [
        stored(rows, width),
        stored(rows, ff),
        stored(rows, ff),
        stored(rows, width),
        stored(rows, width),
        stored(rows, kv_width),
        stored(rows, kv_width),
        stored(2, 8, width, dtype=F32),
    ]
    backward_scratch = [
        pltpu.VMEM((rows, width), F32),
        pltpu.VMEM((rows, query_pad), F32),
    ]
    reads = (hidden, query_rot, key_rot, value_rows, probs, middle, slopes)
    sent = {}
    state = None
    for tick in range(ticks):
        rounded, *state = run_tick(
            backward_kernel,
            dict(sizes, tick=tick, backward=True),
            lengths,
            tables,
            cotangent_parts if tick < CHUNKS else (),
            sent.get(tick - depth_step),
            backward_weights,
            reads,
            state,
            backward_shapes,
            backward_scratch,
            "layer_pair_backward",
        )
        route = [
            (s, s - 1)
            for s in range(1, sections)
            if 0 <= tick - depth_step * (sections - 1 - s) < CHUNKS
        ]
        if route:
            sent[tick] = lax.ppermute(rounded, "pipe", route)
    input_grads = state[0]
    branch, gate_grad, up_grad, attn_grad, query_grad, key_grad, value_grad, gains = state[1:]

    def all_rows(store):
        return store.reshape(CHUNKS * 2 * rows, store.shape[-1])

    def product(left, right):
        return dot_rows(all_rows(left), all_rows(right)).astype(BF16)

    attention_grads = jnp.concatenate(
        [all_rows(query_grad), all_rows(key_grad), all_rows(value_grad)], axis=1
    )
    grad_attention = line_first(dot_rows(all_rows(normed_attn), attention_grads).astype(BF16))
    grad_gate = pair_first(product(normed_mlp, gate_grad))
    grad_up = pair_first(product(normed_mlp, up_grad))
    grad_down = pair_first(product(inner, branch))
    grad_proj = pair_first(product(mixed, attn_grad))
    grad_query = grad_attention[:, :width]
    grad_key = grad_attention[:, width : width + kv_width]
    grad_value = grad_attention[:, width + kv_width :]
    gain_sums = jnp.sum(gains, axis=(0, 1, 3))
    grad_gain_attn = lax.psum_scatter(gain_sums[0], "dp", scatter_dimension=0, tiled=True)
    grad_gain_mlp = lax.psum_scatter(gain_sums[1], "dp", scatter_dimension=0, tiled=True)

    def spread(store, source):
        rows_all = store.reshape(CHUNKS * rows, width)[:total_rows]
        own = rows_all[:, source * columns : (source + 1) * columns]
        arrived = jnp.where(section == source, own, 0.0)
        for target in range(sections):
            if target != source:
                block = rows_all[:, target * columns : (target + 1) * columns]
                arrived = arrived + lax.ppermute(block, "pipe", [(source, target)])
        return arrived

    position = jnp.arange(total_rows)
    long_rows = position < rows
    offsets = jnp.where(long_rows, position, position % segment)
    micro = jnp.where(long_rows, 0, position // segment - 1)
    bound = jnp.zeros_like(position)
    for m in range(MICRO):
        bound = jnp.where(micro == m, group[m], bound)
    valid = (offsets < bound)[:, None]
    results, input_grads, _ = lax.optimization_barrier((results, input_grads, grad_gate))
    layer_output = jnp.where(valid, spread(results, sections - 1), 0.0)
    grad_input = spread(input_grads, 0)
    return (
        layer_output,
        grad_input,
        grad_query[None],
        grad_key[None],
        grad_value[None],
        grad_proj[None],
        grad_gate[None],
        grad_up[None],
        grad_down[None],
        grad_gain_attn[None],
        grad_gain_mlp[None],
    )


def solution(mesh):
    placed = (
        P("dp", "pipe"),
        P("dp", "pipe"),
        P("dp", None),
        P("pipe", None, None),
        P("pipe", None, None),
        P("pipe", None, None),
        P("pipe", None, None),
        P("pipe", None, None),
        P("pipe", None, None),
        P("pipe", None, None),
        P("pipe", None),
        P("pipe", None),
    )
    return jax.shard_map(
        per_device,
        mesh=mesh,
        in_specs=placed,
        out_specs=(
            P("dp", "pipe"),
            P("dp", "pipe"),
            P("pipe", "dp", None),
            P("pipe", "dp", None),
            P("pipe", "dp", None),
            P("pipe", "dp", None),
            P("pipe", "dp", None),
            P("pipe", "dp", None),
            P("pipe", "dp", None),
            P("pipe", "dp"),
            P("pipe", "dp"),
        ),
        check_vma=False,
    )
```

```python
import functools

import jax
import jax.numpy as jnp
import numpy as np
from jax import lax
from jax.experimental import pallas as pl
from jax.experimental.layout import Layout, with_layout_constraint
from jax.experimental.pallas import tpu as pltpu
from jax.sharding import PartitionSpec as P

HEAD_DIM = 64
HALF = HEAD_DIM // 2
LANES = 128
MICRO = 4
CHUNKS = 3
SCALE = HEAD_DIM**-0.5
BF16 = jnp.bfloat16
F32 = jnp.float32

epsilon = 1e-05
rope_base = 10000.0
masked_score = -1e30

def round_up(value, multiple):
    return -(-value // multiple) * multiple


def dot(left, right):
    return jnp.dot(left, right, preferred_element_type=F32)


def dot_t(left, right):
    return lax.dot_general(left, right, (((1,), (1,)), ((), ())), preferred_element_type=F32)


def dot_rows(left, right):
    return lax.dot_general(left, right, (((0,), (0,)), ((), ())), preferred_element_type=F32)


def lane_ids(rows):
    return lax.broadcasted_iota(jnp.int32, (rows, LANES), 1)


def in_low_half(rows):
    return lane_ids(rows) < HEAD_DIM


def rotate(slab, cosine, signed_sine):
    first = (lane_ids(slab.shape[0]) % HEAD_DIM) < HALF
    partner = jnp.where(
        first, pltpu.roll(slab, LANES - HALF, 1), pltpu.roll(slab, HALF, 1)
    )
    return slab * cosine + partner * signed_sine


def both_halves(slab, upper):
    swapped = pltpu.roll(slab, HEAD_DIM, 1)
    low = in_low_half(slab.shape[0])
    return jnp.where(low, swapped, slab) if upper else jnp.where(low, slab, swapped)


def sort_halves(slab, j, low, heads, kv_heads, key_rows, queries, keys, values):
    for head in (2 * j, 2 * j + 1):
        upper = head % 2 == 1
        if head < heads:
            kept = jnp.where(low, 0.0, slab) if upper else jnp.where(low, slab, 0.0)
            queries.append(kept.astype(BF16))
        elif head < heads + kv_heads:
            keys.append(pad_rows(both_halves(slab, upper).astype(BF16), key_rows))
        elif head < heads + 2 * kv_heads:
            values.append(pad_rows(both_halves(slab, upper).astype(BF16), key_rows))


def reciprocal_rms(value):
    return lax.rsqrt(jnp.mean(value * value, axis=-1, keepdims=True) + epsilon)


class Tick:
    def __init__(self, sizes, lengths):
        sections, depth_step, segment = sizes["sections"], sizes["depth_step"], sizes["rows"] // 2
        section = lax.axis_index("pipe")
        depth = sections - 1 - section if sizes["backward"] else section
        chunk = sizes["tick"] - depth_step * depth
        self.active = (chunk >= 0) & (chunk < CHUNKS)
        self.slot = jnp.clip(chunk, 0, CHUNKS - 1)
        self.edge = depth == 0
        self.final = depth == sections - 1
        self.is_long = self.slot == 0
        self.table = jnp.where(self.is_long, 1, 0)
        self.first_length = jnp.where(
            self.is_long, lengths[0, 0], jnp.where(self.slot == 1, lengths[0, 1], lengths[0, 3])
        )
        self.second_length = jnp.where(self.slot == 1, lengths[0, 2], segment)

    def bound(self, position, segment):
        return jnp.where(
            self.is_long,
            self.first_length,
            jnp.where(position < segment, self.first_length, self.second_length + segment),
        )


def score_bias(tick, query_rows, key_rows):
    query = lax.broadcasted_iota(jnp.int32, (query_rows, key_rows), 0)
    key = lax.broadcasted_iota(jnp.int32, (query_rows, key_rows), 1)
    segment = key_rows // 2
    start = jnp.where(tick.is_long, 0, jnp.where(query < segment, 0, segment))
    allowed = (key <= query) & (key < tick.bound(key, segment)) & (key >= start)
    return jnp.where(allowed, 0.0, masked_score).astype(F32)


def assemble(target, parts, at):
    count = min(target.shape[0], parts[0].shape[0] - at)
    target[:count, :] = jnp.concatenate(
        [part[at : at + count, :].astype(F32) for part in parts], axis=1
    )


def kept_at(kind, buffer, array, app, slot, rows, chunk, columns=None):
    columns = pl.ds(0, buffer.shape[-1]) if columns is None else columns
    if kind == "gains":
        return buffer.at[app], array.at[slot, app]
    if kind == "probs":
        taken = pl.ds(0, buffer.shape[2] * rows // chunk)
        return buffer.at[app, :, taken], array.at[slot, app, :, taken]
    at = pl.ds(pl.multiple_of(slot * chunk, chunk), rows)
    if kind == "slopes":
        return buffer.at[app, :, pl.ds(0, rows), columns], array.at[app, :, at, columns]
    return buffer.at[app, pl.ds(0, rows), columns], array.at[app, at, columns]


def chunk_sizes(sizes):
    full, total = sizes["rows"], sizes["total_rows"]
    found = {}
    for depth in range(sizes["sections"]):
        slot = sizes["tick"] - sizes["depth_step"] * depth
        if 0 <= slot < CHUNKS:
            found.setdefault(min(full, total - slot * full), []).append(slot)
    return found


def pad_rows(value, rows):
    missing = rows - value.shape[0]
    if not missing:
        return value
    return jnp.concatenate([value, jnp.zeros((missing, value.shape[1]), value.dtype)], axis=0)


def when(condition, action):
    pl.when(condition)(action)


def run_active(tick, sizes, run):
    found = chunk_sizes(sizes)
    for rows, slots in found.items():
        mine = functools.reduce(jnp.logical_or, [tick.slot == slot for slot in slots])
        when(tick.active & mine, functools.partial(run, rows))


def final_at(rows_s, array, slot, rows):
    chunk = rows_s.shape[0]
    at = pl.ds(pl.multiple_of(slot * chunk, chunk), rows)
    return rows_s.at[pl.ds(0, rows)], array.at[at]


def forward_kernel(sizes, lengths, *refs):
    tick = Tick(sizes, lengths)
    refs = list(refs)

    def take(count):
        taken = refs[:count]
        del refs[:count]
        return taken

    cosine_ref, sine_ref, gain_attn, gain_mlp = take(4)
    edge_parts, inbound = take(sizes["edge_parts"]), take(sizes["inbound"])
    w_heads, wp, wg, wu, wd = take(5)
    take(sizes["aliased"])
    out_round, out_full = take(2)
    stores = take(sizes["stores"])
    hidden_s, heads_s = take(2)
    buffers = take(sizes["stores"])
    (
        hidden_b,
        normed_attn_b,
        heads_b,
        probs_b,
        mixed_b,
        middle_b,
        normed_mlp_b,
        slopes_b,
        inner_b,
    ) = buffers
    store_sems, final_sem = refs
    chunk, width = hidden_s.shape
    heads = width // HEAD_DIM
    all_width = w_heads.shape[1]
    kv_heads = (all_width // HEAD_DIM - heads) // 2
    share = heads // kv_heads
    ff = wg.shape[1]
    slot = tick.slot

    step = sizes["ff_step"]

    def store(buffer, app, rows, part=None):
        i = [other is buffer for other in buffers].index(True)
        columns = None if part is None else pl.ds(part * step, step)
        source, target = kept_at(
            sizes["store_kinds"][i], buffer, stores[i], app, slot, rows, chunk, columns
        )
        return pltpu.make_async_copy(source, target, store_sems.at[i, app, part or 0])

    def apply(rows, app, carry):
        hidden = hidden_s[:rows]
        hidden_b[app, :rows] = hidden
        store(hidden_b, app, rows).start()
        normed = (hidden * reciprocal_rms(hidden) * gain_attn[...]).astype(BF16)
        normed_attn_b[app, :rows] = normed
        store(normed_attn_b, app, rows).start()
        heads_s[:rows, :all_width] = dot(normed, w_heads[...])
        cosine = cosine_ref[tick.table, :rows]
        sine = sine_ref[tick.table, :rows]
        low = in_low_half(rows)
        query_parts, keys, values = [], [], []
        for j in range(heads_s.shape[1] // LANES):
            slab = heads_s[:rows, j * LANES : (j + 1) * LANES]
            if 2 * j < heads + kv_heads:
                slab = rotate(slab, cosine, sine)
            heads_b[app, :rows, j * LANES : (j + 1) * LANES] = slab.astype(BF16)
            sort_halves(slab, j, low, heads, kv_heads, chunk, query_parts, keys, values)
        store(heads_b, app, rows).start()
        bias = score_bias(tick, rows, chunk)
        bias = jnp.concatenate([bias] * share, axis=0)
        mixed_parts = []
        for kv in range(kv_heads):
            grouped = jnp.concatenate(query_parts[kv * share : (kv + 1) * share], axis=0)
            scores = dot_t(grouped, keys[kv]) * SCALE + bias
            exponent = jnp.exp(scores - jnp.max(scores, axis=-1, keepdims=True))
            total = jnp.sum(exponent, axis=-1, keepdims=True)
            probs = (exponent * (1.0 / total)).astype(BF16)
            probs_b[app, kv, : share * rows] = probs
            mixed = dot(probs, values[kv])
            mixed_parts += [mixed[i * rows : (i + 1) * rows] for i in range(share)]
        store(probs_b, app, rows).start()
        for j in range(heads // 2):
            mixed_b[app, :rows, j * LANES : (j + 1) * LANES] = jnp.where(
                low, mixed_parts[2 * j], mixed_parts[2 * j + 1]
            ).astype(BF16)
        if heads % 2:
            mixed_b[app, :rows, width - HEAD_DIM :] = mixed_parts[-1][:, :HEAD_DIM].astype(BF16)
        store(mixed_b, app, rows).start()
        middle = hidden + dot(mixed_b[app, :rows], wp[...])
        middle_b[app, :rows] = middle
        store(middle_b, app, rows).start()
        normed = (middle * reciprocal_rms(middle) * gain_mlp[...]).astype(BF16)
        normed_mlp_b[app, :rows] = normed
        store(normed_mlp_b, app, rows).start()
        for part, at in enumerate(range(0, ff, step)):
            gate = dot(normed, wg[:, at : at + step])
            up = dot(normed, wu[:, at : at + step])
            sigma = 1.0 / (1.0 + jnp.exp(-gate))
            silu = gate * sigma
            inner_b[app, :rows, at : at + step] = (silu * up).astype(BF16)
            slopes_b[app, 0, :rows, at : at + step] = (
                up * (sigma * (1.0 + gate * (1.0 - sigma)))
            ).astype(BF16)
            slopes_b[app, 1, :rows, at : at + step] = silu.astype(BF16)
            store(inner_b, app, rows, part).start()
            store(slopes_b, app, rows, part).start()
        hidden_s[:rows] = middle + dot(inner_b[app, :rows], wd[...])
        return carry

    def run(rows):
        if edge_parts:

            @pl.when(tick.edge)
            def _():
                assemble(hidden_s, edge_parts, sizes["tick"] * chunk)

        if inbound:

            @pl.when(jnp.logical_not(tick.edge))
            def _():
                hidden_s[:rows] = inbound[0][:rows].astype(F32)

        heads_s[:, heads_s.shape[1] - LANES :] = jnp.zeros((chunk, LANES), F32)
        lax.fori_loop(0, 2, functools.partial(apply, rows), 0)
        out_round[:rows] = hidden_s[:rows].astype(BF16)
        source, target = final_at(hidden_s, out_full, slot, rows)
        final = pltpu.make_async_copy(source, target, final_sem.at[0])
        when(tick.final, final.start)
        for app in (0, 1):
            for buffer in buffers[:-2]:
                store(buffer, app, rows).wait()
            for part in range(ff // step):
                store(inner_b, app, rows, part).wait()
                store(slopes_b, app, rows, part).wait()
        when(tick.final, final.wait)

    run_active(tick, sizes, run)


def backward_kernel(sizes, lengths, *refs):
    tick = Tick(sizes, lengths)
    refs = list(refs)

    def take(count):
        taken = refs[:count]
        del refs[:count]
        return taken

    cosine_ref, sine_ref, gain_attn, gain_mlp = take(4)
    edge_parts, inbound = take(sizes["edge_parts"]), take(sizes["inbound"])
    w_heads, wp, wg, wu, wd = take(5)
    saved = take(sizes["reads"])
    take(sizes["aliased"])
    out_round, out_full = take(2)
    stores = take(sizes["stores"])
    grad_s, mixed_s, inner_s = take(3)
    kept = take(sizes["reads"])
    hidden_k, heads_k, probs_k, middle_k, slopes_k = kept
    buffers = take(sizes["stores"])
    branch_b, gate_b, up_b, attn_b, heads_b, gains_b = buffers
    read_sems, store_sems, final_sem = refs
    chunk, width = grad_s.shape
    heads = width // HEAD_DIM
    all_width = w_heads.shape[0]
    kv_heads = (all_width // HEAD_DIM - heads) // 2
    share = heads // kv_heads
    ff = wd.shape[1]
    slot = tick.slot

    def read(buffer, app, rows):
        i = [other is buffer for other in kept].index(True)
        kind = sizes["read_kinds"][i]
        target, source = kept_at(kind, buffer, saved[i], app, slot, rows, chunk)
        return pltpu.make_async_copy(source, target, read_sems.at[i, app])

    def store(buffer, app, rows):
        i = [other is buffer for other in buffers].index(True)
        kind = sizes["store_kinds"][i]
        source, target = kept_at(kind, buffer, stores[i], app, slot, rows, chunk)
        return pltpu.make_async_copy(source, target, store_sems.at[i, app, 0])

    def rms_backward(value, gain, grad, running):
        scale = reciprocal_rms(value)
        unit = value * scale
        pulled = grad * gain
        gain_terms = grad * unit
        gain_rows = jnp.sum(gain_terms.reshape(grad.shape[0] // 8, 8, width), axis=0)
        shared = jnp.mean(gain_terms * gain, axis=-1, keepdims=True)
        return running + scale * (pulled - unit * shared), gain_rows

    def apply(rows, step_id, carry):
        app = 1 - step_id
        low = in_low_half(rows)
        grad_top = grad_s[:rows]
        branch = grad_top.astype(BF16)
        branch_b[app, :rows] = branch
        store(branch_b, app, rows).start()
        step = sizes["ff_step"]
        inner_s[:rows] = dot(branch, wd[...])
        read(slopes_k, app, rows).wait()
        for at in range(0, ff, step):
            inner_grad = inner_s[:rows, at : at + step]
            gate_b[app, :rows, at : at + step] = (
                inner_grad * slopes_k[app, 0, :rows, at : at + step].astype(F32)
            ).astype(BF16)
            up_b[app, :rows, at : at + step] = (
                inner_grad * slopes_k[app, 1, :rows, at : at + step].astype(F32)
            ).astype(BF16)
        store(gate_b, app, rows).start()
        store(up_b, app, rows).start()
        pulled = dot(gate_b[app, :rows], wg[...])
        pulled += dot(up_b[app, :rows], wu[...])
        read(middle_k, app, rows).wait()
        middle_grad, gain_rows = rms_backward(
            middle_k[app, :rows], gain_mlp[...], pulled, grad_top
        )
        gains_b[app, 1] = gain_rows
        attn_grad = middle_grad.astype(BF16)
        attn_b[app, :rows] = attn_grad
        store(attn_b, app, rows).start()
        mixed_s[:rows, :width] = dot(attn_grad, wp[...])
        mixed_parts, query_parts, keys, values = [], [], [], []
        for j in range(mixed_s.shape[1] // LANES):
            slab = mixed_s[:rows, j * LANES : (j + 1) * LANES]
            mixed_parts.append(jnp.where(low, slab, 0.0).astype(BF16))
            mixed_parts.append(jnp.where(low, 0.0, slab).astype(BF16))
        read(heads_k, app, rows).wait()
        for j in range(heads_k.shape[-1] // LANES):
            slab = heads_k[app, :rows, j * LANES : (j + 1) * LANES].astype(F32)
            sort_halves(slab, j, low, heads, kv_heads, chunk, query_parts, keys, values)
        cosine = cosine_ref[tick.table, :rows]
        sine = -sine_ref[tick.table, :rows]
        ones = jnp.ones((chunk, LANES), BF16)
        query_grads, key_grads, value_grads = [], [], []
        read(probs_k, app, rows).wait()
        for kv in range(kv_heads):
            mixed = jnp.concatenate(mixed_parts[kv * share : (kv + 1) * share], axis=0)
            grouped = jnp.concatenate(query_parts[kv * share : (kv + 1) * share], axis=0)
            probs = probs_k[app, kv, : share * rows]
            probs_wide = probs.astype(F32)
            probs_grad = dot_t(mixed, values[kv])
            weighted = probs_wide * probs_grad
            shared = dot(weighted.astype(BF16), ones)
            score_grad = (weighted - probs_wide * shared).astype(BF16)
            pulled = dot(score_grad, keys[kv])
            query_grads += [pulled[i * rows : (i + 1) * rows] for i in range(share)]
            pulled = dot_rows(score_grad, grouped)[:rows]
            key_grads.append(pulled + pltpu.roll(pulled, HEAD_DIM, 1))
            pulled = dot_rows(probs, mixed)[:rows]
            value_grads.append(pulled + pltpu.roll(pulled, HEAD_DIM, 1))

        parts = query_grads + key_grads + value_grads
        for j in range(len(parts) // 2):
            slab = jnp.where(low, parts[2 * j], parts[2 * j + 1])
            if 2 * j < heads + kv_heads:
                slab = rotate(slab * SCALE, cosine, sine)
            heads_b[app, :rows, j * LANES : (j + 1) * LANES] = slab.astype(BF16)
        if len(parts) % 2:
            heads_b[app, :rows, all_width - HEAD_DIM :] = parts[-1][:, :HEAD_DIM].astype(BF16)
        store(heads_b, app, rows).start()
        pulled = dot(heads_b[app, :rows], w_heads[...])
        read(hidden_k, app, rows).wait()
        result, gain_rows = rms_backward(
            hidden_k[app, :rows], gain_attn[...], pulled, middle_grad
        )
        gains_b[app, 0] = gain_rows
        store(gains_b, app, rows).start()
        grad_s[:rows] = result
        return carry

    def run(rows):
        for app in (1, 0):
            for buffer in (slopes_k, middle_k, heads_k, probs_k, hidden_k):
                read(buffer, app, rows).start()
        if edge_parts:

            @pl.when(tick.edge)
            def _():
                assemble(grad_s, edge_parts, sizes["tick"] * chunk)
                row = lax.broadcasted_iota(jnp.int32, (chunk, 1), 0)
                grad_s[...] = jnp.where(row < tick.bound(row, chunk // 2), grad_s[...], 0.0)

        if inbound:

            @pl.when(jnp.logical_not(tick.edge))
            def _():
                grad_s[:rows] = inbound[0][:rows].astype(F32)

        mixed_s[:, mixed_s.shape[1] - LANES :] = jnp.zeros((chunk, LANES), F32)
        lax.fori_loop(0, 2, functools.partial(apply, rows), 0)
        out_round[:rows] = grad_s[:rows].astype(BF16)
        source, target = final_at(grad_s, out_full, slot, rows)
        final = pltpu.make_async_copy(source, target, final_sem.at[0])
        when(tick.final, final.start)
        for buffer in buffers:
            store(buffer, 0, rows).wait()
            store(buffer, 1, rows).wait()
        when(tick.final, final.wait)

    run_active(tick, sizes, run)


def transpose_to(target, source):
    for at in range(0, source.shape[1], 256):
        end = min(at + 256, source.shape[1])
        target[at:end, :] = jnp.transpose(source[:, at:end])


def load_kernel(extras, *refs):
    key_t, value_t, query, proj, gate, up, down_t = refs[:7]
    extra_in, refs = refs[7 : 7 + extras], refs[7 + extras :]
    heads_t, heads, proj_v, gate_v, up_v, down_tv, down = refs[:7]
    extra_out, (query_v, sems) = refs[7 : 7 + extras], refs[7 + extras :]
    width, kv_width = query.shape[1], key_t.shape[0]
    pairs = (
        (down_t, down_tv),
        (query, query_v),
        (key_t, heads_t.at[pl.ds(width, kv_width)]),
        (value_t, heads_t.at[pl.ds(width + kv_width, kv_width)]),
        (proj, proj_v),
        (gate, gate_v),
        (up, up_v),
        *zip(extra_in, extra_out),
    )
    copies = [
        pltpu.make_async_copy(source, target, sems.at[i])
        for i, (source, target) in enumerate(pairs)
    ]
    for copy in copies:
        copy.start()
    copies[0].wait()
    transpose_to(down, down_tv)
    copies[1].wait()
    transpose_to(heads_t, query_v)
    copies[2].wait()
    copies[3].wait()
    transpose_to(heads, heads_t)
    for copy in copies[4:]:
        copy.wait()


def turn_kernel(first, count, *refs):
    sources, targets = refs[:count], refs[-count:]

    @pl.when((lax.axis_index("pipe") == 0) == first)
    def _():
        for source, target in zip(sources, targets):
            transpose_to(target, source)


def load_weights(query, key_t, value_t, proj, gate, up, down_t, *extra):
    sources = (key_t, value_t, query, proj, gate, up, down_t, *extra)
    all_width = query.shape[1] + 2 * key_t.shape[0]
    shapes = (
        (all_width, query.shape[0]),
        (query.shape[0], all_width),
        proj.shape,
        gate.shape,
        up.shape,
        down_t.shape,
        down_t.shape[::-1],
    )
    outs = [pltpu.VMEM(tuple(shape), BF16) for shape in shapes]
    outs += [pltpu.VMEM(array.shape, array.dtype) for array in extra]
    return pl.pallas_call(
        functools.partial(load_kernel, len(extra)),
        out_shape=outs,
        in_specs=[in_hbm() for _ in sources],
        out_specs=[in_vmem() for _ in outs],
        scratch_shapes=[
            pltpu.VMEM(query.shape, BF16),
            pltpu.SemaphoreType.DMA((len(sources),)),
        ],
        compiler_params=pltpu.CompilerParams(vmem_limit_bytes=12 * 2**20),
        name="load_weights",
    )(*[pltpu.with_memory_space_constraint(array, pltpu.HBM) for array in sources])


def turn_weights(weights, first, turned=()):
    count = len(weights)
    return pl.pallas_call(
        functools.partial(turn_kernel, first, count),
        out_shape=[pltpu.VMEM(tuple(weight.shape[::-1]), BF16) for weight in weights],
        in_specs=[in_vmem() for _ in (*weights, *turned)],
        out_specs=[in_vmem() for _ in weights],
        input_output_aliases={count + i: i for i in range(len(turned))},
        compiler_params=pltpu.CompilerParams(vmem_limit_bytes=12 * 2**20),
        name="turn_weights",
    )(*[pltpu.with_memory_space_constraint(weight, pltpu.VMEM) for weight in (*weights, *turned)])


def in_vmem():
    return pl.BlockSpec(memory_space=pltpu.VMEM)


def in_hbm():
    return pl.BlockSpec(memory_space=pltpu.HBM)


def kind_of(array):
    return {5: "probs" if array.dtype == BF16 else "gains", 4: "slopes", 3: "rows"}[len(array.shape)]


def buffers_for(arrays, rows):
    shapes = []
    for array in arrays:
        kind, shape = kind_of(array), tuple(array.shape)
        if kind in ("probs", "gains"):
            shapes.append(shape[1:])
        else:
            shapes.append(shape[:-2] + (rows, shape[-1]))
    return [pltpu.VMEM(shape, array.dtype) for shape, array in zip(shapes, arrays)]


def run_tick(
    kernel, sizes, lengths, tables, edge_parts, inbound, weights, reads, state, shapes, scratch, name
):
    rows, width = sizes["rows"], sizes["width"]
    aliased = [] if state is None else list(state)
    inbound = [] if inbound is None else [inbound]
    outs = [jax.ShapeDtypeStruct((rows, width), BF16)] + [
        pltpu.HBM(shape.shape, shape.dtype)
        for shape in (jax.ShapeDtypeStruct((sizes["total_rows"], width), F32), *shapes)
    ]
    scratch = scratch + buffers_for(reads, rows) + buffers_for(shapes, rows)
    if reads:
        scratch.append(pltpu.SemaphoreType.DMA((len(reads), 2)))
    scratch.append(pltpu.SemaphoreType.DMA((len(shapes), 2, 2)))
    scratch.append(pltpu.SemaphoreType.DMA((1,)))
    blocks = [*tables, *edge_parts, *inbound]
    tables = [pltpu.with_memory_space_constraint(array, pltpu.VMEM) for array in tables]
    first_alias = 1 + len(blocks) + len(weights) + len(reads)
    sizes = dict(
        sizes,
        edge_parts=len(edge_parts),
        inbound=len(inbound),
        aliased=len(aliased),
        stores=len(shapes),
        reads=len(reads),
        store_kinds=[kind_of(shape) for shape in shapes],
        read_kinds=[kind_of(read) for read in reads],
    )
    flops = 4 * rows * sum(int(np.prod(weight.shape)) for weight in weights)
    return pl.pallas_call(
        functools.partial(kernel, sizes),
        out_shape=outs,
        grid_spec=pltpu.PrefetchScalarGridSpec(
            num_scalar_prefetch=1,
            grid=(1,),
            in_specs=[in_vmem() for _ in (*blocks, *weights)]
            + [in_hbm() for _ in (*reads, *aliased)],
            out_specs=[in_vmem()] + [in_hbm() for _ in outs[1:]],
            scratch_shapes=scratch,
        ),
        input_output_aliases={first_alias + i: 1 + i for i in range(len(aliased))},
        compiler_params=pltpu.CompilerParams(
            dimension_semantics=("arbitrary",), vmem_limit_bytes=18 * 2**20
        ),
        cost_estimate=pl.CostEstimate(
            flops=flops, bytes_accessed=flops // (2 * rows), transcendentals=0
        ),
        name=name,
    )(
        lengths,
        *tables,
        *edge_parts,
        *inbound,
        *[pltpu.with_memory_space_constraint(weight, pltpu.VMEM) for weight in weights],
        *[pltpu.with_memory_space_constraint(array, pltpu.HBM) for array in (*reads, *aliased)],
    )


def rope_tables(rows):
    segment = rows // 2
    frequency = rope_base ** (-np.arange(HALF, dtype=np.float64) / HALF)
    positions = np.stack([np.arange(rows) % segment, np.arange(rows)]).astype(np.float64)
    angles = np.tile(positions[:, :, None] * frequency, (1, 1, LANES // HALF))
    sign = np.where(np.arange(LANES) % HEAD_DIM < HALF, -1.0, 1.0)
    return (
        jnp.asarray(np.cos(angles), F32),
        jnp.asarray(np.sin(angles) * sign, F32),
    )


def gather_ends(inputs, cotangent):
    sections, section = lax.axis_size("pipe"), lax.axis_index("pipe")
    last = sections - 1
    input_parts, cotangent_parts = [inputs] * sections, [cotangent] * sections
    for source in range(1, sections):
        mirror = last - source
        if mirror == source:
            input_parts[source] = lax.ppermute(inputs, "pipe", [(source, 0)])
            cotangent_parts[source] = lax.ppermute(cotangent, "pipe", [(source, last)])
            continue
        sent = jnp.where(section == mirror, cotangent, inputs)
        got = lax.ppermute(sent, "pipe", [(source, 0), (mirror, last)])
        input_parts[source] = cotangent_parts[mirror] = got
    return input_parts, cotangent_parts


def after(values, *tokens):
    return lax.optimization_barrier((values, tokens))[0]


def by_rows(value):
    return with_layout_constraint(value, Layout(major_to_minor=(0, 1)))


def odd_device():
    return lax.axis_index("dp") % 2


def pair_view(value):
    devices = lax.axis_size("dp")
    rows, columns = value.shape
    return value.reshape(devices // 2, 2, rows // devices, columns)


def neighbours_half(view):
    return lax.dynamic_index_in_dim(view, 1 - odd_device(), 1, keepdims=False)


def own_half(view):
    return lax.dynamic_index_in_dim(view, odd_device(), 1, keepdims=False)


def to_neighbour(part):
    devices = lax.axis_size("dp")
    return lax.ppermute(part, "dp", [(i, i ^ 1) for i in range(devices)])


def line_scatter(part):
    devices = lax.axis_size("dp")
    lines = [list(range(first, devices, 2)) for first in range(2)]
    line, rows, columns = part.shape
    return lax.psum_scatter(
        part.reshape(line * rows, columns),
        "dp",
        scatter_dimension=0,
        tiled=True,
        axis_index_groups=lines,
    )


def per_device(
    inputs,
    cotangent,
    lengths,
    w_query,
    w_key,
    w_value,
    w_proj,
    w_gate,
    w_up,
    w_down,
    gain_attn,
    gain_mlp,
):
    sections = lax.axis_size("pipe")
    section = lax.axis_index("pipe")
    total_rows, columns = inputs.shape
    width = columns * sections
    rows = 2 * total_rows // (MICRO + 1)
    segment = rows // 2
    kv_width = w_key.shape[-1]
    ff = w_gate.shape[-1]
    kv_heads = kv_width // HEAD_DIM
    share = width // kv_width
    depth_step = 2
    ticks = CHUNKS + depth_step * (sections - 1)
    sizes = dict(
        rows=rows,
        total_rows=total_rows,
        width=width,
        ff_step=ff // 2,
        sections=sections,
        depth_step=depth_step,
    )
    group = lengths[0]
    input_parts, cotangent_parts = gather_ends(inputs, cotangent)
    w_heads_t, w_heads, wp, wg, wu, wd_t, wd, *tables = load_weights(
        w_query[0],
        jnp.swapaxes(w_key[0], 0, 1),
        jnp.swapaxes(w_value[0], 0, 1),
        w_proj[0],
        w_gate[0],
        w_up[0],
        jnp.swapaxes(w_down[0], 0, 1),
        *rope_tables(rows),
        gain_attn,
        gain_mlp,
        inputs,
    )
    input_parts[0] = tables.pop()
    turned = turn_weights((wp, wg, wu), False)
    forward_weights = (w_heads, wp, wg, wu, wd)

    def stored(*shape, dtype=BF16):
        return jax.ShapeDtypeStruct(shape, dtype)

    query_pad = round_up(width, LANES)
    all_width = width + 2 * kv_width
    heads_pad = round_up(all_width, LANES)
    forward_shapes = [
        stored(2, total_rows, width, dtype=F32),
        stored(2, total_rows, width),
        stored(2, total_rows, heads_pad),
        stored(CHUNKS, 2, kv_heads, share * rows, rows),
        stored(2, total_rows, width),
        stored(2, total_rows, width, dtype=F32),
        stored(2, total_rows, width),
        stored(2, 2, total_rows, ff),
        stored(2, total_rows, ff),
    ]
    forward_scratch = [
        pltpu.VMEM((rows, width), F32),
        pltpu.VMEM((rows, heads_pad), F32),
    ]
    sent = {}
    state = None
    for tick in range(ticks):
        rounded, *state = run_tick(
            forward_kernel,
            dict(sizes, tick=tick, backward=False),
            lengths,
            tables,
            input_parts if tick < CHUNKS else (),
            sent.get(tick - depth_step),
            forward_weights,
            (),
            state,
            forward_shapes,
            forward_scratch,
            "layer_pair_forward",
        )
        route = [
            (s, s + 1) for s in range(sections - 1) if 0 <= tick - depth_step * s < CHUNKS
        ]
        if route:
            sent[tick] = lax.ppermute(rounded, "pipe", route)
        if tick == CHUNKS - 1:
            ready, _ = lax.optimization_barrier(((wp, wg, wu), rounded))
            turned = turn_weights(ready, True, turned)
    backward_weights = (w_heads_t, *turned, wd_t)
    results = state[0]
    hidden, normed_attn, heads, probs, mixed, middle, normed_mlp, slopes, inner = state[1:]

    backward_shapes = [
        stored(2, total_rows, width),
        stored(2, total_rows, ff),
        stored(2, total_rows, ff),
        stored(2, total_rows, width),
        stored(2, total_rows, all_width),
        stored(CHUNKS, 2, 2, 8, width, dtype=F32),
    ]
    backward_scratch = [
        pltpu.VMEM((rows, width), F32),
        pltpu.VMEM((rows, query_pad), F32),
        pltpu.VMEM((rows, ff), F32),
    ]
    reads = (hidden, heads, probs, middle, slopes)
    sent = {}
    state = None
    for tick in range(ticks):
        rounded, *state = run_tick(
            backward_kernel,
            dict(sizes, tick=tick, backward=True),
            lengths,
            tables,
            cotangent_parts if tick < CHUNKS else (),
            sent.get(tick - depth_step),
            backward_weights,
            reads,
            state,
            backward_shapes,
            backward_scratch,
            "layer_pair_backward",
        )
        route = [
            (s, s - 1)
            for s in range(1, sections)
            if 0 <= tick - depth_step * (sections - 1 - s) < CHUNKS
        ]
        if route:
            sent[tick] = lax.ppermute(rounded, "pipe", route)
    input_grads = state[0]
    branch, gate_grad, up_grad, attn_grad, heads_grad, gains = state[1:]

    def product(left, right):
        left = left.reshape(2 * total_rows, left.shape[-1])
        right = right.reshape(2 * total_rows, right.shape[-1])
        return by_rows(dot_rows(left, right).astype(BF16))

    heads_grads = product(normed_attn, heads_grad)
    line = lax.axis_size("dp") // 2
    own_heads = line_scatter(heads_grads.reshape(line, width // line, all_width))
    gate_view = pair_view(product(*after((normed_mlp, gate_grad), heads_grads)))
    gate_sent = neighbours_half(gate_view)
    gate_got = to_neighbour(gate_sent)
    up_view = pair_view(product(*after((normed_mlp, up_grad), gate_sent)))
    up_sent = neighbours_half(up_view)
    up_got = to_neighbour(up_sent)
    down_view = pair_view(product(*after((inner, branch), up_sent)))
    down_sent = neighbours_half(down_view)
    down_got = to_neighbour(down_sent)
    proj_view = pair_view(product(*after((mixed, attn_grad), down_sent)))
    proj_sent = neighbours_half(proj_view)
    proj_got = to_neighbour(proj_sent)

    gate_part = own_half(gate_view) + after(gate_got, proj_sent)
    grad_gate = line_scatter(gate_part)
    up_part = own_half(up_view) + after(up_got, gate_part)
    grad_up = line_scatter(after(up_part, own_heads))
    down_part = own_half(down_view) + after(down_got, up_part)
    grad_down = line_scatter(after(down_part, grad_gate))
    proj_part = own_half(proj_view) + after(proj_got, down_part)
    grad_proj = line_scatter(after(proj_part, grad_up)).astype(F32)
    grad_gate, grad_up, grad_down = [
        grad.astype(F32) for grad in (grad_gate, grad_up, grad_down)
    ]

    own_heads = own_heads.reshape(1, 2, width // (2 * line), all_width)
    heads_got = to_neighbour(neighbours_half(own_heads))
    grad_heads = (own_half(own_heads) + heads_got)[0].astype(F32)
    grad_query = grad_heads[:, :width]
    grad_key = grad_heads[:, width : width + kv_width]
    grad_value = grad_heads[:, width + kv_width :]
    gain_sums = jnp.sum(gains, axis=(0, 1, 3))
    grad_gain_attn = lax.psum_scatter(gain_sums[0], "dp", scatter_dimension=0, tiled=True)
    grad_gain_mlp = lax.psum_scatter(gain_sums[1], "dp", scatter_dimension=0, tiled=True)

    def spread(store, source):
        own = store[:, source * columns : (source + 1) * columns]
        arrived = jnp.where(section == source, own, 0.0)
        for target in range(sections):
            if target != source:
                block = store[:, target * columns : (target + 1) * columns]
                arrived = arrived + lax.ppermute(block, "pipe", [(source, target)])
        return arrived

    position = jnp.arange(total_rows)
    long_rows = position < rows
    offsets = jnp.where(long_rows, position, position % segment)
    micro = jnp.where(long_rows, 0, position // segment - 1)
    bound = jnp.zeros_like(position)
    for m in range(MICRO):
        bound = jnp.where(micro == m, group[m], bound)
    valid = (offsets < bound)[:, None]
    results, input_grads = after((results, input_grads), up_part)
    layer_output = jnp.where(valid, spread(results, sections - 1), 0.0)
    grad_input = spread(input_grads, 0)
    return (
        layer_output,
        grad_input,
        grad_query[None],
        grad_key[None],
        grad_value[None],
        grad_proj[None],
        grad_gate[None],
        grad_up[None],
        grad_down[None],
        grad_gain_attn[None],
        grad_gain_mlp[None],
    )


def solution(mesh):
    placed = (
        P("dp", "pipe"),
        P("dp", "pipe"),
        P("dp", None),
        P("pipe", None, None),
        P("pipe", None, None),
        P("pipe", None, None),
        P("pipe", None, None),
        P("pipe", None, None),
        P("pipe", None, None),
        P("pipe", None, None),
        P("pipe", None),
        P("pipe", None),
    )
    return jax.shard_map(
        per_device,
        mesh=mesh,
        in_specs=placed,
        out_specs=(
            P("dp", "pipe"),
            P("dp", "pipe"),
            P("pipe", "dp", None),
            P("pipe", "dp", None),
            P("pipe", "dp", None),
            P("pipe", "dp", None),
            P("pipe", "dp", None),
            P("pipe", "dp", None),
            P("pipe", "dp", None),
            P("pipe", "dp"),
            P("pipe", "dp"),
        ),
        check_vma=False,
    )
```

```python
import functools

import jax
import jax.numpy as jnp
import numpy as np
from jax import lax
from jax.experimental import pallas as pl
from jax.experimental.layout import Layout, with_layout_constraint
from jax.experimental.pallas import tpu as pltpu
from jax.sharding import PartitionSpec as P

HEAD_DIM = 64
HALF = HEAD_DIM // 2
LANES = 128
MICRO = 4
CHUNKS = 3
SCALE = HEAD_DIM**-0.5
BF16 = jnp.bfloat16
F32 = jnp.float32

epsilon = 1e-05
rope_base = 10000.0
masked_score = -1e30

def round_up(value, multiple):
    return -(-value // multiple) * multiple


def dot(left, right):
    return jnp.dot(left, right, preferred_element_type=F32)


def dot_t(left, right):
    return lax.dot_general(left, right, (((1,), (1,)), ((), ())), preferred_element_type=F32)


def dot_rows(left, right):
    return lax.dot_general(left, right, (((0,), (0,)), ((), ())), preferred_element_type=F32)


def lane_ids(rows):
    return lax.broadcasted_iota(jnp.int32, (rows, LANES), 1)


def in_low_half(rows):
    return lane_ids(rows) < HEAD_DIM


def rotate(slab, cosine, signed_sine):
    first = (lane_ids(slab.shape[0]) % HEAD_DIM) < HALF
    partner = jnp.where(
        first, pltpu.roll(slab, LANES - HALF, 1), pltpu.roll(slab, HALF, 1)
    )
    return slab * cosine + partner * signed_sine


def both_halves(slab, upper):
    swapped = pltpu.roll(slab, HEAD_DIM, 1)
    low = in_low_half(slab.shape[0])
    return jnp.where(low, swapped, slab) if upper else jnp.where(low, slab, swapped)


def sort_halves(slab, j, low, heads, kv_heads, key_rows, queries, keys, values):
    for head in (2 * j, 2 * j + 1):
        upper = head % 2 == 1
        if head < heads:
            kept = jnp.where(low, 0.0, slab) if upper else jnp.where(low, slab, 0.0)
            queries.append(kept.astype(BF16))
        elif head < heads + kv_heads:
            keys.append(pad_rows(both_halves(slab, upper).astype(BF16), key_rows))
        elif head < heads + 2 * kv_heads:
            values.append(pad_rows(both_halves(slab, upper).astype(BF16), key_rows))


def reciprocal_rms(value):
    return lax.rsqrt(jnp.mean(value * value, axis=-1, keepdims=True) + epsilon)


class Tick:
    def __init__(self, sizes, lengths):
        sections, depth_step, segment = sizes["sections"], sizes["depth_step"], sizes["rows"] // 2
        section = lax.axis_index("pipe")
        depth = sections - 1 - section if sizes["backward"] else section
        chunk = sizes["tick"] - depth_step * depth
        self.active = (chunk >= 0) & (chunk < CHUNKS)
        self.slot = jnp.clip(chunk, 0, CHUNKS - 1)
        self.edge = depth == 0
        self.final = depth == sections - 1
        self.is_long = self.slot == 0
        self.table = jnp.where(self.is_long, 1, 0)
        self.first_length = jnp.where(
            self.is_long, lengths[0, 0], jnp.where(self.slot == 1, lengths[0, 1], lengths[0, 3])
        )
        self.second_length = jnp.where(self.slot == 1, lengths[0, 2], segment)

    def bound(self, position, segment):
        return jnp.where(
            self.is_long,
            self.first_length,
            jnp.where(position < segment, self.first_length, self.second_length + segment),
        )


def score_bias(tick, query_rows, key_rows):
    query = lax.broadcasted_iota(jnp.int32, (query_rows, key_rows), 0)
    key = lax.broadcasted_iota(jnp.int32, (query_rows, key_rows), 1)
    segment = key_rows // 2
    start = jnp.where(tick.is_long, 0, jnp.where(query < segment, 0, segment))
    allowed = (key <= query) & (key < tick.bound(key, segment)) & (key >= start)
    return jnp.where(allowed, 0.0, masked_score).astype(F32)


def assemble(target, parts, at):
    count = min(target.shape[0], parts[0].shape[0] - at)
    target[:count, :] = jnp.concatenate(
        [part[at : at + count, :].astype(F32) for part in parts], axis=1
    )


def kept_at(kind, buffer, array, app, slot, rows, chunk, columns=None):
    columns = pl.ds(0, buffer.shape[-1]) if columns is None else columns
    if kind == "gains":
        return buffer.at[app], array.at[slot, app]
    if kind == "probs":
        taken = pl.ds(0, buffer.shape[2] * rows // chunk)
        return buffer.at[app, :, taken], array.at[slot, app, :, taken]
    at = pl.ds(pl.multiple_of(slot * chunk, chunk), rows)
    if kind == "slopes":
        return buffer.at[app, :, pl.ds(0, rows), columns], array.at[app, :, at, columns]
    return buffer.at[app, pl.ds(0, rows), columns], array.at[app, at, columns]


def chunk_sizes(sizes):
    full, total = sizes["rows"], sizes["total_rows"]
    found = {}
    for depth in range(sizes["sections"]):
        slot = sizes["tick"] - sizes["depth_step"] * depth
        if 0 <= slot < CHUNKS:
            found.setdefault(min(full, total - slot * full), []).append(slot)
    return found


def pad_rows(value, rows):
    missing = rows - value.shape[0]
    if not missing:
        return value
    return jnp.concatenate([value, jnp.zeros((missing, value.shape[1]), value.dtype)], axis=0)


def when(condition, action):
    pl.when(condition)(action)


def run_active(tick, sizes, run):
    found = chunk_sizes(sizes)
    for rows, slots in found.items():
        mine = functools.reduce(jnp.logical_or, [tick.slot == slot for slot in slots])
        when(tick.active & mine, functools.partial(run, rows))


def final_at(rows_s, array, slot, rows):
    chunk = rows_s.shape[0]
    at = pl.ds(pl.multiple_of(slot * chunk, chunk), rows)
    return rows_s.at[pl.ds(0, rows)], array.at[at]


def forward_kernel(sizes, lengths, *refs):
    tick = Tick(sizes, lengths)
    refs = list(refs)

    def take(count):
        taken = refs[:count]
        del refs[:count]
        return taken

    cosine_ref, sine_ref, gain_attn, gain_mlp = take(4)
    edge_parts, inbound = take(sizes["edge_parts"]), take(sizes["inbound"])
    w_heads, wp, wg, wu, wd = take(5)
    take(sizes["aliased"])
    out_round, out_full = take(2)
    stores = take(sizes["stores"])
    hidden_s, heads_s = take(2)
    buffers = take(sizes["stores"])
    (
        hidden_b,
        normed_attn_b,
        heads_b,
        probs_b,
        mixed_b,
        middle_b,
        normed_mlp_b,
        slopes_b,
        inner_b,
    ) = buffers
    store_sems, final_sem = refs
    chunk, width = hidden_s.shape
    heads = width // HEAD_DIM
    all_width = w_heads.shape[1]
    kv_heads = (all_width // HEAD_DIM - heads) // 2
    share = heads // kv_heads
    ff = wg.shape[1]
    slot = tick.slot

    step = sizes["ff_step"]

    def store(buffer, app, rows, part=None):
        i = [other is buffer for other in buffers].index(True)
        columns = None if part is None else pl.ds(part * step, step)
        source, target = kept_at(
            sizes["store_kinds"][i], buffer, stores[i], app, slot, rows, chunk, columns
        )
        return pltpu.make_async_copy(source, target, store_sems.at[i, app, part or 0])

    def apply(rows, app, carry):
        hidden = hidden_s[:rows]
        hidden_b[app, :rows] = hidden
        store(hidden_b, app, rows).start()
        normed = (hidden * reciprocal_rms(hidden) * gain_attn[...]).astype(BF16)
        normed_attn_b[app, :rows] = normed
        store(normed_attn_b, app, rows).start()
        heads_s[:rows, :all_width] = dot(normed, w_heads[...])
        cosine = cosine_ref[tick.table, :rows]
        sine = sine_ref[tick.table, :rows]
        low = in_low_half(rows)
        query_parts, keys, values = [], [], []
        for j in range(heads_s.shape[1] // LANES):
            slab = heads_s[:rows, j * LANES : (j + 1) * LANES]
            if 2 * j < heads + kv_heads:
                slab = rotate(slab, cosine, sine)
            heads_b[app, :rows, j * LANES : (j + 1) * LANES] = slab.astype(BF16)
            sort_halves(slab, j, low, heads, kv_heads, chunk, query_parts, keys, values)
        store(heads_b, app, rows).start()
        bias = score_bias(tick, rows, chunk)
        bias = jnp.concatenate([bias] * share, axis=0)
        mixed_parts = []
        for kv in range(kv_heads):
            grouped = jnp.concatenate(query_parts[kv * share : (kv + 1) * share], axis=0)
            scores = dot_t(grouped, keys[kv]) * SCALE + bias
            exponent = jnp.exp(scores - jnp.max(scores, axis=-1, keepdims=True))
            total = jnp.sum(exponent, axis=-1, keepdims=True)
            probs = (exponent * (1.0 / total)).astype(BF16)
            probs_b[app, kv, : share * rows] = probs
            mixed = dot(probs, values[kv])
            mixed_parts += [mixed[i * rows : (i + 1) * rows] for i in range(share)]
        store(probs_b, app, rows).start()
        for j in range(heads // 2):
            mixed_b[app, :rows, j * LANES : (j + 1) * LANES] = jnp.where(
                low, mixed_parts[2 * j], mixed_parts[2 * j + 1]
            ).astype(BF16)
        if heads % 2:
            mixed_b[app, :rows, width - HEAD_DIM :] = mixed_parts[-1][:, :HEAD_DIM].astype(BF16)
        store(mixed_b, app, rows).start()
        middle = hidden + dot(mixed_b[app, :rows], wp[...])
        middle_b[app, :rows] = middle
        store(middle_b, app, rows).start()
        normed = (middle * reciprocal_rms(middle) * gain_mlp[...]).astype(BF16)
        normed_mlp_b[app, :rows] = normed
        store(normed_mlp_b, app, rows).start()
        for part, at in enumerate(range(0, ff, step)):
            gate = dot(normed, wg[:, at : at + step])
            up = dot(normed, wu[:, at : at + step])
            sigma = 1.0 / (1.0 + jnp.exp(-gate))
            silu = gate * sigma
            inner_b[app, :rows, at : at + step] = (silu * up).astype(BF16)
            slopes_b[app, 0, :rows, at : at + step] = (
                up * (sigma * (1.0 + gate * (1.0 - sigma)))
            ).astype(BF16)
            slopes_b[app, 1, :rows, at : at + step] = silu.astype(BF16)
            store(inner_b, app, rows, part).start()
            store(slopes_b, app, rows, part).start()
        hidden_s[:rows] = middle + dot(inner_b[app, :rows], wd[...])
        return carry

    def run(rows):
        if edge_parts:

            @pl.when(tick.edge)
            def _():
                assemble(hidden_s, edge_parts, sizes["tick"] * chunk)

        if inbound:

            @pl.when(jnp.logical_not(tick.edge))
            def _():
                hidden_s[:rows] = inbound[0][:rows].astype(F32)

        heads_s[:, heads_s.shape[1] - LANES :] = jnp.zeros((chunk, LANES), F32)
        lax.fori_loop(0, 2, functools.partial(apply, rows), 0)
        out_round[:rows] = hidden_s[:rows].astype(BF16)
        source, target = final_at(hidden_s, out_full, slot, rows)
        final = pltpu.make_async_copy(source, target, final_sem.at[0])
        when(tick.final, final.start)
        for app in (0, 1):
            for buffer in buffers[:-2]:
                store(buffer, app, rows).wait()
            for part in range(ff // step):
                store(inner_b, app, rows, part).wait()
                store(slopes_b, app, rows, part).wait()
        when(tick.final, final.wait)

    run_active(tick, sizes, run)


def backward_kernel(sizes, lengths, *refs):
    tick = Tick(sizes, lengths)
    refs = list(refs)

    def take(count):
        taken = refs[:count]
        del refs[:count]
        return taken

    cosine_ref, sine_ref, gain_attn, gain_mlp = take(4)
    edge_parts, inbound = take(sizes["edge_parts"]), take(sizes["inbound"])
    w_heads, wp, wg, wu, wd = take(5)
    saved = take(sizes["reads"])
    take(sizes["aliased"])
    out_round, out_full = take(2)
    stores = take(sizes["stores"])
    grad_s, mixed_s, inner_s = take(3)
    kept = take(sizes["reads"])
    hidden_k, heads_k, probs_k, middle_k, slopes_k = kept
    buffers = take(sizes["stores"])
    branch_b, gate_b, up_b, attn_b, heads_b, gains_b = buffers
    read_sems, store_sems, final_sem = refs
    chunk, width = grad_s.shape
    heads = width // HEAD_DIM
    all_width = w_heads.shape[0]
    kv_heads = (all_width // HEAD_DIM - heads) // 2
    share = heads // kv_heads
    ff = wd.shape[1]
    slot = tick.slot

    def read(buffer, app, rows):
        i = [other is buffer for other in kept].index(True)
        kind = sizes["read_kinds"][i]
        target, source = kept_at(kind, buffer, saved[i], app, slot, rows, chunk)
        return pltpu.make_async_copy(source, target, read_sems.at[i, app])

    def store(buffer, app, rows):
        i = [other is buffer for other in buffers].index(True)
        kind = sizes["store_kinds"][i]
        source, target = kept_at(kind, buffer, stores[i], app, slot, rows, chunk)
        return pltpu.make_async_copy(source, target, store_sems.at[i, app, 0])

    def rms_backward(value, gain, grad, running):
        scale = reciprocal_rms(value)
        unit = value * scale
        pulled = grad * gain
        gain_terms = grad * unit
        gain_rows = jnp.sum(gain_terms.reshape(grad.shape[0] // 8, 8, width), axis=0)
        shared = jnp.mean(gain_terms * gain, axis=-1, keepdims=True)
        return running + scale * (pulled - unit * shared), gain_rows

    def apply(rows, step_id, carry):
        app = 1 - step_id
        low = in_low_half(rows)
        grad_top = grad_s[:rows]
        branch = grad_top.astype(BF16)
        branch_b[app, :rows] = branch
        store(branch_b, app, rows).start()
        step = sizes["ff_step"]
        inner_s[:rows] = dot(branch, wd[...])
        read(slopes_k, app, rows).wait()
        for at in range(0, ff, step):
            inner_grad = inner_s[:rows, at : at + step]
            gate_b[app, :rows, at : at + step] = (
                inner_grad * slopes_k[app, 0, :rows, at : at + step].astype(F32)
            ).astype(BF16)
            up_b[app, :rows, at : at + step] = (
                inner_grad * slopes_k[app, 1, :rows, at : at + step].astype(F32)
            ).astype(BF16)
        store(gate_b, app, rows).start()
        store(up_b, app, rows).start()
        pulled = dot(gate_b[app, :rows], wg[...])
        pulled += dot(up_b[app, :rows], wu[...])
        read(middle_k, app, rows).wait()
        middle_grad, gain_rows = rms_backward(
            middle_k[app, :rows], gain_mlp[...], pulled, grad_top
        )
        gains_b[app, 1] = gain_rows
        attn_grad = middle_grad.astype(BF16)
        attn_b[app, :rows] = attn_grad
        store(attn_b, app, rows).start()
        mixed_s[:rows, :width] = dot(attn_grad, wp[...])
        mixed_parts, query_parts, keys, values = [], [], [], []
        for j in range(mixed_s.shape[1] // LANES):
            slab = mixed_s[:rows, j * LANES : (j + 1) * LANES]
            mixed_parts.append(jnp.where(low, slab, 0.0).astype(BF16))
            mixed_parts.append(jnp.where(low, 0.0, slab).astype(BF16))
        read(heads_k, app, rows).wait()
        for j in range(heads_k.shape[-1] // LANES):
            slab = heads_k[app, :rows, j * LANES : (j + 1) * LANES].astype(F32)
            sort_halves(slab, j, low, heads, kv_heads, chunk, query_parts, keys, values)
        cosine = cosine_ref[tick.table, :rows]
        sine = -sine_ref[tick.table, :rows]
        ones = jnp.ones((chunk, LANES), BF16)
        query_grads, key_grads, value_grads = [], [], []
        read(probs_k, app, rows).wait()
        for kv in range(kv_heads):
            mixed = jnp.concatenate(mixed_parts[kv * share : (kv + 1) * share], axis=0)
            grouped = jnp.concatenate(query_parts[kv * share : (kv + 1) * share], axis=0)
            probs = probs_k[app, kv, : share * rows]
            probs_wide = probs.astype(F32)
            probs_grad = dot_t(mixed, values[kv])
            weighted = probs_wide * probs_grad
            shared = dot(weighted.astype(BF16), ones)
            score_grad = (weighted - probs_wide * shared).astype(BF16)
            pulled = dot(score_grad, keys[kv])
            query_grads += [pulled[i * rows : (i + 1) * rows] for i in range(share)]
            pulled = dot_rows(score_grad, grouped)[:rows]
            key_grads.append(pulled + pltpu.roll(pulled, HEAD_DIM, 1))
            pulled = dot_rows(probs, mixed)[:rows]
            value_grads.append(pulled + pltpu.roll(pulled, HEAD_DIM, 1))

        parts = query_grads + key_grads + value_grads
        for j in range(len(parts) // 2):
            slab = jnp.where(low, parts[2 * j], parts[2 * j + 1])
            if 2 * j < heads + kv_heads:
                slab = rotate(slab * SCALE, cosine, sine)
            heads_b[app, :rows, j * LANES : (j + 1) * LANES] = slab.astype(BF16)
        if len(parts) % 2:
            heads_b[app, :rows, all_width - HEAD_DIM :] = parts[-1][:, :HEAD_DIM].astype(BF16)
        store(heads_b, app, rows).start()
        pulled = dot(heads_b[app, :rows], w_heads[...])
        read(hidden_k, app, rows).wait()
        result, gain_rows = rms_backward(
            hidden_k[app, :rows], gain_attn[...], pulled, middle_grad
        )
        gains_b[app, 0] = gain_rows
        store(gains_b, app, rows).start()
        grad_s[:rows] = result
        return carry

    def run(rows):
        for app in (1, 0):
            for buffer in (slopes_k, middle_k, heads_k, probs_k, hidden_k):
                read(buffer, app, rows).start()
        if edge_parts:

            @pl.when(tick.edge)
            def _():
                assemble(grad_s, edge_parts, sizes["tick"] * chunk)
                row = lax.broadcasted_iota(jnp.int32, (chunk, 1), 0)
                grad_s[...] = jnp.where(row < tick.bound(row, chunk // 2), grad_s[...], 0.0)

        if inbound:

            @pl.when(jnp.logical_not(tick.edge))
            def _():
                grad_s[:rows] = inbound[0][:rows].astype(F32)

        mixed_s[:, mixed_s.shape[1] - LANES :] = jnp.zeros((chunk, LANES), F32)
        lax.fori_loop(0, 2, functools.partial(apply, rows), 0)
        out_round[:rows] = grad_s[:rows].astype(BF16)
        source, target = final_at(grad_s, out_full, slot, rows)
        final = pltpu.make_async_copy(source, target, final_sem.at[0])
        when(tick.final, final.start)
        for buffer in buffers:
            store(buffer, 0, rows).wait()
            store(buffer, 1, rows).wait()
        when(tick.final, final.wait)

    run_active(tick, sizes, run)


def transpose_to(target, source):
    for at in range(0, source.shape[1], 256):
        end = min(at + 256, source.shape[1])
        target[at:end, :] = jnp.transpose(source[:, at:end])


def load_kernel(extras, *refs):
    key_t, value_t, query, proj, gate, up, down_t = refs[:7]
    extra_in, refs = refs[7 : 7 + extras], refs[7 + extras :]
    heads_t, heads, proj_v, gate_v, up_v, down_tv, down = refs[:7]
    extra_out, (query_v, sems) = refs[7 : 7 + extras], refs[7 + extras :]
    width, kv_width = query.shape[1], key_t.shape[0]
    pairs = (
        (down_t, down_tv),
        (query, query_v),
        (key_t, heads_t.at[pl.ds(width, kv_width)]),
        (value_t, heads_t.at[pl.ds(width + kv_width, kv_width)]),
        (proj, proj_v),
        (gate, gate_v),
        (up, up_v),
        *zip(extra_in, extra_out),
    )
    copies = [
        pltpu.make_async_copy(source, target, sems.at[i])
        for i, (source, target) in enumerate(pairs)
    ]
    for copy in copies:
        copy.start()
    copies[0].wait()
    transpose_to(down, down_tv)
    copies[1].wait()
    transpose_to(heads_t, query_v)
    copies[2].wait()
    copies[3].wait()
    transpose_to(heads, heads_t)
    for copy in copies[4:]:
        copy.wait()


def turn_kernel(first, count, *refs):
    sources, targets = refs[:count], refs[-count:]

    @pl.when((lax.axis_index("pipe") == 0) == first)
    def _():
        for source, target in zip(sources, targets):
            transpose_to(target, source)


def load_weights(query, key_t, value_t, proj, gate, up, down_t, *extra):
    sources = (key_t, value_t, query, proj, gate, up, down_t, *extra)
    all_width = query.shape[1] + 2 * key_t.shape[0]
    shapes = (
        (all_width, query.shape[0]),
        (query.shape[0], all_width),
        proj.shape,
        gate.shape,
        up.shape,
        down_t.shape,
        down_t.shape[::-1],
    )
    outs = [pltpu.VMEM(tuple(shape), BF16) for shape in shapes]
    outs += [pltpu.VMEM(array.shape, array.dtype) for array in extra]
    return pl.pallas_call(
        functools.partial(load_kernel, len(extra)),
        out_shape=outs,
        in_specs=[in_hbm() for _ in sources],
        out_specs=[in_vmem() for _ in outs],
        scratch_shapes=[
            pltpu.VMEM(query.shape, BF16),
            pltpu.SemaphoreType.DMA((len(sources),)),
        ],
        compiler_params=pltpu.CompilerParams(vmem_limit_bytes=12 * 2**20),
        name="load_weights",
    )(*[pltpu.with_memory_space_constraint(array, pltpu.HBM) for array in sources])


def turn_weights(weights, first, turned=()):
    count = len(weights)
    return pl.pallas_call(
        functools.partial(turn_kernel, first, count),
        out_shape=[pltpu.VMEM(tuple(weight.shape[::-1]), BF16) for weight in weights],
        in_specs=[in_vmem() for _ in (*weights, *turned)],
        out_specs=[in_vmem() for _ in weights],
        input_output_aliases={count + i: i for i in range(len(turned))},
        compiler_params=pltpu.CompilerParams(vmem_limit_bytes=12 * 2**20),
        name="turn_weights",
    )(*[pltpu.with_memory_space_constraint(weight, pltpu.VMEM) for weight in (*weights, *turned)])


def in_vmem():
    return pl.BlockSpec(memory_space=pltpu.VMEM)


def in_hbm():
    return pl.BlockSpec(memory_space=pltpu.HBM)


def kind_of(array):
    return {5: "probs" if array.dtype == BF16 else "gains", 4: "slopes", 3: "rows"}[len(array.shape)]


def buffers_for(arrays, rows):
    shapes = []
    for array in arrays:
        kind, shape = kind_of(array), tuple(array.shape)
        if kind in ("probs", "gains"):
            shapes.append(shape[1:])
        else:
            shapes.append(shape[:-2] + (rows, shape[-1]))
    return [pltpu.VMEM(shape, array.dtype) for shape, array in zip(shapes, arrays)]


def run_tick(
    kernel, sizes, lengths, tables, edge_parts, inbound, weights, reads, state, shapes, scratch, name
):
    rows, width = sizes["rows"], sizes["width"]
    aliased = [] if state is None else list(state)
    inbound = [] if inbound is None else [inbound]
    outs = [jax.ShapeDtypeStruct((rows, width), BF16)] + [
        pltpu.HBM(shape.shape, shape.dtype)
        for shape in (jax.ShapeDtypeStruct((sizes["total_rows"], width), F32), *shapes)
    ]
    scratch = scratch + buffers_for(reads, rows) + buffers_for(shapes, rows)
    if reads:
        scratch.append(pltpu.SemaphoreType.DMA((len(reads), 2)))
    scratch.append(pltpu.SemaphoreType.DMA((len(shapes), 2, 2)))
    scratch.append(pltpu.SemaphoreType.DMA((1,)))
    blocks = [*tables, *edge_parts, *inbound]
    kept = len(tables) + (0 if sizes["backward"] else len(edge_parts))
    blocks[:kept] = [pltpu.with_memory_space_constraint(array, pltpu.VMEM) for array in blocks[:kept]]
    first_alias = 1 + len(blocks) + len(weights) + len(reads)
    sizes = dict(
        sizes,
        edge_parts=len(edge_parts),
        inbound=len(inbound),
        aliased=len(aliased),
        stores=len(shapes),
        reads=len(reads),
        store_kinds=[kind_of(shape) for shape in shapes],
        read_kinds=[kind_of(read) for read in reads],
    )
    flops = 4 * rows * sum(int(np.prod(weight.shape)) for weight in weights)
    return pl.pallas_call(
        functools.partial(kernel, sizes),
        out_shape=outs,
        grid_spec=pltpu.PrefetchScalarGridSpec(
            num_scalar_prefetch=1,
            grid=(1,),
            in_specs=[in_vmem() for _ in (*blocks, *weights)]
            + [in_hbm() for _ in (*reads, *aliased)],
            out_specs=[in_vmem()] + [in_hbm() for _ in outs[1:]],
            scratch_shapes=scratch,
        ),
        input_output_aliases={first_alias + i: 1 + i for i in range(len(aliased))},
        compiler_params=pltpu.CompilerParams(
            dimension_semantics=("arbitrary",), vmem_limit_bytes=18 * 2**20
        ),
        cost_estimate=pl.CostEstimate(
            flops=flops, bytes_accessed=flops // (2 * rows), transcendentals=0
        ),
        name=name,
    )(
        lengths,
        *blocks,
        *[pltpu.with_memory_space_constraint(weight, pltpu.VMEM) for weight in weights],
        *[pltpu.with_memory_space_constraint(array, pltpu.HBM) for array in (*reads, *aliased)],
    )


def rope_tables(rows):
    segment = rows // 2
    frequency = rope_base ** (-np.arange(HALF, dtype=np.float64) / HALF)
    positions = np.stack([np.arange(rows) % segment, np.arange(rows)]).astype(np.float64)
    angles = np.tile(positions[:, :, None] * frequency, (1, 1, LANES // HALF))
    sign = np.where(np.arange(LANES) % HEAD_DIM < HALF, -1.0, 1.0)
    return (
        jnp.asarray(np.cos(angles), F32),
        jnp.asarray(np.sin(angles) * sign, F32),
    )


def gather_ends(inputs, cotangent):
    sections, section = lax.axis_size("pipe"), lax.axis_index("pipe")
    last = sections - 1
    input_parts, cotangent_parts = [inputs] * sections, [cotangent] * sections
    for source in range(1, sections):
        mirror = last - source
        if mirror == source:
            input_parts[source] = lax.ppermute(inputs, "pipe", [(source, 0)])
            cotangent_parts[source] = lax.ppermute(cotangent, "pipe", [(source, last)])
            continue
        sent = jnp.where(section == mirror, cotangent, inputs)
        got = lax.ppermute(sent, "pipe", [(source, 0), (mirror, last)])
        input_parts[source] = cotangent_parts[mirror] = got
    return input_parts, cotangent_parts


def spread_ends(results, input_grads):
    sections, section = lax.axis_size("pipe"), lax.axis_index("pipe")
    last = sections - 1
    columns = results.shape[1] // sections

    def block(value, at):
        return value[:, at * columns : (at + 1) * columns]

    outputs = jnp.where(section == last, block(results, last), 0.0)
    grads = jnp.where(section == 0, block(input_grads, 0), 0.0)
    for target in range(last):
        mirror = last - target
        if mirror == target:
            outputs += lax.ppermute(block(results, target), "pipe", [(last, target)])
            grads += lax.ppermute(block(input_grads, target), "pipe", [(0, target)])
            continue
        sent = jnp.where(section == 0, block(input_grads, mirror), block(results, target))
        got = lax.ppermute(sent, "pipe", [(last, target), (0, mirror)])
        outputs = jnp.where(section == target, got, outputs)
        grads = jnp.where(section == mirror, got, grads)
    return outputs, grads


def after(values, *tokens):
    return lax.optimization_barrier((values, tokens))[0]


def by_rows(value):
    return with_layout_constraint(value, Layout(major_to_minor=(0, 1)))


def cube_view(value):
    bits = lax.axis_size("dp").bit_length() - 1
    rows, columns = value.shape
    return value.reshape((2,) * bits + (rows >> bits, columns))


class Piece:
    def __init__(self, value, bits):
        self.value, self.bits, self.got = value, list(bits), None

    def send(self, *tokens):
        devices = lax.axis_size("dp")
        bit = self.bits.pop(0)
        axis = devices.bit_length() - 2 - bit
        mine = (lax.axis_index("dp") >> bit) & 1
        sent = lax.dynamic_index_in_dim(self.value, 1 - mine, axis)
        if tokens:
            sent = after(sent, *tokens)
        self.kept = (axis, mine)
        self.got = lax.ppermute(sent, "dp", [(i, i ^ (1 << bit)) for i in range(devices)])
        return sent

    def take(self, *tokens):
        axis, mine = self.kept
        got = after(self.got, *tokens) if tokens else self.got
        self.value = lax.dynamic_index_in_dim(self.value, mine, axis) + got
        return self.value

    def finish(self, *tokens):
        self.take(*tokens)
        while self.bits:
            self.send()
            self.take()
        return self.value.reshape(self.value.shape[-2:])


def per_device(
    inputs,
    cotangent,
    lengths,
    w_query,
    w_key,
    w_value,
    w_proj,
    w_gate,
    w_up,
    w_down,
    gain_attn,
    gain_mlp,
):
    sections = lax.axis_size("pipe")
    section = lax.axis_index("pipe")
    total_rows, columns = inputs.shape
    width = columns * sections
    rows = 2 * total_rows // (MICRO + 1)
    segment = rows // 2
    kv_width = w_key.shape[-1]
    ff = w_gate.shape[-1]
    kv_heads = kv_width // HEAD_DIM
    share = width // kv_width
    depth_step = 2
    ticks = CHUNKS + depth_step * (sections - 1)
    sizes = dict(
        rows=rows,
        total_rows=total_rows,
        width=width,
        ff_step=ff // 2,
        sections=sections,
        depth_step=depth_step,
    )
    group = lengths[0]
    input_parts, cotangent_parts = gather_ends(inputs, cotangent)
    w_heads_t, w_heads, wp, wg, wu, wd_t, wd, *tables = load_weights(
        w_query[0],
        jnp.swapaxes(w_key[0], 0, 1),
        jnp.swapaxes(w_value[0], 0, 1),
        w_proj[0],
        w_gate[0],
        w_up[0],
        jnp.swapaxes(w_down[0], 0, 1),
        *rope_tables(rows),
        gain_attn,
        gain_mlp,
        inputs,
    )
    input_parts[0] = tables.pop()
    turned = turn_weights((wp, wg, wu), False)
    forward_weights = (w_heads, wp, wg, wu, wd)

    def stored(*shape, dtype=BF16):
        return jax.ShapeDtypeStruct(shape, dtype)

    query_pad = round_up(width, LANES)
    all_width = width + 2 * kv_width
    heads_pad = round_up(all_width, LANES)
    forward_shapes = [
        stored(2, total_rows, width, dtype=F32),
        stored(2, total_rows, width),
        stored(2, total_rows, heads_pad),
        stored(CHUNKS, 2, kv_heads, share * rows, rows),
        stored(2, total_rows, width),
        stored(2, total_rows, width, dtype=F32),
        stored(2, total_rows, width),
        stored(2, 2, total_rows, ff),
        stored(2, total_rows, ff),
    ]
    forward_scratch = [
        pltpu.VMEM((rows, width), F32),
        pltpu.VMEM((rows, heads_pad), F32),
    ]
    sent = {}
    state = None
    for tick in range(ticks):
        rounded, *state = run_tick(
            forward_kernel,
            dict(sizes, tick=tick, backward=False),
            lengths,
            tables,
            input_parts if tick < CHUNKS else (),
            sent.get(tick - depth_step),
            forward_weights,
            (),
            state,
            forward_shapes,
            forward_scratch,
            "layer_pair_forward",
        )
        route = [
            (s, s + 1) for s in range(sections - 1) if 0 <= tick - depth_step * s < CHUNKS
        ]
        if route:
            sent[tick] = lax.ppermute(rounded, "pipe", route)
        if tick == CHUNKS - 1:
            ready, _ = lax.optimization_barrier(((wp, wg, wu), rounded))
            turned = turn_weights(ready, True, turned)
    backward_weights = (w_heads_t, *turned, wd_t)
    results = state[0]
    hidden, normed_attn, heads, probs, mixed, middle, normed_mlp, slopes, inner = state[1:]

    backward_shapes = [
        stored(2, total_rows, width),
        stored(2, total_rows, ff),
        stored(2, total_rows, ff),
        stored(2, total_rows, width),
        stored(2, total_rows, all_width),
        stored(CHUNKS, 2, 2, 8, width, dtype=F32),
    ]
    backward_scratch = [
        pltpu.VMEM((rows, width), F32),
        pltpu.VMEM((rows, query_pad), F32),
        pltpu.VMEM((rows, ff), F32),
    ]
    reads = (hidden, heads, probs, middle, slopes)
    sent = {}
    state = None
    for tick in range(ticks):
        rounded, *state = run_tick(
            backward_kernel,
            dict(sizes, tick=tick, backward=True),
            lengths,
            tables,
            cotangent_parts if tick < CHUNKS else (),
            sent.get(tick - depth_step),
            backward_weights,
            reads,
            state,
            backward_shapes,
            backward_scratch,
            "layer_pair_backward",
        )
        route = [
            (s, s - 1)
            for s in range(1, sections)
            if 0 <= tick - depth_step * (sections - 1 - s) < CHUNKS
        ]
        if route:
            sent[tick] = lax.ppermute(rounded, "pipe", route)
    input_grads = state[0]
    branch, gate_grad, up_grad, attn_grad, heads_grad, gains = state[1:]

    def product(left, right):
        left = left.reshape(2 * total_rows, left.shape[-1])
        right = right.reshape(2 * total_rows, right.shape[-1])
        return by_rows(dot_rows(left, right).astype(BF16))

    bits = lax.axis_size("dp").bit_length() - 1
    across_first, along_first = range(bits), range(1, bits)
    attn = Piece(cube_view(product(normed_attn, heads_grad)), along_first)
    token = attn.send()
    gate = Piece(cube_view(product(*after((normed_mlp, gate_grad), token))), across_first)
    token = gate.send()
    gain_sums = jnp.swapaxes(jnp.sum(gains, axis=(0, 1, 3)), 0, 1).astype(BF16)
    proj_product = product(*after((mixed, attn_grad), token))
    proj = Piece(cube_view(jnp.concatenate([proj_product, gain_sums], axis=1)), along_first)
    token = proj.send()
    attn.take(token)
    token = attn.send()
    up = Piece(cube_view(product(*after((normed_mlp, up_grad), token))), across_first)
    token = up.send()
    gate.take(token)
    token = gate.send()
    down_view = cube_view(product(*after((inner, branch), token)))
    part = down_view.shape[-2] * 3 // 5
    down = [Piece(view, across_first) for view in (down_view[..., :part, :], down_view[..., part:, :])]
    proj.take(down_view)
    token = proj.send()
    while attn.bits:
        attn.take(token)
        token = attn.send()
    token = attn.take(token)
    gate.take(token)
    token = gate.send()
    while proj.bits:
        proj.take(token)
        token = proj.send()
    token = proj.take(token)
    up.take(token)
    token = up.send()
    token = down[0].send(token)
    token = down[1].send(token)
    token = grad_gate = gate.finish(token)
    attn.bits, proj.bits = [0], [0]
    token = attn.send(token)
    up.take(token)
    token = up.send()
    token = proj.send(token)
    down[0].take(token)
    token = down[0].send()
    down[0].take(token)
    token = down[0].send()
    down[1].take(token)
    token = down[1].send()
    token = grad_up = up.finish(token)
    token = grad_heads = attn.finish(token)
    token = grad_proj = proj.finish(token)
    token = down_end = down[0].finish(token)
    down[1].take(token)
    token = down[1].send()
    layer_output, grad_input = spread_ends(*after((results, input_grads), token))
    grad_down = jnp.concatenate([down_end, down[1].finish(layer_output, grad_input)], axis=0)
    grad_down = grad_down.astype(F32)
    grad_gate, grad_up, grad_heads, grad_proj = [
        grad.astype(F32) for grad in (grad_gate, grad_up, grad_heads, grad_proj)
    ]
    grad_query = grad_heads[:, :width]
    grad_key = grad_heads[:, width : width + kv_width]
    grad_value = grad_heads[:, width + kv_width :]
    grad_gain_attn, grad_gain_mlp = grad_proj[:, width], grad_proj[:, width + 1]
    grad_proj = grad_proj[:, :width]

    position = jnp.arange(total_rows)
    long_rows = position < rows
    offsets = jnp.where(long_rows, position, position % segment)
    micro = jnp.where(long_rows, 0, position // segment - 1)
    bound = jnp.zeros_like(position)
    for m in range(MICRO):
        bound = jnp.where(micro == m, group[m], bound)
    valid = (offsets < bound)[:, None]
    layer_output = jnp.where(valid, layer_output, 0.0)
    return (
        layer_output,
        grad_input,
        grad_query[None],
        grad_key[None],
        grad_value[None],
        grad_proj[None],
        grad_gate[None],
        grad_up[None],
        grad_down[None],
        grad_gain_attn[None],
        grad_gain_mlp[None],
    )


def solution(mesh):
    placed = (
        P("dp", "pipe"),
        P("dp", "pipe"),
        P("dp", None),
        P("pipe", None, None),
        P("pipe", None, None),
        P("pipe", None, None),
        P("pipe", None, None),
        P("pipe", None, None),
        P("pipe", None, None),
        P("pipe", None, None),
        P("pipe", None),
        P("pipe", None),
    )
    return jax.shard_map(
        per_device,
        mesh=mesh,
        in_specs=placed,
        out_specs=(
            P("dp", "pipe"),
            P("dp", "pipe"),
            P("pipe", "dp", None),
            P("pipe", "dp", None),
            P("pipe", "dp", None),
            P("pipe", "dp", None),
            P("pipe", "dp", None),
            P("pipe", "dp", None),
            P("pipe", "dp", None),
            P("pipe", "dp"),
            P("pipe", "dp"),
        ),
        check_vma=False,
    )
```

```python
import functools

import jax
import jax.numpy as jnp
import numpy as np
from jax import lax
from jax.experimental import pallas as pl
from jax.experimental.layout import Layout, with_layout_constraint
from jax.experimental.pallas import tpu as pltpu
from jax.sharding import PartitionSpec as P

HEAD_DIM = 64
HALF = HEAD_DIM // 2
LANES = 128
MICRO = 4
CHUNKS = 3
SCALE = HEAD_DIM**-0.5
BF16 = jnp.bfloat16
F32 = jnp.float32

epsilon = 1e-05
rope_base = 10000.0
masked_score = -1e30

ORDER = (
    *("H>", "G>", "P>", "H", "U>", "G", "D", "P", "H.", "G", "P.", "U", "d>", "e>", "G."),
    *("H>", "U", "P>", "d", "d", "e", "U.", "H.", "P.", "S", "d.", "e", "e."),
)
DOWN_PART = 13

def round_up(value, multiple):
    return -(-value // multiple) * multiple


def dot(left, right):
    return jnp.dot(left, right, preferred_element_type=F32)


def dot_t(left, right):
    return lax.dot_general(left, right, (((1,), (1,)), ((), ())), preferred_element_type=F32)


def dot_rows(left, right):
    return lax.dot_general(left, right, (((0,), (0,)), ((), ())), preferred_element_type=F32)


def lane_ids(rows):
    return lax.broadcasted_iota(jnp.int32, (rows, LANES), 1)


def in_low_half(rows):
    return lane_ids(rows) < HEAD_DIM


def rotate(slab, cosine, signed_sine):
    first = (lane_ids(slab.shape[0]) % HEAD_DIM) < HALF
    partner = jnp.where(
        first, pltpu.roll(slab, LANES - HALF, 1), pltpu.roll(slab, HALF, 1)
    )
    return slab * cosine + partner * signed_sine


def both_halves(slab, upper):
    swapped = pltpu.roll(slab, HEAD_DIM, 1)
    low = in_low_half(slab.shape[0])
    return jnp.where(low, swapped, slab) if upper else jnp.where(low, slab, swapped)


def sort_halves(slab, j, low, heads, kv_heads, key_rows, queries, keys, values):
    for head in (2 * j, 2 * j + 1):
        upper = head % 2 == 1
        if head < heads:
            kept = jnp.where(low, 0.0, slab) if upper else jnp.where(low, slab, 0.0)
            queries.append(kept.astype(BF16))
        elif head < heads + kv_heads:
            keys.append(pad_rows(both_halves(slab, upper).astype(BF16), key_rows))
        elif head < heads + 2 * kv_heads:
            values.append(pad_rows(both_halves(slab, upper).astype(BF16), key_rows))


def reciprocal_rms(value):
    return lax.rsqrt(jnp.mean(value * value, axis=-1, keepdims=True) + epsilon)


class Tick:
    def __init__(self, sizes, lengths):
        sections, depth_step, segment = sizes["sections"], sizes["depth_step"], sizes["rows"] // 2
        section = lax.axis_index("pipe")
        depth = sections - 1 - section if sizes["backward"] else section
        chunk = sizes["tick"] - depth_step * depth
        self.active = (chunk >= 0) & (chunk < CHUNKS)
        self.slot = jnp.clip(chunk, 0, CHUNKS - 1)
        self.edge = depth == 0
        self.final = depth == sections - 1
        self.is_long = self.slot == 0
        self.table = jnp.where(self.is_long, 1, 0)
        self.first_length = jnp.where(
            self.is_long, lengths[0, 0], jnp.where(self.slot == 1, lengths[0, 1], lengths[0, 3])
        )
        self.second_length = jnp.where(self.slot == 1, lengths[0, 2], segment)

    def bound(self, position, segment):
        return jnp.where(
            self.is_long,
            self.first_length,
            jnp.where(position < segment, self.first_length, self.second_length + segment),
        )


def score_bias(tick, query_rows, key_rows):
    query = lax.broadcasted_iota(jnp.int32, (query_rows, key_rows), 0)
    key = lax.broadcasted_iota(jnp.int32, (query_rows, key_rows), 1)
    segment = key_rows // 2
    start = jnp.where(tick.is_long, 0, jnp.where(query < segment, 0, segment))
    allowed = (key <= query) & (key < tick.bound(key, segment)) & (key >= start)
    return jnp.where(allowed, 0.0, masked_score).astype(F32)


def assemble(target, parts, at):
    count = min(target.shape[0], parts[0].shape[0] - at)
    target[:count, :] = jnp.concatenate(
        [part[at : at + count, :].astype(F32) for part in parts], axis=1
    )


def kept_at(kind, buffer, array, app, slot, rows, chunk, columns=None):
    columns = pl.ds(0, buffer.shape[-1]) if columns is None else columns
    if kind == "gains":
        return buffer.at[app], array.at[slot, app]
    if kind == "probs":
        taken = pl.ds(0, buffer.shape[2] * rows // chunk)
        return buffer.at[app, :, taken], array.at[slot, app, :, taken]
    at = pl.ds(pl.multiple_of(slot * chunk, chunk), rows)
    if kind == "slopes":
        return buffer.at[app, :, pl.ds(0, rows), columns], array.at[app, :, at, columns]
    return buffer.at[app, pl.ds(0, rows), columns], array.at[app, at, columns]


def chunk_sizes(sizes):
    full, total = sizes["rows"], sizes["total_rows"]
    found = {}
    for depth in range(sizes["sections"]):
        slot = sizes["tick"] - sizes["depth_step"] * depth
        if 0 <= slot < CHUNKS:
            found.setdefault(min(full, total - slot * full), []).append(slot)
    return found


def pad_rows(value, rows):
    missing = rows - value.shape[0]
    if not missing:
        return value
    return jnp.concatenate([value, jnp.zeros((missing, value.shape[1]), value.dtype)], axis=0)


def when(condition, action):
    pl.when(condition)(action)


def run_active(tick, sizes, run):
    found = chunk_sizes(sizes)
    for rows, slots in found.items():
        mine = functools.reduce(jnp.logical_or, [tick.slot == slot for slot in slots])
        when(tick.active & mine, functools.partial(run, rows))


def forward_kernel(sizes, lengths, *refs):
    tick = Tick(sizes, lengths)
    refs = list(refs)

    def take(count):
        taken = refs[:count]
        del refs[:count]
        return taken

    cosine_ref, sine_ref, gain_attn, gain_mlp = take(4)
    edge_parts, inbound = take(sizes["edge_parts"]), take(sizes["inbound"])
    w_heads, wp, wg, wu, wd = take(5)
    take(sizes["aliased"])
    out_round, out_full = take(2)
    stores = take(sizes["stores"])
    hidden_s, heads_s = take(2)
    buffers = take(sizes["stores"])
    (
        hidden_b,
        normed_attn_b,
        heads_b,
        probs_b,
        mixed_b,
        middle_b,
        normed_mlp_b,
        slopes_b,
        inner_b,
    ) = buffers
    (store_sems,) = refs
    chunk, width = hidden_s.shape
    heads = width // HEAD_DIM
    all_width = w_heads.shape[1]
    kv_heads = (all_width // HEAD_DIM - heads) // 2
    share = heads // kv_heads
    ff = wg.shape[1]
    slot = tick.slot

    step = sizes["ff_step"]

    def store(buffer, app, rows, part=None):
        i = [other is buffer for other in buffers].index(True)
        columns = None if part is None else pl.ds(part * step, step)
        source, target = kept_at(
            sizes["store_kinds"][i], buffer, stores[i], app, slot, rows, chunk, columns
        )
        return pltpu.make_async_copy(source, target, store_sems.at[i, app, part or 0])

    def apply(rows, app, carry):
        hidden = hidden_s[:rows]
        hidden_b[app, :rows] = hidden
        store(hidden_b, app, rows).start()
        normed = (hidden * reciprocal_rms(hidden) * gain_attn[...]).astype(BF16)
        normed_attn_b[app, :rows] = normed
        store(normed_attn_b, app, rows).start()
        heads_s[:rows, :all_width] = dot(normed, w_heads[...])
        cosine = cosine_ref[tick.table, :rows]
        sine = sine_ref[tick.table, :rows]
        low = in_low_half(rows)
        query_parts, keys, values = [], [], []
        for j in range(heads_s.shape[1] // LANES):
            slab = heads_s[:rows, j * LANES : (j + 1) * LANES]
            if 2 * j < heads + kv_heads:
                slab = rotate(slab, cosine, sine)
            heads_b[app, :rows, j * LANES : (j + 1) * LANES] = slab.astype(BF16)
            sort_halves(slab, j, low, heads, kv_heads, chunk, query_parts, keys, values)
        store(heads_b, app, rows).start()
        bias = score_bias(tick, rows, chunk)
        bias = jnp.concatenate([bias] * share, axis=0)
        mixed_parts = []
        for kv in range(kv_heads):
            grouped = jnp.concatenate(query_parts[kv * share : (kv + 1) * share], axis=0)
            scores = dot_t(grouped, keys[kv]) * SCALE + bias
            exponent = jnp.exp(scores - jnp.max(scores, axis=-1, keepdims=True))
            total = jnp.sum(exponent, axis=-1, keepdims=True)
            probs = (exponent * (1.0 / total)).astype(BF16)
            probs_b[app, kv, : share * rows] = probs
            mixed = dot(probs, values[kv])
            mixed_parts += [mixed[i * rows : (i + 1) * rows] for i in range(share)]
        store(probs_b, app, rows).start()
        for j in range(heads // 2):
            mixed_b[app, :rows, j * LANES : (j + 1) * LANES] = jnp.where(
                low, mixed_parts[2 * j], mixed_parts[2 * j + 1]
            ).astype(BF16)
        if heads % 2:
            mixed_b[app, :rows, width - HEAD_DIM :] = mixed_parts[-1][:, :HEAD_DIM].astype(BF16)
        store(mixed_b, app, rows).start()
        middle = hidden + dot(mixed_b[app, :rows], wp[...])
        middle_b[app, :rows] = middle
        store(middle_b, app, rows).start()
        normed = (middle * reciprocal_rms(middle) * gain_mlp[...]).astype(BF16)
        normed_mlp_b[app, :rows] = normed
        store(normed_mlp_b, app, rows).start()
        for part, at in enumerate(range(0, ff, step)):
            gate = dot(normed, wg[:, at : at + step])
            up = dot(normed, wu[:, at : at + step])
            sigma = 1.0 / (1.0 + jnp.exp(-gate))
            silu = gate * sigma
            inner_b[app, :rows, at : at + step] = (silu * up).astype(BF16)
            slopes_b[app, 0, :rows, at : at + step] = (
                up * (sigma * (1.0 + gate * (1.0 - sigma)))
            ).astype(BF16)
            slopes_b[app, 1, :rows, at : at + step] = silu.astype(BF16)
            store(inner_b, app, rows, part).start()
            store(slopes_b, app, rows, part).start()
        hidden_s[:rows] = middle + dot(inner_b[app, :rows], wd[...])
        return carry

    def run(rows):
        if edge_parts:

            @pl.when(tick.edge)
            def _():
                assemble(hidden_s, edge_parts, sizes["tick"] * chunk)

        if inbound:

            @pl.when(jnp.logical_not(tick.edge))
            def _():
                hidden_s[:rows] = inbound[0][:rows].astype(F32)

        heads_s[:, heads_s.shape[1] - LANES :] = jnp.zeros((chunk, LANES), F32)
        lax.fori_loop(0, 2, functools.partial(apply, rows), 0)
        out_round[:rows] = hidden_s[:rows].astype(BF16)

        @pl.when(tick.final)
        def _():
            row = lax.broadcasted_iota(jnp.int32, (rows, 1), 0)
            valid = row < tick.bound(row, chunk // 2)
            at = pl.ds(pl.multiple_of(slot * chunk, chunk), rows)
            out_full[at] = jnp.where(valid, hidden_s[:rows], 0.0).astype(BF16)

        for app in (0, 1):
            for buffer in buffers[:-2]:
                store(buffer, app, rows).wait()
            for part in range(ff // step):
                store(inner_b, app, rows, part).wait()
                store(slopes_b, app, rows, part).wait()

    run_active(tick, sizes, run)


def backward_kernel(sizes, lengths, *refs):
    tick = Tick(sizes, lengths)
    refs = list(refs)

    def take(count):
        taken = refs[:count]
        del refs[:count]
        return taken

    cosine_ref, sine_ref, gain_attn, gain_mlp = take(4)
    edge_parts, inbound = take(sizes["edge_parts"]), take(sizes["inbound"])
    w_heads, wp, wg, wu, wd = take(5)
    saved = take(sizes["reads"])
    take(sizes["aliased"])
    out_round, out_full = take(2)
    stores = take(sizes["stores"])
    grad_s, mixed_s, inner_s = take(3)
    kept = take(sizes["reads"])
    hidden_k, heads_k, probs_k, middle_k, slopes_k = kept
    buffers = take(sizes["stores"])
    branch_b, gate_b, up_b, attn_b, heads_b, gains_b = buffers
    read_sems, store_sems = refs
    chunk, width = grad_s.shape
    heads = width // HEAD_DIM
    all_width = w_heads.shape[0]
    kv_heads = (all_width // HEAD_DIM - heads) // 2
    share = heads // kv_heads
    ff = wd.shape[1]
    slot = tick.slot

    def read(buffer, app, rows):
        i = [other is buffer for other in kept].index(True)
        kind = sizes["read_kinds"][i]
        target, source = kept_at(kind, buffer, saved[i], app, slot, rows, chunk)
        return pltpu.make_async_copy(source, target, read_sems.at[i, app])

    def store(buffer, app, rows):
        i = [other is buffer for other in buffers].index(True)
        kind = sizes["store_kinds"][i]
        source, target = kept_at(kind, buffer, stores[i], app, slot, rows, chunk)
        return pltpu.make_async_copy(source, target, store_sems.at[i, app, 0])

    def rms_backward(value, gain, grad, running):
        scale = reciprocal_rms(value)
        unit = value * scale
        pulled = grad * gain
        gain_terms = grad * unit
        gain_rows = jnp.sum(gain_terms.reshape(grad.shape[0] // 8, 8, width), axis=0)
        shared = jnp.mean(gain_terms * gain, axis=-1, keepdims=True)
        return running + scale * (pulled - unit * shared), gain_rows

    def apply(rows, step_id, carry):
        app = 1 - step_id
        low = in_low_half(rows)
        grad_top = grad_s[:rows]
        branch = grad_top.astype(BF16)
        branch_b[app, :rows] = branch
        store(branch_b, app, rows).start()
        step = sizes["ff_step"]
        inner_s[:rows] = dot(branch, wd[...])
        read(slopes_k, app, rows).wait()
        for at in range(0, ff, step):
            inner_grad = inner_s[:rows, at : at + step]
            gate_b[app, :rows, at : at + step] = (
                inner_grad * slopes_k[app, 0, :rows, at : at + step].astype(F32)
            ).astype(BF16)
            up_b[app, :rows, at : at + step] = (
                inner_grad * slopes_k[app, 1, :rows, at : at + step].astype(F32)
            ).astype(BF16)
        store(gate_b, app, rows).start()
        store(up_b, app, rows).start()
        pulled = dot(gate_b[app, :rows], wg[...])
        pulled += dot(up_b[app, :rows], wu[...])
        read(middle_k, app, rows).wait()
        middle_grad, gain_rows = rms_backward(
            middle_k[app, :rows], gain_mlp[...], pulled, grad_top
        )
        gains_b[app, 1] = gain_rows
        attn_grad = middle_grad.astype(BF16)
        attn_b[app, :rows] = attn_grad
        store(attn_b, app, rows).start()
        mixed_s[:rows, :width] = dot(attn_grad, wp[...])
        mixed_parts, query_parts, keys, values = [], [], [], []
        for j in range(mixed_s.shape[1] // LANES):
            slab = mixed_s[:rows, j * LANES : (j + 1) * LANES]
            mixed_parts.append(jnp.where(low, slab, 0.0).astype(BF16))
            mixed_parts.append(jnp.where(low, 0.0, slab).astype(BF16))
        read(heads_k, app, rows).wait()
        for j in range(heads_k.shape[-1] // LANES):
            slab = heads_k[app, :rows, j * LANES : (j + 1) * LANES].astype(F32)
            sort_halves(slab, j, low, heads, kv_heads, chunk, query_parts, keys, values)
        cosine = cosine_ref[tick.table, :rows]
        sine = -sine_ref[tick.table, :rows]
        ones = jnp.ones((chunk, LANES), BF16)
        query_grads, key_grads, value_grads = [], [], []
        read(probs_k, app, rows).wait()
        for kv in range(kv_heads):
            mixed = jnp.concatenate(mixed_parts[kv * share : (kv + 1) * share], axis=0)
            grouped = jnp.concatenate(query_parts[kv * share : (kv + 1) * share], axis=0)
            probs = probs_k[app, kv, : share * rows]
            probs_wide = probs.astype(F32)
            probs_grad = dot_t(mixed, values[kv])
            weighted = probs_wide * probs_grad
            shared = dot(weighted.astype(BF16), ones)
            score_grad = (weighted - probs_wide * shared).astype(BF16)
            pulled = dot(score_grad, keys[kv])
            query_grads += [pulled[i * rows : (i + 1) * rows] for i in range(share)]
            pulled = dot_rows(score_grad, grouped)[:rows]
            key_grads.append(pulled + pltpu.roll(pulled, HEAD_DIM, 1))
            pulled = dot_rows(probs, mixed)[:rows]
            value_grads.append(pulled + pltpu.roll(pulled, HEAD_DIM, 1))

        parts = query_grads + key_grads + value_grads
        for j in range(len(parts) // 2):
            slab = jnp.where(low, parts[2 * j], parts[2 * j + 1])
            if 2 * j < heads + kv_heads:
                slab = rotate(slab * SCALE, cosine, sine)
            heads_b[app, :rows, j * LANES : (j + 1) * LANES] = slab.astype(BF16)
        if len(parts) % 2:
            heads_b[app, :rows, all_width - HEAD_DIM :] = parts[-1][:, :HEAD_DIM].astype(BF16)
        store(heads_b, app, rows).start()
        pulled = dot(heads_b[app, :rows], w_heads[...])
        read(hidden_k, app, rows).wait()
        result, gain_rows = rms_backward(
            hidden_k[app, :rows], gain_attn[...], pulled, middle_grad
        )
        gains_b[app, 0] = gain_rows
        store(gains_b, app, rows).start()
        grad_s[:rows] = result
        return carry

    def run(rows):
        for app in (1, 0):
            for buffer in (slopes_k, middle_k, heads_k, probs_k, hidden_k):
                read(buffer, app, rows).start()
        if edge_parts:

            @pl.when(tick.edge)
            def _():
                assemble(grad_s, edge_parts, sizes["tick"] * chunk)
                row = lax.broadcasted_iota(jnp.int32, (chunk, 1), 0)
                grad_s[...] = jnp.where(row < tick.bound(row, chunk // 2), grad_s[...], 0.0)

        if inbound:

            @pl.when(jnp.logical_not(tick.edge))
            def _():
                grad_s[:rows] = inbound[0][:rows].astype(F32)

        mixed_s[:, mixed_s.shape[1] - LANES :] = jnp.zeros((chunk, LANES), F32)
        lax.fori_loop(0, 2, functools.partial(apply, rows), 0)
        out_round[:rows] = grad_s[:rows].astype(BF16)

        @pl.when(tick.final)
        def _():
            at = pl.ds(pl.multiple_of(slot * chunk, chunk), rows)
            out_full[at] = grad_s[:rows].astype(BF16)

        for buffer in buffers:
            store(buffer, 0, rows).wait()
            store(buffer, 1, rows).wait()

    run_active(tick, sizes, run)


def transpose_to(target, source):
    for at in range(0, source.shape[1], 256):
        end = min(at + 256, source.shape[1])
        target[at:end, :] = jnp.transpose(source[:, at:end])


def load_kernel(extras, *refs):
    key_t, value_t, query, proj, gate, up, down_t = refs[:7]
    extra_in, refs = refs[7 : 7 + extras], refs[7 + extras :]
    heads_t, heads, proj_v, gate_v, up_v, down_tv, down = refs[:7]
    extra_out, (query_v, sems) = refs[7 : 7 + extras], refs[7 + extras :]
    width, kv_width = query.shape[1], key_t.shape[0]
    pairs = (
        (down_t, down_tv),
        (query, query_v),
        (key_t, heads_t.at[pl.ds(width, kv_width)]),
        (value_t, heads_t.at[pl.ds(width + kv_width, kv_width)]),
        (proj, proj_v),
        (gate, gate_v),
        (up, up_v),
        *zip(extra_in, extra_out),
    )
    copies = [
        pltpu.make_async_copy(source, target, sems.at[i])
        for i, (source, target) in enumerate(pairs)
    ]
    for copy in copies:
        copy.start()
    copies[0].wait()
    transpose_to(down, down_tv)
    copies[1].wait()
    transpose_to(heads_t, query_v)
    copies[2].wait()
    copies[3].wait()
    transpose_to(heads, heads_t)
    for copy in copies[4:]:
        copy.wait()


def turn_kernel(first, count, *refs):
    sources, targets = refs[:count], refs[-count:]

    @pl.when((lax.axis_index("pipe") == 0) == first)
    def _():
        for source, target in zip(sources, targets):
            transpose_to(target, source)


def load_weights(query, key_t, value_t, proj, gate, up, down_t, *extra):
    sources = (key_t, value_t, query, proj, gate, up, down_t, *extra)
    all_width = query.shape[1] + 2 * key_t.shape[0]
    shapes = (
        (all_width, query.shape[0]),
        (query.shape[0], all_width),
        proj.shape,
        gate.shape,
        up.shape,
        down_t.shape,
        down_t.shape[::-1],
    )
    outs = [pltpu.VMEM(tuple(shape), BF16) for shape in shapes]
    outs += [pltpu.VMEM(array.shape, array.dtype) for array in extra]
    return pl.pallas_call(
        functools.partial(load_kernel, len(extra)),
        out_shape=outs,
        in_specs=[in_hbm() for _ in sources],
        out_specs=[in_vmem() for _ in outs],
        scratch_shapes=[
            pltpu.VMEM(query.shape, BF16),
            pltpu.SemaphoreType.DMA((len(sources),)),
        ],
        compiler_params=pltpu.CompilerParams(vmem_limit_bytes=8 * 2**20),
        name="load_weights",
    )(*[pltpu.with_memory_space_constraint(array, pltpu.HBM) for array in sources])


def turn_weights(weights, first, turned=()):
    count = len(weights)
    return pl.pallas_call(
        functools.partial(turn_kernel, first, count),
        out_shape=[pltpu.VMEM(tuple(weight.shape[::-1]), BF16) for weight in weights],
        in_specs=[in_vmem() for _ in (*weights, *turned)],
        out_specs=[in_vmem() for _ in weights],
        input_output_aliases={count + i: i for i in range(len(turned))},
        compiler_params=pltpu.CompilerParams(vmem_limit_bytes=8 * 2**20),
        name="turn_weights",
    )(*[pltpu.with_memory_space_constraint(weight, pltpu.VMEM) for weight in (*weights, *turned)])


def in_vmem():
    return pl.BlockSpec(memory_space=pltpu.VMEM)


def in_hbm():
    return pl.BlockSpec(memory_space=pltpu.HBM)


def kind_of(array):
    return {5: "probs" if array.dtype == BF16 else "gains", 4: "slopes", 3: "rows"}[len(array.shape)]


def buffers_for(arrays, rows):
    shapes = []
    for array in arrays:
        kind, shape = kind_of(array), tuple(array.shape)
        if kind in ("probs", "gains"):
            shapes.append(shape[1:])
        else:
            shapes.append(shape[:-2] + (rows, shape[-1]))
    return [pltpu.VMEM(shape, array.dtype) for shape, array in zip(shapes, arrays)]


def run_tick(
    kernel, sizes, lengths, tables, edge_parts, inbound, weights, reads, state, shapes, scratch, name
):
    rows, width = sizes["rows"], sizes["width"]
    aliased = [] if state is None else list(state)
    inbound = [] if inbound is None else [inbound]
    outs = [jax.ShapeDtypeStruct((rows, width), BF16), pltpu.VMEM((sizes["total_rows"], width), BF16)]
    outs += [pltpu.HBM(shape.shape, shape.dtype) for shape in shapes]
    scratch = scratch + buffers_for(reads, rows) + buffers_for(shapes, rows)
    if reads:
        scratch.append(pltpu.SemaphoreType.DMA((len(reads), 2)))
    scratch.append(pltpu.SemaphoreType.DMA((len(shapes), 2, 2)))
    blocks = [*tables, *edge_parts, *inbound]
    kept = len(tables) + (0 if sizes["backward"] else len(edge_parts))
    blocks[:kept] = [pltpu.with_memory_space_constraint(array, pltpu.VMEM) for array in blocks[:kept]]
    first_alias = 1 + len(blocks) + len(weights) + len(reads)
    sizes = dict(
        sizes,
        edge_parts=len(edge_parts),
        inbound=len(inbound),
        aliased=len(aliased),
        stores=len(shapes),
        reads=len(reads),
        store_kinds=[kind_of(shape) for shape in shapes],
        read_kinds=[kind_of(read) for read in reads],
    )
    flops = 4 * rows * sum(int(np.prod(weight.shape)) for weight in weights)
    return pl.pallas_call(
        functools.partial(kernel, sizes),
        out_shape=outs,
        grid_spec=pltpu.PrefetchScalarGridSpec(
            num_scalar_prefetch=1,
            grid=(1,),
            in_specs=[in_vmem() for _ in (*blocks, *weights)]
            + [in_hbm() for _ in reads]
            + [in_vmem() for _ in aliased[:1]]
            + [in_hbm() for _ in aliased[1:]],
            out_specs=[in_vmem(), in_vmem()] + [in_hbm() for _ in shapes],
            scratch_shapes=scratch,
        ),
        input_output_aliases={first_alias + i: 1 + i for i in range(len(aliased))},
        compiler_params=pltpu.CompilerParams(
            dimension_semantics=("arbitrary",), vmem_limit_bytes=61 * 2**18
        ),
        cost_estimate=pl.CostEstimate(
            flops=flops, bytes_accessed=flops // (2 * rows), transcendentals=0
        ),
        name=name,
    )(
        lengths,
        *blocks,
        *[pltpu.with_memory_space_constraint(weight, pltpu.VMEM) for weight in weights],
        *[pltpu.with_memory_space_constraint(array, pltpu.HBM) for array in reads],
        *[pltpu.with_memory_space_constraint(array, pltpu.VMEM) for array in aliased[:1]],
        *[pltpu.with_memory_space_constraint(array, pltpu.HBM) for array in aliased[1:]],
    )


def rope_tables(rows):
    segment = rows // 2
    frequency = rope_base ** (-np.arange(HALF, dtype=np.float64) / HALF)
    positions = np.stack([np.arange(rows) % segment, np.arange(rows)]).astype(np.float64)
    angles = np.tile(positions[:, :, None] * frequency, (1, 1, LANES // HALF))
    sign = np.where(np.arange(LANES) % HEAD_DIM < HALF, -1.0, 1.0)
    return (
        jnp.asarray(np.cos(angles), F32),
        jnp.asarray(np.sin(angles) * sign, F32),
    )


def gather_ends(inputs, cotangent):
    sections, section = lax.axis_size("pipe"), lax.axis_index("pipe")
    last = sections - 1
    input_parts, cotangent_parts = [inputs] * sections, [cotangent] * sections
    for source in range(1, sections):
        mirror = last - source
        if mirror == source:
            input_parts[source] = lax.ppermute(inputs, "pipe", [(source, 0)])
            cotangent_parts[source] = lax.ppermute(cotangent, "pipe", [(source, last)])
            continue
        sent = jnp.where(section == mirror, cotangent, inputs)
        got = lax.ppermute(sent, "pipe", [(source, 0), (mirror, last)])
        input_parts[source] = cotangent_parts[mirror] = got
    return input_parts, cotangent_parts


def spread_ends(results, input_grads):
    sections, section = lax.axis_size("pipe"), lax.axis_index("pipe")
    last = sections - 1
    columns = results.shape[1] // sections

    def block(value, at):
        return value[:, at * columns : (at + 1) * columns]

    outputs, grads = block(results, last), block(input_grads, 0)
    for target in range(last):
        mirror = last - target
        if mirror == target:
            got = lax.ppermute(block(results, target), "pipe", [(last, target)])
            outputs = jnp.where(section == target, got, outputs)
            got = lax.ppermute(block(input_grads, target), "pipe", [(0, target)])
            grads = jnp.where(section == target, got, grads)
            continue
        sent = jnp.where(section == 0, block(input_grads, mirror), block(results, target))
        got = lax.ppermute(sent, "pipe", [(last, target), (0, mirror)])
        outputs = jnp.where(section == target, got, outputs)
        grads = jnp.where(section == mirror, got, grads)
    return outputs.astype(F32), grads.astype(F32)


def after(values, *tokens):
    return lax.optimization_barrier((values, tokens))[0]


def by_rows(value):
    return with_layout_constraint(value, Layout(major_to_minor=(0, 1)))


def cube_view(value):
    bits = lax.axis_size("dp").bit_length() - 1
    rows, columns = value.shape
    return value.reshape((2,) * bits + (rows >> bits, columns))


class Piece:
    def __init__(self, value, bits):
        self.value, self.bits, self.got = value, list(bits), None

    def send(self, *tokens):
        devices = lax.axis_size("dp")
        bit = self.bits.pop(0)
        axis = devices.bit_length() - 2 - bit
        mine = (lax.axis_index("dp") >> bit) & 1
        sent = lax.dynamic_index_in_dim(self.value, 1 - mine, axis)
        if tokens:
            sent = after(sent, *tokens)
        self.kept = (axis, mine)
        self.got = lax.ppermute(sent, "dp", [(i, i ^ (1 << bit)) for i in range(devices)])
        return sent

    def take(self, *tokens):
        axis, mine = self.kept
        got = after(self.got, *tokens) if tokens else self.got
        self.value = lax.dynamic_index_in_dim(self.value, mine, axis) + got
        return self.value


def per_device(
    inputs,
    cotangent,
    lengths,
    w_query,
    w_key,
    w_value,
    w_proj,
    w_gate,
    w_up,
    w_down,
    gain_attn,
    gain_mlp,
):
    sections = lax.axis_size("pipe")
    section = lax.axis_index("pipe")
    total_rows, columns = inputs.shape
    width = columns * sections
    rows = 2 * total_rows // (MICRO + 1)
    segment = rows // 2
    kv_width = w_key.shape[-1]
    ff = w_gate.shape[-1]
    kv_heads = kv_width // HEAD_DIM
    share = width // kv_width
    depth_step = 2
    ticks = CHUNKS + depth_step * (sections - 1)
    sizes = dict(
        rows=rows,
        total_rows=total_rows,
        width=width,
        ff_step=ff // 2,
        sections=sections,
        depth_step=depth_step,
    )
    group = lengths[0]
    input_parts, cotangent_parts = gather_ends(inputs, cotangent)
    w_heads_t, w_heads, wp, wg, wu, wd_t, wd, *tables = load_weights(
        w_query[0],
        jnp.swapaxes(w_key[0], 0, 1),
        jnp.swapaxes(w_value[0], 0, 1),
        w_proj[0],
        w_gate[0],
        w_up[0],
        jnp.swapaxes(w_down[0], 0, 1),
        *rope_tables(rows),
        gain_attn,
        gain_mlp,
        inputs,
    )
    input_parts[0] = tables.pop()
    turned = turn_weights((wp, wg, wu), False)
    forward_weights = (w_heads, wp, wg, wu, wd)

    def stored(*shape, dtype=BF16):
        return jax.ShapeDtypeStruct(shape, dtype)

    query_pad = round_up(width, LANES)
    all_width = width + 2 * kv_width
    heads_pad = round_up(all_width, LANES)
    forward_shapes = [
        stored(2, total_rows, width, dtype=F32),
        stored(2, total_rows, width),
        stored(2, total_rows, heads_pad),
        stored(CHUNKS, 2, kv_heads, share * rows, rows),
        stored(2, total_rows, width),
        stored(2, total_rows, width, dtype=F32),
        stored(2, total_rows, width),
        stored(2, 2, total_rows, ff),
        stored(2, total_rows, ff),
    ]
    forward_scratch = [
        pltpu.VMEM((rows, width), F32),
        pltpu.VMEM((rows, heads_pad), F32),
    ]
    sent = {}
    state = None
    for tick in range(ticks):
        rounded, *state = run_tick(
            forward_kernel,
            dict(sizes, tick=tick, backward=False),
            lengths,
            tables,
            input_parts if tick < CHUNKS else (),
            sent.get(tick - depth_step),
            forward_weights,
            (),
            state,
            forward_shapes,
            forward_scratch,
            "layer_pair_forward",
        )
        route = [
            (s, s + 1) for s in range(sections - 1) if 0 <= tick - depth_step * s < CHUNKS
        ]
        if route:
            sent[tick] = lax.ppermute(rounded, "pipe", route)
        if tick == CHUNKS - 1:
            ready, _ = lax.optimization_barrier(((wp, wg, wu), rounded))
            turned = turn_weights(ready, True, turned)
    backward_weights = (w_heads_t, *turned, wd_t)
    results = state[0]
    hidden, normed_attn, heads, probs, mixed, middle, normed_mlp, slopes, inner = state[1:]

    backward_shapes = [
        stored(2, total_rows, width),
        stored(2, total_rows, ff),
        stored(2, total_rows, ff),
        stored(2, total_rows, width),
        stored(2, total_rows, all_width),
        stored(CHUNKS, 2, 2, 8, width, dtype=F32),
    ]
    backward_scratch = [
        pltpu.VMEM((rows, width), F32),
        pltpu.VMEM((rows, query_pad), F32),
        pltpu.VMEM((rows, ff), F32),
    ]
    reads = (hidden, heads, probs, middle, slopes)
    sent = {}
    state = None
    for tick in range(ticks):
        rounded, *state = run_tick(
            backward_kernel,
            dict(sizes, tick=tick, backward=True),
            lengths,
            tables,
            cotangent_parts if tick < CHUNKS else (),
            sent.get(tick - depth_step),
            backward_weights,
            reads,
            state,
            backward_shapes,
            backward_scratch,
            "layer_pair_backward",
        )
        route = [
            (s, s - 1)
            for s in range(1, sections)
            if 0 <= tick - depth_step * (sections - 1 - s) < CHUNKS
        ]
        if route:
            sent[tick] = lax.ppermute(rounded, "pipe", route)
    input_grads = state[0]
    branch, gate_grad, up_grad, attn_grad, heads_grad, gains = state[1:]

    def product(left, right):
        left = left.reshape(2 * total_rows, left.shape[-1])
        right = right.reshape(2 * total_rows, right.shape[-1])
        return by_rows(dot_rows(left, right).astype(BF16))

    bits = lax.axis_size("dp").bit_length() - 1
    across_first, along_first = range(bits), [*range(1, bits), 0]
    gain_sums = jnp.swapaxes(jnp.sum(gains, axis=(0, 1, 3)), 0, 1).astype(BF16)

    def make(name, token):
        terms = dict(
            G=(normed_mlp, gate_grad),
            U=(normed_mlp, up_grad),
            H=(normed_attn, heads_grad),
            P=(mixed, attn_grad),
            D=(inner, branch),
        )[name]
        value = product(*(terms if token is None else after(terms, token)))
        if name == "P":
            value = jnp.concatenate([value, gain_sums], axis=1)
        view = cube_view(value)
        if name != "D":
            return {name: Piece(view, along_first if name in "HP" else across_first)}
        part = view.shape[-2] * DOWN_PART // 20 // 16 * 16
        return {
            "d": Piece(view[..., :part, :], across_first),
            "e": Piece(view[..., part:, :], across_first),
        }

    pieces, token, outputs = {}, None, None
    for step in ORDER:
        name, mark = step[0], step[1:]
        if name == "S":
            outputs = spread_ends(*after((results, input_grads), token))
            continue
        if name not in pieces:
            pieces.update(make(name, token))
            if name == "D":
                token = pieces["e"].value
                continue
        piece = pieces[name]
        if mark != ">":
            token = piece.take(token)
        if mark == ".":
            spare = 0 if name in "HP" and 0 in piece.bits else len(piece.bits)
            spare = len(piece.bits) - 1 if name in "HP" and 0 in piece.bits else spare
            for _ in range(spare):
                piece.send()
                token = piece.take()
        else:
            token = piece.send(*(() if token is None else (token,)))
    layer_output, grad_input = outputs
    ends = {name: piece.value.reshape(piece.value.shape[-2:]) for name, piece in pieces.items()}
    grad_down = jnp.concatenate([ends["d"], ends["e"]], axis=0).astype(F32)
    grad_gate, grad_up, grad_heads, grad_proj = [ends[name] for name in "GUHP"]
    grad_gate, grad_up, grad_heads, grad_proj = [
        grad.astype(F32) for grad in (grad_gate, grad_up, grad_heads, grad_proj)
    ]
    grad_query = grad_heads[:, :width]
    grad_key = grad_heads[:, width : width + kv_width]
    grad_value = grad_heads[:, width + kv_width :]
    grad_gain_attn, grad_gain_mlp = grad_proj[:, width], grad_proj[:, width + 1]
    grad_proj = grad_proj[:, :width]

    return (
        layer_output,
        grad_input,
        grad_query[None],
        grad_key[None],
        grad_value[None],
        grad_proj[None],
        grad_gate[None],
        grad_up[None],
        grad_down[None],
        grad_gain_attn[None],
        grad_gain_mlp[None],
    )


def solution(mesh):
    placed = (
        P("dp", "pipe"),
        P("dp", "pipe"),
        P("dp", None),
        P("pipe", None, None),
        P("pipe", None, None),
        P("pipe", None, None),
        P("pipe", None, None),
        P("pipe", None, None),
        P("pipe", None, None),
        P("pipe", None, None),
        P("pipe", None),
        P("pipe", None),
    )
    return jax.shard_map(
        per_device,
        mesh=mesh,
        in_specs=placed,
        out_specs=(
            P("dp", "pipe"),
            P("dp", "pipe"),
            P("pipe", "dp", None),
            P("pipe", "dp", None),
            P("pipe", "dp", None),
            P("pipe", "dp", None),
            P("pipe", "dp", None),
            P("pipe", "dp", None),
            P("pipe", "dp", None),
            P("pipe", "dp"),
            P("pipe", "dp"),
        ),
        check_vma=False,
    )
```

```python
import functools

import jax
import jax.numpy as jnp
import numpy as np
from jax import lax
from jax.experimental import pallas as pl
from jax.experimental.layout import Layout, with_layout_constraint
from jax.experimental.pallas import tpu as pltpu
from jax.sharding import PartitionSpec as P

HEAD_DIM = 64
HALF = HEAD_DIM // 2
LANES = 128
MICRO = 4
CHUNKS = 3
SCALE = HEAD_DIM**-0.5
BF16 = jnp.bfloat16
F32 = jnp.float32

epsilon = 1e-05
rope_base = 10000.0
masked_score = -1e30

ORDER = (
    *("H>", "G>", "P>", "H", "U>", "G", "D", "P", "H.", "G", "P.", "U", "d>", "e>", "G."),
    *("H>", "U", "P>", "d", "d", "e", "U.", "H.", "P.", "S", "d.", "e", "e."),
)
DOWN_PART = 13

def round_up(value, multiple):
    return -(-value // multiple) * multiple


def dot(left, right):
    return jnp.dot(left, right, preferred_element_type=F32)


def dot_t(left, right):
    return lax.dot_general(left, right, (((1,), (1,)), ((), ())), preferred_element_type=F32)


def dot_rows(left, right):
    return lax.dot_general(left, right, (((0,), (0,)), ((), ())), preferred_element_type=F32)


def lane_ids(rows):
    return lax.broadcasted_iota(jnp.int32, (rows, LANES), 1)


def in_low_half(rows):
    return lane_ids(rows) < HEAD_DIM


def rotate(slab, cosine, signed_sine):
    first = (lane_ids(slab.shape[0]) % HEAD_DIM) < HALF
    partner = jnp.where(
        first, pltpu.roll(slab, LANES - HALF, 1), pltpu.roll(slab, HALF, 1)
    )
    return slab * cosine + partner * signed_sine


def both_halves(slab, upper):
    swapped = pltpu.roll(slab, HEAD_DIM, 1)
    low = in_low_half(slab.shape[0])
    return jnp.where(low, swapped, slab) if upper else jnp.where(low, slab, swapped)


def sort_halves(slab, j, low, heads, kv_heads, key_rows, queries, keys, values):
    for head in (2 * j, 2 * j + 1):
        upper = head % 2 == 1
        if head < heads:
            kept = jnp.where(low, 0.0, slab) if upper else jnp.where(low, slab, 0.0)
            queries.append(kept.astype(BF16))
        elif head < heads + kv_heads:
            keys.append(pad_rows(both_halves(slab, upper).astype(BF16), key_rows))
        elif head < heads + 2 * kv_heads:
            values.append(pad_rows(both_halves(slab, upper).astype(BF16), key_rows))


def reciprocal_rms(value):
    return lax.rsqrt(jnp.mean(value * value, axis=-1, keepdims=True) + epsilon)


class Tick:
    def __init__(self, sizes, lengths):
        sections, depth_step, segment = sizes["sections"], sizes["depth_step"], sizes["rows"] // 2
        section = lax.axis_index("pipe")
        depth = sections - 1 - section if sizes["backward"] else section
        chunk = sizes["tick"] - depth_step * depth
        self.active = (chunk >= 0) & (chunk < CHUNKS)
        self.slot = jnp.clip(chunk, 0, CHUNKS - 1)
        self.edge = depth == 0
        self.final = depth == sections - 1
        self.is_long = self.slot == 0
        self.table = jnp.where(self.is_long, 1, 0)
        self.first_length = jnp.where(
            self.is_long, lengths[0, 0], jnp.where(self.slot == 1, lengths[0, 1], lengths[0, 3])
        )
        self.second_length = jnp.where(self.slot == 1, lengths[0, 2], segment)

    def bound(self, position, segment):
        return jnp.where(
            self.is_long,
            self.first_length,
            jnp.where(position < segment, self.first_length, self.second_length + segment),
        )


def score_bias(tick, query_rows, key_rows):
    query = lax.broadcasted_iota(jnp.int32, (query_rows, key_rows), 0)
    key = lax.broadcasted_iota(jnp.int32, (query_rows, key_rows), 1)
    segment = key_rows // 2
    start = jnp.where(tick.is_long, 0, jnp.where(query < segment, 0, segment))
    allowed = (key <= query) & (key < tick.bound(key, segment)) & (key >= start)
    return jnp.where(allowed, 0.0, masked_score).astype(F32)


def assemble(target, parts, at):
    count = min(target.shape[0], parts[0].shape[0] - at)
    target[:count, :] = jnp.concatenate(
        [part[at : at + count, :].astype(F32) for part in parts], axis=1
    )


def kept_at(kind, buffer, array, app, slot, rows, chunk, columns=None):
    columns = pl.ds(0, buffer.shape[-1]) if columns is None else columns
    if kind == "gains":
        return buffer.at[app], array.at[slot, app]
    if kind == "probs":
        taken = pl.ds(0, buffer.shape[2] * rows // chunk)
        return buffer.at[app, :, taken], array.at[slot, app, :, taken]
    at = pl.ds(pl.multiple_of(slot * chunk, chunk), rows)
    if kind == "slopes":
        return buffer.at[app, :, pl.ds(0, rows), columns], array.at[app, :, at, columns]
    return buffer.at[app, pl.ds(0, rows), columns], array.at[app, at, columns]


def chunk_sizes(sizes):
    full, total = sizes["rows"], sizes["total_rows"]
    found = {}
    for depth in range(sizes["sections"]):
        slot = sizes["tick"] - sizes["depth_step"] * depth
        if 0 <= slot < CHUNKS:
            found.setdefault(min(full, total - slot * full), []).append(slot)
    return found


def pad_rows(value, rows):
    missing = rows - value.shape[0]
    if not missing:
        return value
    return jnp.concatenate([value, jnp.zeros((missing, value.shape[1]), value.dtype)], axis=0)


def when(condition, action):
    pl.when(condition)(action)


def run_active(tick, sizes, run):
    found = chunk_sizes(sizes)
    for rows, slots in found.items():
        mine = functools.reduce(jnp.logical_or, [tick.slot == slot for slot in slots])
        when(tick.active & mine, functools.partial(run, rows))


def forward_kernel(sizes, lengths, *refs):
    tick = Tick(sizes, lengths)
    refs = list(refs)

    def take(count):
        taken = refs[:count]
        del refs[:count]
        return taken

    cosine_ref, sine_ref, gain_attn, gain_mlp = take(4)
    edge_parts, inbound = take(sizes["edge_parts"]), take(sizes["inbound"])
    w_heads, wp, wg, wu, wd = take(5)
    take(sizes["aliased"])
    out_round, out_full = take(2)
    stores = take(sizes["stores"])
    hidden_s, heads_s = take(2)
    buffers = take(sizes["stores"])
    (
        hidden_b,
        normed_attn_b,
        heads_b,
        probs_b,
        mixed_b,
        middle_b,
        normed_mlp_b,
        slopes_b,
        inner_b,
    ) = buffers
    (store_sems,) = refs
    chunk, width = hidden_s.shape
    heads = width // HEAD_DIM
    all_width = w_heads.shape[1]
    kv_heads = (all_width // HEAD_DIM - heads) // 2
    share = heads // kv_heads
    ff = wg.shape[1]
    slot = tick.slot

    step = sizes["ff_step"]

    def store(buffer, app, rows, part=None):
        i = [other is buffer for other in buffers].index(True)
        columns = None if part is None else pl.ds(part * step, step)
        source, target = kept_at(
            sizes["store_kinds"][i], buffer, stores[i], app, slot, rows, chunk, columns
        )
        return pltpu.make_async_copy(source, target, store_sems.at[i, app, part or 0])

    def apply(rows, app, carry):
        hidden = hidden_s[:rows]
        hidden_b[app, :rows] = hidden
        store(hidden_b, app, rows).start()
        normed = (hidden * reciprocal_rms(hidden) * gain_attn[...]).astype(BF16)
        normed_attn_b[app, :rows] = normed
        store(normed_attn_b, app, rows).start()
        heads_s[:rows, :all_width] = dot(normed, w_heads[...])
        cosine = cosine_ref[tick.table, :rows]
        sine = sine_ref[tick.table, :rows]
        low = in_low_half(rows)
        query_parts, keys, values = [], [], []
        for j in range(heads_s.shape[1] // LANES):
            slab = heads_s[:rows, j * LANES : (j + 1) * LANES]
            if 2 * j < heads + kv_heads:
                slab = rotate(slab, cosine, sine)
            heads_b[app, :rows, j * LANES : (j + 1) * LANES] = slab.astype(BF16)
            sort_halves(slab, j, low, heads, kv_heads, chunk, query_parts, keys, values)
        store(heads_b, app, rows).start()
        bias = score_bias(tick, rows, chunk)
        bias = jnp.concatenate([bias] * share, axis=0)
        mixed_parts = []
        for kv in range(kv_heads):
            grouped = jnp.concatenate(query_parts[kv * share : (kv + 1) * share], axis=0)
            scores = dot_t(grouped, keys[kv]) * SCALE + bias
            exponent = jnp.exp(scores - jnp.max(scores, axis=-1, keepdims=True))
            total = jnp.sum(exponent, axis=-1, keepdims=True)
            probs = (exponent * (1.0 / total)).astype(BF16)
            probs_b[app, kv, : share * rows] = probs
            mixed = dot(probs, values[kv])
            mixed_parts += [mixed[i * rows : (i + 1) * rows] for i in range(share)]
        store(probs_b, app, rows).start()
        for j in range(heads // 2):
            mixed_b[app, :rows, j * LANES : (j + 1) * LANES] = jnp.where(
                low, mixed_parts[2 * j], mixed_parts[2 * j + 1]
            ).astype(BF16)
        if heads % 2:
            mixed_b[app, :rows, width - HEAD_DIM :] = mixed_parts[-1][:, :HEAD_DIM].astype(BF16)
        store(mixed_b, app, rows).start()
        middle = hidden + dot(mixed_b[app, :rows], wp[...])
        middle_b[app, :rows] = middle
        store(middle_b, app, rows).start()
        normed = (middle * reciprocal_rms(middle) * gain_mlp[...]).astype(BF16)
        normed_mlp_b[app, :rows] = normed
        store(normed_mlp_b, app, rows).start()
        for part, at in enumerate(range(0, ff, step)):
            gate = dot(normed, wg[:, at : at + step])
            up = dot(normed, wu[:, at : at + step])
            sigma = 1.0 / (1.0 + jnp.exp(-gate))
            silu = gate * sigma
            inner_b[app, :rows, at : at + step] = (silu * up).astype(BF16)
            slopes_b[app, 0, :rows, at : at + step] = (
                up * (sigma * (1.0 + gate * (1.0 - sigma)))
            ).astype(BF16)
            slopes_b[app, 1, :rows, at : at + step] = silu.astype(BF16)
            store(inner_b, app, rows, part).start()
            store(slopes_b, app, rows, part).start()
        hidden_s[:rows] = middle + dot(inner_b[app, :rows], wd[...])
        return carry

    def run(rows):
        if edge_parts:

            @pl.when(tick.edge)
            def _():
                assemble(hidden_s, edge_parts, sizes["tick"] * chunk)

        if inbound:

            @pl.when(jnp.logical_not(tick.edge))
            def _():
                hidden_s[:rows] = inbound[0][:rows].astype(F32)

        heads_s[:, heads_s.shape[1] - LANES :] = jnp.zeros((chunk, LANES), F32)
        lax.fori_loop(0, 2, functools.partial(apply, rows), 0)
        out_round[:rows] = hidden_s[:rows].astype(BF16)

        @pl.when(tick.final)
        def _():
            row = lax.broadcasted_iota(jnp.int32, (rows, 1), 0)
            valid = row < tick.bound(row, chunk // 2)
            at = pl.ds(pl.multiple_of(slot * chunk, chunk), rows)
            out_full[at] = jnp.where(valid, hidden_s[:rows], 0.0).astype(BF16)

        for app in (0, 1):
            for buffer in buffers[:-2]:
                store(buffer, app, rows).wait()
            for part in range(ff // step):
                store(inner_b, app, rows, part).wait()
                store(slopes_b, app, rows, part).wait()

    run_active(tick, sizes, run)


def backward_kernel(sizes, lengths, *refs):
    tick = Tick(sizes, lengths)
    refs = list(refs)

    def take(count):
        taken = refs[:count]
        del refs[:count]
        return taken

    cosine_ref, sine_ref, gain_attn, gain_mlp = take(4)
    edge_parts, inbound = take(sizes["edge_parts"]), take(sizes["inbound"])
    w_heads, wp, wg, wu, wd = take(5)
    saved = take(sizes["reads"])
    take(sizes["aliased"])
    out_round, out_full = take(2)
    stores = take(sizes["stores"])
    grad_s, mixed_s, inner_s = take(3)
    kept = take(sizes["reads"])
    hidden_k, heads_k, probs_k, middle_k, slopes_k = kept
    buffers = take(sizes["stores"])
    branch_b, gate_b, up_b, attn_b, heads_b, gains_b = buffers
    read_sems, store_sems = refs
    chunk, width = grad_s.shape
    heads = width // HEAD_DIM
    all_width = w_heads.shape[0]
    kv_heads = (all_width // HEAD_DIM - heads) // 2
    share = heads // kv_heads
    ff = wd.shape[1]
    slot = tick.slot

    def read(buffer, app, rows):
        i = [other is buffer for other in kept].index(True)
        kind = sizes["read_kinds"][i]
        target, source = kept_at(kind, buffer, saved[i], app, slot, rows, chunk)
        return pltpu.make_async_copy(source, target, read_sems.at[i, app])

    def store(buffer, app, rows):
        i = [other is buffer for other in buffers].index(True)
        kind = sizes["store_kinds"][i]
        source, target = kept_at(kind, buffer, stores[i], app, slot, rows, chunk)
        return pltpu.make_async_copy(source, target, store_sems.at[i, app, 0])

    def rms_backward(value, gain, grad, running):
        scale = reciprocal_rms(value)
        unit = value * scale
        pulled = grad * gain
        gain_terms = grad * unit
        gain_rows = jnp.sum(gain_terms.reshape(grad.shape[0] // 8, 8, width), axis=0)
        shared = jnp.mean(gain_terms * gain, axis=-1, keepdims=True)
        return running + scale * (pulled - unit * shared), gain_rows

    def apply(rows, step_id, carry):
        app = 1 - step_id
        low = in_low_half(rows)
        grad_top = grad_s[:rows]
        branch = grad_top.astype(BF16)
        branch_b[app, :rows] = branch
        store(branch_b, app, rows).start()
        step = sizes["ff_step"]
        inner_s[:rows] = dot(branch, wd[...])
        read(slopes_k, app, rows).wait()
        for at in range(0, ff, step):
            inner_grad = inner_s[:rows, at : at + step]
            gate_b[app, :rows, at : at + step] = (
                inner_grad * slopes_k[app, 0, :rows, at : at + step].astype(F32)
            ).astype(BF16)
            up_b[app, :rows, at : at + step] = (
                inner_grad * slopes_k[app, 1, :rows, at : at + step].astype(F32)
            ).astype(BF16)
        store(gate_b, app, rows).start()
        store(up_b, app, rows).start()
        pulled = dot(gate_b[app, :rows], wg[...])
        pulled += dot(up_b[app, :rows], wu[...])
        read(middle_k, app, rows).wait()
        middle_grad, gain_rows = rms_backward(
            middle_k[app, :rows], gain_mlp[...], pulled, grad_top
        )
        gains_b[app, 1] = gain_rows
        attn_grad = middle_grad.astype(BF16)
        attn_b[app, :rows] = attn_grad
        store(attn_b, app, rows).start()
        mixed_s[:rows, :width] = dot(attn_grad, wp[...])
        mixed_parts, query_parts, keys, values = [], [], [], []
        for j in range(mixed_s.shape[1] // LANES):
            slab = mixed_s[:rows, j * LANES : (j + 1) * LANES]
            mixed_parts.append(jnp.where(low, slab, 0.0).astype(BF16))
            mixed_parts.append(jnp.where(low, 0.0, slab).astype(BF16))
        read(heads_k, app, rows).wait()
        for j in range(heads_k.shape[-1] // LANES):
            slab = heads_k[app, :rows, j * LANES : (j + 1) * LANES].astype(F32)
            sort_halves(slab, j, low, heads, kv_heads, chunk, query_parts, keys, values)
        cosine = cosine_ref[tick.table, :rows]
        sine = -sine_ref[tick.table, :rows]
        ones = jnp.ones((chunk, LANES), BF16)
        query_grads, key_grads, value_grads = [], [], []
        read(probs_k, app, rows).wait()
        for kv in range(kv_heads):
            mixed = jnp.concatenate(mixed_parts[kv * share : (kv + 1) * share], axis=0)
            grouped = jnp.concatenate(query_parts[kv * share : (kv + 1) * share], axis=0)
            probs = probs_k[app, kv, : share * rows]
            probs_wide = probs.astype(F32)
            probs_grad = dot_t(mixed, values[kv])
            weighted = probs_wide * probs_grad
            shared = dot(weighted.astype(BF16), ones)
            score_grad = (weighted - probs_wide * shared).astype(BF16)
            pulled = dot(score_grad, keys[kv])
            query_grads += [pulled[i * rows : (i + 1) * rows] for i in range(share)]
            both = dot_rows(
                jnp.concatenate([score_grad, probs], axis=1),
                jnp.concatenate([grouped, mixed], axis=1),
            )
            pulled = both[:rows, :LANES]
            key_grads.append(pulled + pltpu.roll(pulled, HEAD_DIM, 1))
            pulled = both[chunk : chunk + rows, LANES:]
            value_grads.append(pulled + pltpu.roll(pulled, HEAD_DIM, 1))

        parts = query_grads + key_grads + value_grads
        for j in range(len(parts) // 2):
            slab = jnp.where(low, parts[2 * j], parts[2 * j + 1])
            if 2 * j < heads + kv_heads:
                slab = rotate(slab * SCALE, cosine, sine)
            heads_b[app, :rows, j * LANES : (j + 1) * LANES] = slab.astype(BF16)
        if len(parts) % 2:
            heads_b[app, :rows, all_width - HEAD_DIM :] = parts[-1][:, :HEAD_DIM].astype(BF16)
        store(heads_b, app, rows).start()
        pulled = dot(heads_b[app, :rows], w_heads[...])
        read(hidden_k, app, rows).wait()
        result, gain_rows = rms_backward(
            hidden_k[app, :rows], gain_attn[...], pulled, middle_grad
        )
        gains_b[app, 0] = gain_rows
        store(gains_b, app, rows).start()
        grad_s[:rows] = result
        return carry

    def run(rows):
        for app in (1, 0):
            for buffer in (slopes_k, middle_k, heads_k, probs_k, hidden_k):
                read(buffer, app, rows).start()
        if edge_parts:

            @pl.when(tick.edge)
            def _():
                assemble(grad_s, edge_parts, sizes["tick"] * chunk)
                row = lax.broadcasted_iota(jnp.int32, (chunk, 1), 0)
                grad_s[...] = jnp.where(row < tick.bound(row, chunk // 2), grad_s[...], 0.0)

        if inbound:

            @pl.when(jnp.logical_not(tick.edge))
            def _():
                grad_s[:rows] = inbound[0][:rows].astype(F32)

        mixed_s[:, mixed_s.shape[1] - LANES :] = jnp.zeros((chunk, LANES), F32)
        lax.fori_loop(0, 2, functools.partial(apply, rows), 0)
        out_round[:rows] = grad_s[:rows].astype(BF16)

        @pl.when(tick.final)
        def _():
            at = pl.ds(pl.multiple_of(slot * chunk, chunk), rows)
            out_full[at] = grad_s[:rows].astype(BF16)

        for buffer in buffers:
            store(buffer, 0, rows).wait()
            store(buffer, 1, rows).wait()

    run_active(tick, sizes, run)


def transpose_to(target, source):
    for at in range(0, source.shape[1], 256):
        end = min(at + 256, source.shape[1])
        target[at:end, :] = jnp.transpose(source[:, at:end])


def load_kernel(extras, *refs):
    key_t, value_t, query, proj, gate, up, down_t = refs[:7]
    extra_in, refs = refs[7 : 7 + extras], refs[7 + extras :]
    heads_t, heads, proj_v, gate_v, up_v, down_tv, down = refs[:7]
    extra_out, (query_v, sems) = refs[7 : 7 + extras], refs[7 + extras :]
    width, kv_width = query.shape[1], key_t.shape[0]
    pairs = (
        (down_t, down_tv),
        (query, query_v),
        (key_t, heads_t.at[pl.ds(width, kv_width)]),
        (value_t, heads_t.at[pl.ds(width + kv_width, kv_width)]),
        (proj, proj_v),
        (gate, gate_v),
        (up, up_v),
        *zip(extra_in, extra_out),
    )
    copies = [
        pltpu.make_async_copy(source, target, sems.at[i])
        for i, (source, target) in enumerate(pairs)
    ]
    for copy in copies:
        copy.start()
    copies[0].wait()
    transpose_to(down, down_tv)
    copies[1].wait()
    transpose_to(heads_t, query_v)
    copies[2].wait()
    copies[3].wait()
    transpose_to(heads, heads_t)
    for copy in copies[4:]:
        copy.wait()


def turn_kernel(first, count, *refs):
    sources, targets = refs[:count], refs[-count:]

    @pl.when((lax.axis_index("pipe") == 0) == first)
    def _():
        for source, target in zip(sources, targets):
            transpose_to(target, source)


def load_weights(query, key_t, value_t, proj, gate, up, down_t, *extra):
    sources = (key_t, value_t, query, proj, gate, up, down_t, *extra)
    all_width = query.shape[1] + 2 * key_t.shape[0]
    shapes = (
        (all_width, query.shape[0]),
        (query.shape[0], all_width),
        proj.shape,
        gate.shape,
        up.shape,
        down_t.shape,
        down_t.shape[::-1],
    )
    outs = [pltpu.VMEM(tuple(shape), BF16) for shape in shapes]
    outs += [pltpu.VMEM(array.shape, array.dtype) for array in extra]
    return pl.pallas_call(
        functools.partial(load_kernel, len(extra)),
        out_shape=outs,
        in_specs=[in_hbm() for _ in sources],
        out_specs=[in_vmem() for _ in outs],
        scratch_shapes=[
            pltpu.VMEM(query.shape, BF16),
            pltpu.SemaphoreType.DMA((len(sources),)),
        ],
        compiler_params=pltpu.CompilerParams(vmem_limit_bytes=8 * 2**20),
        name="load_weights",
    )(*[pltpu.with_memory_space_constraint(array, pltpu.HBM) for array in sources])


def turn_weights(weights, first, turned=()):
    count = len(weights)
    return pl.pallas_call(
        functools.partial(turn_kernel, first, count),
        out_shape=[pltpu.VMEM(tuple(weight.shape[::-1]), BF16) for weight in weights],
        in_specs=[in_vmem() for _ in (*weights, *turned)],
        out_specs=[in_vmem() for _ in weights],
        input_output_aliases={count + i: i for i in range(len(turned))},
        compiler_params=pltpu.CompilerParams(vmem_limit_bytes=8 * 2**20),
        name="turn_weights",
    )(*[pltpu.with_memory_space_constraint(weight, pltpu.VMEM) for weight in (*weights, *turned)])


def in_vmem():
    return pl.BlockSpec(memory_space=pltpu.VMEM)


def in_hbm():
    return pl.BlockSpec(memory_space=pltpu.HBM)


def kind_of(array):
    return {5: "probs" if array.dtype == BF16 else "gains", 4: "slopes", 3: "rows"}[len(array.shape)]


def buffers_for(arrays, rows):
    shapes = []
    for array in arrays:
        kind, shape = kind_of(array), tuple(array.shape)
        if kind in ("probs", "gains"):
            shapes.append(shape[1:])
        else:
            shapes.append(shape[:-2] + (rows, shape[-1]))
    return [pltpu.VMEM(shape, array.dtype) for shape, array in zip(shapes, arrays)]


def run_tick(
    kernel, sizes, lengths, tables, edge_parts, inbound, weights, reads, state, shapes, scratch, name
):
    rows, width = sizes["rows"], sizes["width"]
    aliased = [] if state is None else list(state)
    inbound = [] if inbound is None else [inbound]
    outs = [jax.ShapeDtypeStruct((rows, width), BF16), pltpu.VMEM((sizes["total_rows"], width), BF16)]
    outs += [pltpu.HBM(shape.shape, shape.dtype) for shape in shapes]
    scratch = scratch + buffers_for(reads, rows) + buffers_for(shapes, rows)
    if reads:
        scratch.append(pltpu.SemaphoreType.DMA((len(reads), 2)))
    scratch.append(pltpu.SemaphoreType.DMA((len(shapes), 2, 2)))
    blocks = [*tables, *edge_parts, *inbound]
    kept = len(tables) + (0 if sizes["backward"] else len(edge_parts))
    blocks[:kept] = [pltpu.with_memory_space_constraint(array, pltpu.VMEM) for array in blocks[:kept]]
    first_alias = 1 + len(blocks) + len(weights) + len(reads)
    sizes = dict(
        sizes,
        edge_parts=len(edge_parts),
        inbound=len(inbound),
        aliased=len(aliased),
        stores=len(shapes),
        reads=len(reads),
        store_kinds=[kind_of(shape) for shape in shapes],
        read_kinds=[kind_of(read) for read in reads],
    )
    flops = 4 * rows * sum(int(np.prod(weight.shape)) for weight in weights)
    return pl.pallas_call(
        functools.partial(kernel, sizes),
        out_shape=outs,
        grid_spec=pltpu.PrefetchScalarGridSpec(
            num_scalar_prefetch=1,
            grid=(1,),
            in_specs=[in_vmem() for _ in (*blocks, *weights)]
            + [in_hbm() for _ in reads]
            + [in_vmem() for _ in aliased[:1]]
            + [in_hbm() for _ in aliased[1:]],
            out_specs=[in_vmem(), in_vmem()] + [in_hbm() for _ in shapes],
            scratch_shapes=scratch,
        ),
        input_output_aliases={first_alias + i: 1 + i for i in range(len(aliased))},
        compiler_params=pltpu.CompilerParams(
            dimension_semantics=("arbitrary",), vmem_limit_bytes=61 * 2**18
        ),
        cost_estimate=pl.CostEstimate(
            flops=flops, bytes_accessed=flops // (2 * rows), transcendentals=0
        ),
        name=name,
    )(
        lengths,
        *blocks,
        *[pltpu.with_memory_space_constraint(weight, pltpu.VMEM) for weight in weights],
        *[pltpu.with_memory_space_constraint(array, pltpu.HBM) for array in reads],
        *[pltpu.with_memory_space_constraint(array, pltpu.VMEM) for array in aliased[:1]],
        *[pltpu.with_memory_space_constraint(array, pltpu.HBM) for array in aliased[1:]],
    )


def rope_tables(rows):
    segment = rows // 2
    frequency = rope_base ** (-np.arange(HALF, dtype=np.float64) / HALF)
    positions = np.stack([np.arange(rows) % segment, np.arange(rows)]).astype(np.float64)
    angles = np.tile(positions[:, :, None] * frequency, (1, 1, LANES // HALF))
    sign = np.where(np.arange(LANES) % HEAD_DIM < HALF, -1.0, 1.0)
    return (
        jnp.asarray(np.cos(angles), F32),
        jnp.asarray(np.sin(angles) * sign, F32),
    )


def gather_ends(inputs, cotangent):
    sections, section = lax.axis_size("pipe"), lax.axis_index("pipe")
    last = sections - 1
    input_parts, cotangent_parts = [inputs] * sections, [cotangent] * sections
    for source in range(1, sections):
        mirror = last - source
        if mirror == source:
            input_parts[source] = lax.ppermute(inputs, "pipe", [(source, 0)])
            cotangent_parts[source] = lax.ppermute(cotangent, "pipe", [(source, last)])
            continue
        sent = jnp.where(section == mirror, cotangent, inputs)
        got = lax.ppermute(sent, "pipe", [(source, 0), (mirror, last)])
        input_parts[source] = cotangent_parts[mirror] = got
    return input_parts, cotangent_parts


def spread_ends(results, input_grads):
    sections, section = lax.axis_size("pipe"), lax.axis_index("pipe")
    last = sections - 1
    columns = results.shape[1] // sections

    def block(value, at):
        return value[:, at * columns : (at + 1) * columns]

    outputs, grads = block(results, last), block(input_grads, 0)
    for target in range(last):
        mirror = last - target
        if mirror == target:
            got = lax.ppermute(block(results, target), "pipe", [(last, target)])
            outputs = jnp.where(section == target, got, outputs)
            got = lax.ppermute(block(input_grads, target), "pipe", [(0, target)])
            grads = jnp.where(section == target, got, grads)
            continue
        sent = jnp.where(section == 0, block(input_grads, mirror), block(results, target))
        got = lax.ppermute(sent, "pipe", [(last, target), (0, mirror)])
        outputs = jnp.where(section == target, got, outputs)
        grads = jnp.where(section == mirror, got, grads)
    return outputs.astype(F32), grads.astype(F32)


def after(values, *tokens):
    return lax.optimization_barrier((values, tokens))[0]


def by_rows(value):
    return with_layout_constraint(value, Layout(major_to_minor=(0, 1)))


def cube_view(value):
    bits = lax.axis_size("dp").bit_length() - 1
    rows, columns = value.shape
    return value.reshape((2,) * bits + (rows >> bits, columns))


class Piece:
    def __init__(self, value, bits):
        self.value, self.bits, self.got = value, list(bits), None

    def send(self, *tokens):
        devices = lax.axis_size("dp")
        bit = self.bits.pop(0)
        axis = devices.bit_length() - 2 - bit
        mine = (lax.axis_index("dp") >> bit) & 1
        sent = lax.dynamic_index_in_dim(self.value, 1 - mine, axis)
        if tokens:
            sent = after(sent, *tokens)
        self.kept = (axis, mine)
        self.got = lax.ppermute(sent, "dp", [(i, i ^ (1 << bit)) for i in range(devices)])
        return sent

    def take(self, *tokens):
        axis, mine = self.kept
        got = after(self.got, *tokens) if tokens else self.got
        self.value = lax.dynamic_index_in_dim(self.value, mine, axis) + got
        return self.value


def per_device(
    inputs,
    cotangent,
    lengths,
    w_query,
    w_key,
    w_value,
    w_proj,
    w_gate,
    w_up,
    w_down,
    gain_attn,
    gain_mlp,
):
    sections = lax.axis_size("pipe")
    section = lax.axis_index("pipe")
    total_rows, columns = inputs.shape
    width = columns * sections
    rows = 2 * total_rows // (MICRO + 1)
    segment = rows // 2
    kv_width = w_key.shape[-1]
    ff = w_gate.shape[-1]
    kv_heads = kv_width // HEAD_DIM
    share = width // kv_width
    depth_step = 2
    ticks = CHUNKS + depth_step * (sections - 1)
    sizes = dict(
        rows=rows,
        total_rows=total_rows,
        width=width,
        ff_step=ff // 2,
        sections=sections,
        depth_step=depth_step,
    )
    group = lengths[0]
    input_parts, cotangent_parts = gather_ends(inputs, cotangent)
    w_heads_t, w_heads, wp, wg, wu, wd_t, wd, *tables = load_weights(
        w_query[0],
        jnp.swapaxes(w_key[0], 0, 1),
        jnp.swapaxes(w_value[0], 0, 1),
        w_proj[0],
        w_gate[0],
        w_up[0],
        jnp.swapaxes(w_down[0], 0, 1),
        *rope_tables(rows),
        gain_attn,
        gain_mlp,
        inputs,
    )
    input_parts[0] = tables.pop()
    turned = turn_weights((wp, wg, wu), False)
    forward_weights = (w_heads, wp, wg, wu, wd)

    def stored(*shape, dtype=BF16):
        return jax.ShapeDtypeStruct(shape, dtype)

    query_pad = round_up(width, LANES)
    all_width = width + 2 * kv_width
    heads_pad = round_up(all_width, LANES)
    forward_shapes = [
        stored(2, total_rows, width, dtype=F32),
        stored(2, total_rows, width),
        stored(2, total_rows, heads_pad),
        stored(CHUNKS, 2, kv_heads, share * rows, rows),
        stored(2, total_rows, width),
        stored(2, total_rows, width, dtype=F32),
        stored(2, total_rows, width),
        stored(2, 2, total_rows, ff),
        stored(2, total_rows, ff),
    ]
    forward_scratch = [
        pltpu.VMEM((rows, width), F32),
        pltpu.VMEM((rows, heads_pad), F32),
    ]
    sent = {}
    state = None
    for tick in range(ticks):
        rounded, *state = run_tick(
            forward_kernel,
            dict(sizes, tick=tick, backward=False),
            lengths,
            tables,
            input_parts if tick < CHUNKS else (),
            sent.get(tick - depth_step),
            forward_weights,
            (),
            state,
            forward_shapes,
            forward_scratch,
            "layer_pair_forward",
        )
        route = [
            (s, s + 1) for s in range(sections - 1) if 0 <= tick - depth_step * s < CHUNKS
        ]
        if route:
            sent[tick] = lax.ppermute(rounded, "pipe", route)
        if tick == CHUNKS - 1:
            ready, _ = lax.optimization_barrier(((wp, wg, wu), rounded))
            turned = turn_weights(ready, True, turned)
    backward_weights = (w_heads_t, *turned, wd_t)
    results = state[0]
    hidden, normed_attn, heads, probs, mixed, middle, normed_mlp, slopes, inner = state[1:]

    backward_shapes = [
        stored(2, total_rows, width),
        stored(2, total_rows, ff),
        stored(2, total_rows, ff),
        stored(2, total_rows, width),
        stored(2, total_rows, all_width),
        stored(CHUNKS, 2, 2, 8, width, dtype=F32),
    ]
    backward_scratch = [
        pltpu.VMEM((rows, width), F32),
        pltpu.VMEM((rows, query_pad), F32),
        pltpu.VMEM((rows, ff), F32),
    ]
    reads = (hidden, heads, probs, middle, slopes)
    sent = {}
    state = None
    for tick in range(ticks):
        rounded, *state = run_tick(
            backward_kernel,
            dict(sizes, tick=tick, backward=True),
            lengths,
            tables,
            cotangent_parts if tick < CHUNKS else (),
            sent.get(tick - depth_step),
            backward_weights,
            reads,
            state,
            backward_shapes,
            backward_scratch,
            "layer_pair_backward",
        )
        route = [
            (s, s - 1)
            for s in range(1, sections)
            if 0 <= tick - depth_step * (sections - 1 - s) < CHUNKS
        ]
        if route:
            sent[tick] = lax.ppermute(rounded, "pipe", route)
    input_grads = state[0]
    branch, gate_grad, up_grad, attn_grad, heads_grad, gains = state[1:]

    def product(left, right):
        left = left.reshape(2 * total_rows, left.shape[-1])
        right = right.reshape(2 * total_rows, right.shape[-1])
        return by_rows(dot_rows(left, right).astype(BF16))

    bits = lax.axis_size("dp").bit_length() - 1
    across_first, along_first = range(bits), [*range(1, bits), 0]
    gain_sums = jnp.swapaxes(jnp.sum(gains, axis=(0, 1, 3)), 0, 1).astype(BF16)

    def make(name, token):
        terms = dict(
            G=(normed_mlp, gate_grad),
            U=(normed_mlp, up_grad),
            H=(normed_attn, heads_grad),
            P=(mixed, attn_grad),
            D=(inner, branch),
        )[name]
        value = product(*(terms if token is None else after(terms, token)))
        if name == "P":
            value = jnp.concatenate([value, gain_sums], axis=1)
        view = cube_view(value)
        if name != "D":
            return {name: Piece(view, along_first if name in "HP" else across_first)}
        part = view.shape[-2] * DOWN_PART // 20 // 16 * 16
        return {
            "d": Piece(view[..., :part, :], across_first),
            "e": Piece(view[..., part:, :], across_first),
        }

    pieces, token, outputs = {}, None, None
    for step in ORDER:
        name, mark = step[0], step[1:]
        if name == "S":
            outputs = spread_ends(*after((results, input_grads), token))
            continue
        if name not in pieces:
            pieces.update(make(name, token))
            if name == "D":
                token = pieces["e"].value
                continue
        piece = pieces[name]
        if mark != ">":
            token = piece.take(token)
        if mark == ".":
            spare = 0 if name in "HP" and 0 in piece.bits else len(piece.bits)
            spare = len(piece.bits) - 1 if name in "HP" and 0 in piece.bits else spare
            for _ in range(spare):
                piece.send()
                token = piece.take()
        else:
            token = piece.send(*(() if token is None else (token,)))
    layer_output, grad_input = outputs
    ends = {name: piece.value.reshape(piece.value.shape[-2:]) for name, piece in pieces.items()}
    grad_down = jnp.concatenate([ends["d"], ends["e"]], axis=0).astype(F32)
    grad_gate, grad_up, grad_heads, grad_proj = [ends[name] for name in "GUHP"]
    grad_gate, grad_up, grad_heads, grad_proj = [
        grad.astype(F32) for grad in (grad_gate, grad_up, grad_heads, grad_proj)
    ]
    grad_query = grad_heads[:, :width]
    grad_key = grad_heads[:, width : width + kv_width]
    grad_value = grad_heads[:, width + kv_width :]
    grad_gain_attn, grad_gain_mlp = grad_proj[:, width], grad_proj[:, width + 1]
    grad_proj = grad_proj[:, :width]

    return (
        layer_output,
        grad_input,
        grad_query[None],
        grad_key[None],
        grad_value[None],
        grad_proj[None],
        grad_gate[None],
        grad_up[None],
        grad_down[None],
        grad_gain_attn[None],
        grad_gain_mlp[None],
    )


def solution(mesh):
    placed = (
        P("dp", "pipe"),
        P("dp", "pipe"),
        P("dp", None),
        P("pipe", None, None),
        P("pipe", None, None),
        P("pipe", None, None),
        P("pipe", None, None),
        P("pipe", None, None),
        P("pipe", None, None),
        P("pipe", None, None),
        P("pipe", None),
        P("pipe", None),
    )
    return jax.shard_map(
        per_device,
        mesh=mesh,
        in_specs=placed,
        out_specs=(
            P("dp", "pipe"),
            P("dp", "pipe"),
            P("pipe", "dp", None),
            P("pipe", "dp", None),
            P("pipe", "dp", None),
            P("pipe", "dp", None),
            P("pipe", "dp", None),
            P("pipe", "dp", None),
            P("pipe", "dp", None),
            P("pipe", "dp"),
            P("pipe", "dp"),
        ),
        check_vma=False,
    )
```
